32 devices in a mesh: space: 8 (over y, x, core), scan: 4 (over z).
Axes of the slice: x: 2, y: 2, z: 4, core: 2. Of those that a mesh axis runs over, the one named last changes fastest.
Arguments:
- act_zero: bfloat16 [4, 8, 512, 96], P('scan', 'space'), may hold values from -6 to 6
- pre_act: bfloat16 [4, 8, 512, 96], P('scan', 'space'), may hold values from -6 to 6
- cot_out: bfloat16 [4, 8, 512, 96], P('scan', 'space'), may hold values from -0.59765625 to 0.59765625
- weight_one: bfloat16 [27, 96, 96], replicated, may hold values from -0.625 to 0.625
- weight_two: bfloat16 [27, 96, 96], replicated, may hold values from -0.625 to 0.625
- in_map: int32 [4, 8, 27, 256], P('scan', 'space'), may hold values from 0 to 640, as said below
- out_map: int32 [4, 8, 27, 256], P('scan', 'space'), may hold values from 0 to 512, as said below
- send_lo: int32 [4, 8, 64], P('scan', 'space'), may hold values from 0 to 511, as said below
- send_hi: int32 [4, 8, 64], P('scan', 'space'), may hold values from 0 to 511, as said below
Outputs:
- grad_act: bfloat16 [4, 8, 512, 96], P('scan', 'space')
- grad_w_one: float32 [27, 96, 96], replicated
- grad_w_two: float32 [27, 96, 96], replicated
The draws below stay inside these ranges and needn't reach their ends.
Inputs may be any that keep to these rules, and one draw needn't show every extreme that they name: Per brick and offset the live slots come first and number a multiple of 32; the input rows of one offset differ, and so do its output rows; empty slots hold in_map 512 + 2 * 64 and out_map 512; in every draw some brick has every slot live. `out_map`: see in_map. send_lo and send_hi of one brick hold 128 different rows. `send_hi`: see send_lo.
All inputs are finite; a program needn't handle non-finite values.
Results may differ from the reference program's by a relative error of at most 0.0049.
Values may be sent and summed in bfloat16 or wider, within the bound.
No kernel may reach another device: no remote copies, remote signals or barrier semaphores. Data moves between devices by JAX's collectives and lax.ppermute only.
A program may use at most 64 MiB of HBM per device.

```python
import jax
import jax.numpy as jnp
from jax import lax

C = 96
OFFSETS = 27
ROWS = 512
PAIRS = 256
RIM = 64
SCENES = 4
BRICKS = 8


def kernel_pairs(key):
    key = jax.random.fold_in(key, 11)
    devices = SCENES * BRICKS
    key_count, key_in, key_out, key_full = jax.random.split(key, 4)
    units = jax.random.randint(key_count, (devices, OFFSETS), 1, 6)
    busiest = jax.random.randint(key_full, (), 0, devices)
    units = jnp.where(jnp.arange(devices)[:, None] == busiest, 8, units)
    counts = units * (PAIRS // 8)
    in_keys = jax.random.split(key_in, devices * OFFSETS)
    out_keys = jax.random.split(key_out, devices * OFFSETS)
    ins = jax.vmap(lambda kk: jax.random.permutation(kk, ROWS + 2 * RIM)[:PAIRS])(in_keys)
    outs = jax.vmap(lambda kk: jax.random.permutation(kk, ROWS)[:PAIRS])(out_keys)
    ins = ins.reshape(devices, OFFSETS, PAIRS)
    outs = outs.reshape(devices, OFFSETS, PAIRS)
    live = jnp.arange(PAIRS)[None, None, :] < counts[:, :, None]
    ins = jnp.where(live, ins, ROWS + 2 * RIM).astype(jnp.int32)
    outs = jnp.where(live, outs, ROWS).astype(jnp.int32)
    return (ins.reshape(SCENES, BRICKS, OFFSETS, PAIRS), outs.reshape(SCENES, BRICKS, OFFSETS, PAIRS))


def rim_rows(key):
    key = jax.random.fold_in(key, 23)
    keys = jax.random.split(key, SCENES * BRICKS)
    rows = jax.vmap(lambda kk: jax.random.permutation(kk, ROWS)[:2 * RIM])(keys)
    return rows.reshape(SCENES, BRICKS, 2 * RIM).astype(jnp.int32)


def draw_in_map(key, part):
    return kernel_pairs(key)[0]


def draw_out_map(key, part):
    return kernel_pairs(key)[1]


def draw_send_lo(key, part):
    return rim_rows(key)[:, :, :RIM]


def draw_send_hi(key, part):
    return rim_rows(key)[:, :, RIM:]


def levels(stream_key, shape, shards, least, high):
    def one(dim, shards_of):
        draws = jax.random.uniform(jax.random.fold_in(jax.random.fold_in(stream_key, 6), dim), (shards_of,), jnp.float32, least / len(shards), high / len(shards))
        return jnp.repeat(jnp.exp(draws), shape[dim] // shards_of).reshape((-1,) + (1,) * (len(shape) - dim - 1))

    factor_of = one(*shards[0])
    for cut in shards[1:]:
        factor_of = factor_of * one(*cut)
    return factor_of


def scatter_about(own_key, shape, deviation, most, cuts=(), held_as=jnp.bfloat16):
    loudness = levels(own_key, shape, cuts, -0.22, 0.18) if cuts else 1.0
    array = jax.random.normal(own_key, shape, jnp.float32) * deviation * loudness
    return jnp.minimum(jnp.maximum(array, -most), most).astype(held_as)


def setup_inputs(seed: int = 0) -> dict:
    arg_keys = jax.random.split(jax.random.key(seed), 10)
    act_zero = scatter_about(arg_keys[0], (SCENES, BRICKS, ROWS, C), 1.0, 6.0, ((0, 4), (1, 8)))
    pre_act = scatter_about(arg_keys[1], (SCENES, BRICKS, ROWS, C), 1.0, 6.0, ((0, 4), (1, 8)))
    cot_out = scatter_about(arg_keys[2], (SCENES, BRICKS, ROWS, C), 0.1, 0.59765625, ((0, 4), (1, 8)))
    weight_one = scatter_about(arg_keys[3], (OFFSETS, C, C), C ** -0.5, 0.625)
    weight_two = scatter_about(arg_keys[4], (OFFSETS, C, C), C ** -0.5, 0.625)
    in_map = draw_in_map(jax.random.fold_in(arg_keys[9], 71), 0)
    out_map = draw_out_map(jax.random.fold_in(arg_keys[9], 71), 0)
    send_lo = draw_send_lo(jax.random.fold_in(arg_keys[9], 71), 0)
    send_hi = draw_send_hi(jax.random.fold_in(arg_keys[9], 71), 0)
    return dict(act_zero=act_zero, pre_act=pre_act, cot_out=cot_out, weight_one=weight_one, weight_two=weight_two, in_map=in_map, out_map=out_map, send_lo=send_lo, send_hi=send_hi)


def extended(feats, send_lo, send_hi):
    pick = jax.vmap(jax.vmap(lambda arr, idx: arr[idx]))
    hi_rows = pick(feats, send_hi)
    lo_rows = pick(feats, send_lo)
    zero = jnp.zeros_like(hi_rows[:, :1])
    left = jnp.concatenate([zero, hi_rows[:, :-1]], 1)
    right = jnp.concatenate([lo_rows[:, 1:], zero], 1)
    pad = jnp.zeros(feats.shape[:2] + (1, feats.shape[3]), feats.dtype)
    return jnp.concatenate([feats, left, right, pad], 2)


def layer_grads(ext_feats, cot, weight, ins, outs):
    padded = jnp.concatenate([cot, jnp.zeros((1, cot.shape[1]), cot.dtype)], 0)
    gathered = ext_feats[ins].astype(jnp.float32)
    cot_rows = padded[outs].astype(jnp.float32)
    delta_w = jnp.einsum('kpc,kpd->kcd', gathered, cot_rows)
    back = jnp.einsum('kpd,kcd->kpc', cot_rows, weight.astype(jnp.float32))
    delta_x = jnp.zeros(ext_feats.shape, jnp.float32).at[ins.reshape(-1)].add(back.reshape(-1, back.shape[2]))
    return delta_w, delta_x


def backward(ext_feats, cot, weight, ins, outs, send_lo, send_hi):
    scenes, bricks = cot.shape[0], cot.shape[1]

    def flat(arr):
        return arr.reshape((scenes * bricks,) + arr.shape[2:])

    def one(total, item):
        delta_w, delta_x = layer_grads(item[0], item[1], weight, item[2], item[3])
        return total + delta_w, delta_x

    init = jnp.zeros(weight.shape, jnp.float32)
    delta_w, delta_x = lax.scan(one, init, (flat(ext_feats), flat(cot), flat(ins), flat(outs)))
    delta_x = delta_x.reshape((scenes, bricks) + delta_x.shape[1:])
    local = delta_x[:, :, :ROWS]
    left_slot = delta_x[:, :, ROWS:ROWS + RIM]
    right_slot = delta_x[:, :, ROWS + RIM:ROWS + 2 * RIM]
    zero = jnp.zeros_like(left_slot[:, :1])
    from_above = jnp.concatenate([left_slot[:, 1:], zero], 1)
    from_below = jnp.concatenate([zero, right_slot[:, :-1]], 1)
    settle = jax.vmap(jax.vmap(lambda base, upper, lower, hi, lo: base.at[hi].add(upper).at[lo].add(lower)))
    return delta_w / SCENES, settle(local, from_above, from_below, send_hi, send_lo)


def reference(act_zero, pre_act, cot_out, weight_one, weight_two, in_map, out_map, send_lo, send_hi):
    act_one = jnp.maximum(pre_act, jnp.zeros_like(pre_act))
    grad_w_two, back_two = backward(extended(act_one, send_lo, send_hi), cot_out, weight_two, in_map, out_map, send_lo, send_hi)
    cot_one = jnp.where(pre_act > 0, back_two, 0.0).astype(jnp.bfloat16)
    grad_w_one, back_one = backward(extended(act_zero, send_lo, send_hi), cot_one, weight_one, in_map, out_map, send_lo, send_hi)
    return back_one.astype(jnp.bfloat16), grad_w_one, grad_w_two
```

```python
import functools

import jax
import jax.numpy as jnp
from jax import lax
from jax.experimental import pallas as pl
from jax.experimental.pallas import tpu as pltpu
from jax.sharding import PartitionSpec as P

F32, BF16, I32 = jnp.float32, jnp.bfloat16, jnp.int32
VMEM = pl.BlockSpec(memory_space=pltpu.VMEM)
LANES = 128
GROUP = 256
UNROLL = 9
NT = (((1,), (1,)), ((), ()))


def call(body, outs, args, scratch=(), flops=0, moved=0):
    single = not isinstance(outs, (list, tuple))
    return pl.pallas_call(
        body,
        out_shape=outs if single else tuple(outs),
        in_specs=[VMEM] * len(args),
        out_specs=VMEM if single else (VMEM,) * len(outs),
        scratch_shapes=scratch,
        compiler_params=pltpu.CompilerParams(vmem_limit_bytes=40 << 20),
        cost_estimate=pl.CostEstimate(flops=flops, bytes_accessed=moved, transcendentals=0),
    )(*args)


def shape(dims, dtype):
    return jax.ShapeDtypeStruct(dims, dtype)


def loop(steps, body):
    unroll = next(u for u in range(UNROLL, 0, -1) if steps % u == 0)

    def step(i, carry):
        body(i)
        return carry

    lax.fori_loop(0, steps, step, 0, unroll=unroll)


def one_hot(rows, index):
    return (lax.broadcasted_iota(I32, (rows, index.shape[1]), 0) == index).astype(F32).astype(BF16)


def dot(a, b):
    return jnp.dot(a, b, preferred_element_type=F32)


def dot_nt(a, b):
    return lax.dot_general(a, b, NT, preferred_element_type=F32)


def offset_rows(k, chans):
    return pl.ds(pl.multiple_of(k * chans, chans), chans)


def rim_index(hi_ref, lo_ref):
    return jnp.concatenate([hi_ref[...], lo_ref[...]], 1)


def first_half(dims, own_parity):
    lane = lax.broadcasted_iota(I32, dims, 1)
    return (lane < dims[1] // 2) == own_parity


def is_even():
    return lax.rem(lax.axis_index("space"), 2) == 0


def rim_body(zero_ref, pre_ref, hi_ref, lo_ref, rim_ref):
    pick = one_hot(zero_ref.shape[1], rim_index(hi_ref, lo_ref))
    one = jnp.maximum(pre_ref[...], jnp.zeros_like(pre_ref))
    chans = zero_ref.shape[0]
    rim_ref[:chans] = dot(zero_ref[...], pick).astype(BF16)
    rim_ref[chans:] = dot(one, pick).astype(BF16)


def add_back(weight_ref, t_ref, total_ref):
    count, chans = weight_ref.shape[0], weight_ref.shape[1]
    total_ref[...] = jnp.zeros_like(total_ref)

    def body(g):
        part = None
        for j in range(3):
            k = g * 3 + j
            term = dot(weight_ref[k], t_ref[offset_rows(k, chans), :])
            part = term if part is None else part + term
        total_ref[...] += part

    assert count % 3 == 0
    loop(count // 3, body)


def split_back(total_ref, own_ref, rim_ref):
    rows = own_ref.shape[1]
    own_ref[...] = total_ref[:, :rows]
    rim_ref[...] = total_ref[:, rows:]


def two_body(ins_ref, outs_ref, cot_ref, weight_ref, t_ref, inv_ref, own_ref, rim_ref, c_ref, total_ref):
    count, pairs = ins_ref.shape[0], ins_ref.shape[2]
    chans, rows = cot_ref.shape
    ext = t_ref.shape[1]
    tall = chans + 16
    row = lax.broadcasted_iota(I32, (16, pairs), 0)

    def pick_outs(k):
        index = outs_ref[k]
        base = pl.multiple_of(k * tall, 16)
        c_ref[pl.ds(base, chans), :] = dot(cot_ref[...], one_hot(rows, index)).astype(BF16)
        left = rows - index
        code = jnp.where(row == 0, left // 16, jnp.where(row == 1, left % 16, 0))
        c_ref[pl.ds(base + chans, 16), :] = code.astype(F32).astype(BF16)

    loop(count, pick_outs)

    def put_ins(k):
        picked = c_ref[pl.ds(pl.multiple_of(k * tall, 16), tall), :]
        placed = dot_nt(picked, one_hot(ext, ins_ref[k]))
        t_ref[offset_rows(k, chans), :] = placed[:chans].astype(BF16)
        code = placed[chans : chans + 1] * 16.0 + placed[chans + 1 : chans + 2]
        inv_ref[k] = rows - code.astype(I32)

    loop(count, put_ins)
    t_ref[count * chans :, :] = jnp.zeros((t_ref.shape[0] - count * chans, ext), BF16)
    add_back(weight_ref, t_ref, total_ref)
    split_back(total_ref, own_ref, rim_ref)


def weight_sums(ext, t_ref, sum_ref, keep_ref, send_ref):
    chans = ext.shape[0]
    tiles = t_ref.shape[0] // LANES
    for start in range(0, tiles, 2):
        width = min(2, tiles - start)
        grad = dot_nt(ext, t_ref[start * LANES : (start + width) * LANES, :])
        for j in range(width):
            sum_ref[(start + j) * chans : (start + j + 1) * chans, :] = grad[:, j * LANES : (j + 1) * LANES]
    sum_ref[tiles * chans :, :] = jnp.zeros((sum_ref.shape[0] - tiles * chans, LANES), F32)
    me = lax.axis_index("space")
    slots = lax.axis_size("space") // 2
    rows = keep_ref.shape[0] // slots
    for slot in range(slots):
        for out_ref, bit in ((keep_ref, 0), (send_ref, 1)):
            piece = jnp.bitwise_xor(me, 2 * slot + bit)
            block = sum_ref[pl.ds(pl.multiple_of(piece * rows, rows), rows), :]
            out_ref[slot * rows : (slot + 1) * rows, :] = block.astype(out_ref.dtype)


def two_weights_body(pre_ref, near_ref, far_ref, t_ref, keep_ref, send_ref, sum_ref):
    chans = pre_ref.shape[0]
    one = jnp.maximum(pre_ref[...], jnp.zeros_like(pre_ref))
    ext = extended(one, near_ref[chans:].astype(F32), far_ref[chans:].astype(F32))
    weight_sums(ext, t_ref, sum_ref, keep_ref, send_ref)


def extended(feats, near, far):
    rim = jnp.where(first_half(near.shape, is_even()), far, near).astype(feats.dtype)
    return jnp.concatenate([feats, rim], 1)


def settled(own, near, far, hi_ref, lo_ref):
    part = jnp.where(first_half(near.shape, is_even()), near, far)
    place = one_hot(own.shape[1], rim_index(hi_ref, lo_ref))
    high = part.astype(BF16)
    low = (part - high.astype(F32)).astype(BF16)
    return own + dot_nt(high, place) + dot_nt(low, place)


def one_body(
    own_ref, near_ref, far_ref, hi_ref, lo_ref, pre_ref, zero_ref, rnear_ref, rfar_ref, inv_ref, t_ref, keep_ref, send_ref, cot_ref, sum_ref
):
    chans, rows = pre_ref.shape
    count, ext = inv_ref.shape[0], inv_ref.shape[2]
    back = settled(own_ref[...], near_ref[...], far_ref[...], hi_ref, lo_ref)
    cot_ref[...] = jnp.where(pre_ref[...].astype(F32) > 0, back, 0.0).astype(BF16)

    def place(k):
        t_ref[offset_rows(k, chans), :] = dot(cot_ref[...], one_hot(rows, inv_ref[k])).astype(BF16)

    loop(count, place)
    t_ref[count * chans :, :] = jnp.zeros((t_ref.shape[0] - count * chans, ext), BF16)
    feats = extended(zero_ref[...], rnear_ref[:chans].astype(F32), rfar_ref[:chans].astype(F32))
    weight_sums(feats, t_ref, sum_ref, keep_ref, send_ref)


def back_body(weight_ref, t_ref, own_ref, rim_ref, total_ref):
    add_back(weight_ref, t_ref, total_ref)
    split_back(total_ref, own_ref, rim_ref)


def settle_body(own_ref, near_ref, far_ref, hi_ref, lo_ref, out_ref):
    out_ref[...] = settled(own_ref[...], near_ref[...], far_ref[...], hi_ref, lo_ref).astype(BF16)


def core_sum_body(keep_ref, got_ref, own_ref, *send_refs):
    rows = own_ref.shape[0]
    own_ref[...] = keep_ref[:rows] + got_ref[:rows].astype(F32)
    for slot, send_ref in enumerate(send_refs, 1):
        part = slice(slot * rows, (slot + 1) * rows)
        send_ref[...] = (keep_ref[part] + got_ref[part].astype(F32)).astype(BF16)


def chip_sum_body(own_ref, *refs):
    total = own_ref[...]
    for got_ref in refs[:-1]:
        total = total + got_ref[...].astype(F32)
    refs[-1][...] = total.astype(BF16)


def scan_sum_body(*refs):
    terms = [ref[...].astype(F32) for ref in refs[:-1]]
    while len(terms) > 1:
        terms = [a + b for a, b in zip(terms[::2], terms[1::2], strict=True)]
    refs[-1][...] = terms[0].astype(BF16)


def unpack_body(scale, *refs):
    *piece_refs, out_ref, all_ref = refs
    me = lax.axis_index("space")
    rows = piece_refs[0].shape[0]
    for slot, piece_ref in enumerate(piece_refs):
        piece = jnp.bitwise_xor(me, slot)
        all_ref[pl.ds(pl.multiple_of(piece * rows, rows), rows), :] = piece_ref[...].astype(F32)
    count, chans = out_ref.shape[0], out_ref.shape[1]
    lane = lax.broadcasted_iota(I32, (chans, LANES), 1)
    for k in range(count):
        tile, shift = divmod(k * chans, LANES)
        block = all_ref[tile * chans : (tile + 1) * chans, :]
        if shift:
            block = pltpu.roll(block, LANES - shift, 1)
        if shift + chans > LANES:
            after = pltpu.roll(all_ref[(tile + 1) * chans : (tile + 2) * chans, :], LANES - shift, 1)
            block = jnp.where(lane < LANES - shift, block, after)
        out_ref[k] = block[:, :chans] * scale


def swap(block, axis, bit):
    return lax.ppermute(block, axis, [(i, i ^ bit) for i in range(lax.axis_size(axis))])


def swap_neighbours(block):
    bricks = lax.axis_size("space")
    near = swap(block, "space", 1)
    inner = range(1, bricks - 1)
    far = lax.ppermute(block, "space", [(i, i + 1 if i % 2 else i - 1) for i in inner])
    return near, far


def summed(keep, send, weight_shape, scale):
    slots = lax.axis_size("space") // 2
    scans = lax.axis_size("scan")
    rows = keep.shape[0] // slots
    got = swap(send, "space", 1)
    outs = [shape((rows, LANES), F32)] + [shape((rows, LANES), BF16)] * (slots - 1)
    own, *sends = call(core_sum_body, outs, [keep, got])
    gots = [swap(block, "space", 2 * slot) for slot, block in enumerate(sends, 1)]
    part = call(chip_sum_body, shape((rows, LANES), BF16), [own, *gots])
    if scans & (scans - 1):
        total = lax.psum(part, "scan")
    else:
        terms = [part] + [swap(part, "scan", bit) for bit in range(1, scans)]
        total = call(scan_sum_body, shape((rows, LANES), BF16), terms)
    pieces = []
    for slot in range(slots):
        piece = swap(total, "space", 2 * slot) if slot else total
        pieces += [piece, swap(piece, "space", 1)]
    packed = 2 * keep.shape[0]
    return call(
        functools.partial(unpack_body, scale), shape(weight_shape, F32), pieces, scratch=[pltpu.VMEM((packed, LANES), F32)]
    )


def shards(act_zero, pre_act, cot_out, weight_one, weight_two, in_map, out_map, send_lo, send_hi):
    zero, pre, cot = (x[0, 0].T for x in (act_zero, pre_act, cot_out))
    ins, outs = (x[0, 0][:, None, :] for x in (in_map, out_map))
    lo, hi = send_lo[0], send_hi[0]
    chans, rows = zero.shape
    count, _, pairs = ins.shape
    rim = 2 * lo.shape[1]
    ext = rows + rim
    scenes = lax.axis_size("scan")
    bricks = lax.axis_size("space")
    tiles = -(-count * chans // LANES)
    tall = tiles * LANES
    unit = 16 * bricks
    packed = -(-tiles * chans // unit) * unit
    halves = [shape((packed // 2, LANES), F32), shape((packed // 2, LANES), BF16)]
    packed_sum = pltpu.VMEM((packed, LANES), F32)
    gather_flops = 2 * count * chans * ext * rows
    back_flops = 2 * count * chans * chans * ext

    rims = call(rim_body, shape((2 * chans, rim), BF16), [zero, pre, hi, lo])
    rims_near, rims_far = swap_neighbours(rims)

    t_two, inv, own, delta = call(
        two_body,
        [shape((tall, ext), BF16), shape((count, 1, ext), I32), shape((chans, rows), F32), shape((chans, rim), F32)],
        [ins, outs, cot, weight_two],
        scratch=[pltpu.VMEM((count * (chans + 16), pairs), BF16), pltpu.VMEM((chans, ext), F32)],
        flops=gather_flops + back_flops,
        moved=8 << 20,
    )
    near, far = swap_neighbours(delta)
    keep_two, send_two = call(
        two_weights_body, halves, [pre, rims_near, rims_far, t_two], scratch=[packed_sum], flops=back_flops, moved=6 << 20
    )
    t_one, keep_one, send_one = call(
        one_body,
        [shape((tall, ext), BF16), *halves],
        [own, near, far, hi, lo, pre, zero, rims_near, rims_far, inv],
        scratch=[pltpu.VMEM((chans, rows), BF16), packed_sum],
        flops=gather_flops + back_flops,
        moved=8 << 20,
    )
    grad_two = summed(keep_two, send_two, weight_two.shape, 1.0 / scenes)
    grad_one = summed(keep_one, send_one, weight_one.shape, 1.0 / scenes)
    own, delta = call(
        back_body,
        [shape((chans, rows), F32), shape((chans, rim), F32)],
        [weight_one, t_one],
        scratch=[pltpu.VMEM((chans, ext), F32)],
        flops=back_flops,
        moved=6 << 20,
    )
    near, far = swap_neighbours(delta)
    grad_act = call(settle_body, shape((chans, rows), BF16), [own, near, far, hi, lo])
    return grad_act.T[None, None], grad_one, grad_two


def solution(mesh):
    return jax.shard_map(
        shards,
        mesh=mesh,
        in_specs=(
            P("scan", "space", None, None),
            P("scan", "space", None, None),
            P("scan", "space", None, None),
            P(),
            P(),
            P("scan", "space", None, None),
            P("scan", "space", None, None),
            P("scan", "space", None),
            P("scan", "space", None),
        ),
        out_specs=(P("scan", "space", None, None), P(), P()),
        check_vma=False,
    )
```

```python
import functools

import jax
import jax.numpy as jnp
from jax import lax
from jax.experimental import pallas as pl
from jax.experimental.pallas import tpu as pltpu
from jax.sharding import PartitionSpec as P

F32, BF16, I32 = jnp.float32, jnp.bfloat16, jnp.int32
VMEM = pl.BlockSpec(memory_space=pltpu.VMEM)
HBM = pl.BlockSpec(memory_space=pltpu.HBM)
LANES = 128
BLOCK = 256
WHOLE = 62 << 20
UNROLL = 9
NT = (((1,), (1,)), ((), ()))


def call(body, outs, args, scratch=(), flops=0, moved=0, args_in=VMEM, outs_in=VMEM, room=40 << 20):
    single = not isinstance(outs, (list, tuple))
    return pl.pallas_call(
        body,
        out_shape=outs if single else tuple(outs),
        in_specs=[args_in] * len(args),
        out_specs=outs_in if single or isinstance(outs_in, tuple) else (outs_in,) * len(outs),
        scratch_shapes=scratch,
        compiler_params=pltpu.CompilerParams(vmem_limit_bytes=room),
        cost_estimate=pl.CostEstimate(flops=flops, bytes_accessed=moved, transcendentals=0),
    )(*args)


def shape(dims, dtype):
    return jax.ShapeDtypeStruct(dims, dtype)


def loop(steps, body):
    unroll = next(u for u in range(UNROLL, 0, -1) if steps % u == 0)

    def step(i, carry):
        body(i)
        return carry

    lax.fori_loop(0, steps, step, 0, unroll=unroll)


def one_hot(rows, index):
    count = lax.broadcasted_iota(I32, (min(rows, BLOCK), index.shape[1]), 0).astype(F32).astype(BF16)
    blocks = []
    for start in range(0, rows, BLOCK):
        wanted = (index - start).astype(F32).astype(BF16)
        hit = count[: min(BLOCK, rows - start)] == wanted
        blocks.append(jnp.where(hit, jnp.ones((), BF16), jnp.zeros((), BF16)))
    return jnp.concatenate(blocks, 0)


def dot(a, b):
    return jnp.dot(a, b, preferred_element_type=F32)


def dot_nt(a, b):
    return lax.dot_general(a, b, NT, preferred_element_type=F32)


def offset_rows(k, chans):
    return pl.ds(pl.multiple_of(k * chans, chans), chans)


def rim_index(hi_ref, lo_ref):
    return jnp.concatenate([hi_ref[...], lo_ref[...]], 1)


def first_half(dims, own_parity):
    lane = lax.broadcasted_iota(I32, dims, 1)
    return (lane < dims[1] // 2) == own_parity


def is_even():
    return lax.rem(lax.axis_index("space"), 2) == 0


def add_back(weight_ref, t_ref, total_ref):
    count, chans = weight_ref.shape[0], weight_ref.shape[1]
    total_ref[...] = jnp.zeros_like(total_ref)

    def body(g):
        part = None
        for j in range(3):
            k = g * 3 + j
            term = dot(weight_ref[k], t_ref[offset_rows(k, chans), :])
            part = term if part is None else part + term
        total_ref[...] += part

    assert count % 3 == 0
    loop(count // 3, body)


def split_parts(value):
    high = value.astype(BF16)
    return high, (value - high.astype(F32)).astype(BF16)


def two_body(*refs):
    operands, (t_out, own_ref, edge_ref), scratch = refs[:8], refs[8:11], refs[11:]
    locals_, (t_ref, c_ref, total_ref, sems) = scratch[:8], scratch[8:]
    copies = [
        pltpu.make_async_copy(operand, local, sems.at[i]) for i, (operand, local) in enumerate(zip(operands, locals_, strict=True))
    ]
    for copy in copies:
        copy.start()
    outs_ref, cot_ref, ins_ref, weight_ref, hi_ref, lo_ref, zero_ref, pre_ref = locals_
    count, pairs = ins_ref.shape[0], ins_ref.shape[2]
    chans, rows = cot_ref.shape
    ext = t_ref.shape[1]
    tall = chans + 16
    row = lax.broadcasted_iota(I32, (16, pairs), 0)
    t_ref[count * chans :, :] = jnp.zeros((t_ref.shape[0] - count * chans, ext), BF16)

    def pick_outs(k):
        index = outs_ref[k]
        base = pl.multiple_of(k * tall, 16)
        c_ref[pl.ds(base, chans), :] = dot(cot_ref[...], one_hot(rows, index)).astype(BF16)
        left = rows - index
        code = jnp.where(row == 0, left // 16, jnp.where(row == 1, left % 16, 0))
        c_ref[pl.ds(base + chans, 16), :] = code.astype(F32).astype(BF16)

    copies[0].wait()
    copies[1].wait()
    loop(count, pick_outs)

    def put_ins(k):
        picked = c_ref[pl.ds(pl.multiple_of(k * tall, 16), tall), :]
        placed = dot_nt(picked, one_hot(ext, ins_ref[k]))
        t_ref[offset_rows(k, chans), :] = placed[:chans].astype(BF16)
        code = placed[chans : chans + 1] * 16.0 + placed[chans + 1 : chans + 2]
        own_ref[pl.ds(chans + k, 1), :] = rows - code

    copies[2].wait()
    loop(count, put_ins)
    stored = pltpu.make_async_copy(t_ref, t_out, sems.at[len(operands)])
    stored.start()
    copies[3].wait()
    add_back(weight_ref, t_ref, total_ref)
    own_ref[:chans] = total_ref[...]
    for i, part in enumerate(split_parts(total_ref[:, rows:])):
        edge_ref[i * chans : (i + 1) * chans] = part
    for copy in copies[4:]:
        copy.wait()
    pick = one_hot(rows, rim_index(hi_ref, lo_ref))
    one = jnp.maximum(pre_ref[...], jnp.zeros_like(pre_ref))
    edge_ref[2 * chans : 3 * chans] = dot(zero_ref[...], pick).astype(BF16)
    edge_ref[3 * chans :] = dot(one, pick).astype(BF16)
    stored.wait()


def weight_sums(ext, t_ref, sum_ref, keep_ref, send_ref):
    chans = ext.shape[0]
    tiles = t_ref.shape[0] // LANES
    for start in range(0, tiles, 2):
        width = min(2, tiles - start)
        grad = dot_nt(ext, t_ref[start * LANES : (start + width) * LANES, :])
        for j in range(width):
            sum_ref[(start + j) * chans : (start + j + 1) * chans, :] = grad[:, j * LANES : (j + 1) * LANES]
    sum_ref[tiles * chans :, :] = jnp.zeros((sum_ref.shape[0] - tiles * chans, LANES), F32)
    me = lax.axis_index("space")
    slots = lax.axis_size("space") // 2
    rows = keep_ref.shape[0] // slots
    for slot in range(slots):
        for out_ref, bit in ((keep_ref, 0), (send_ref, 1)):
            piece = jnp.bitwise_xor(me, 2 * slot + bit)
            block = sum_ref[pl.ds(pl.multiple_of(piece * rows, rows), rows), :]
            out_ref[slot * rows : (slot + 1) * rows, :] = block.astype(out_ref.dtype)


def two_weights_body(pre_ref, near_ref, far_ref, t_ref, keep_ref, send_ref, sum_ref):
    chans = pre_ref.shape[0]
    one = jnp.maximum(pre_ref[...], jnp.zeros_like(pre_ref))
    ext = extended(one, near_ref[3 * chans :].astype(F32), far_ref[3 * chans :].astype(F32))
    weight_sums(ext, t_ref, sum_ref, keep_ref, send_ref)


def extended(feats, near, far):
    rim = jnp.where(first_half(near.shape, is_even()), far, near).astype(feats.dtype)
    return jnp.concatenate([feats, rim], 1)


def settled(own, near, far, hi_ref, lo_ref):
    chans = own.shape[0]
    part = jnp.where(first_half(near.shape, is_even()), near.astype(F32), far.astype(F32)).astype(BF16)
    place = one_hot(own.shape[1], rim_index(hi_ref, lo_ref))
    moved = dot_nt(part, place)
    return own + moved[:chans] + moved[chans:]


def one_body(count, own_ref, near_ref, far_ref, hi_ref, lo_ref, pre_ref, zero_ref, t_ref, keep_ref, send_ref, cot_ref, sum_ref):
    chans, rows = pre_ref.shape
    ext = own_ref.shape[1]
    back = settled(own_ref[:chans, :rows], near_ref[: 2 * chans], far_ref[: 2 * chans], hi_ref, lo_ref)
    cot_ref[...] = jnp.where(pre_ref[...].astype(F32) > 0, back, 0.0).astype(BF16)

    def place(k):
        t_ref[offset_rows(k, chans), :] = dot(cot_ref[...], one_hot(rows, own_ref[pl.ds(chans + k, 1), :])).astype(BF16)

    loop(count, place)
    t_ref[count * chans :, :] = jnp.zeros((t_ref.shape[0] - count * chans, ext), BF16)
    rim = slice(2 * chans, 3 * chans)
    feats = extended(zero_ref[...], near_ref[rim].astype(F32), far_ref[rim].astype(F32))
    weight_sums(feats, t_ref, sum_ref, keep_ref, send_ref)


def back_body(weight_ref, t_ref, own_ref, edge_ref, total_ref):
    chans, rows = own_ref.shape
    add_back(weight_ref, t_ref, total_ref)
    own_ref[...] = total_ref[:, :rows]
    for i, part in enumerate(split_parts(total_ref[:, rows:])):
        edge_ref[i * chans : (i + 1) * chans] = part


def settle_body(own_ref, near_ref, far_ref, hi_ref, lo_ref, out_ref):
    out_ref[...] = settled(own_ref[...], near_ref[...], far_ref[...], hi_ref, lo_ref).astype(BF16)


def core_sum_body(layers, *refs):
    ins, (own_ref, *send_refs) = refs[: 2 * layers], refs[2 * layers :]
    rows = own_ref.shape[0] // layers
    for layer in range(layers):
        keep_ref, got_ref = ins[2 * layer : 2 * layer + 2]
        there = slice(layer * rows, (layer + 1) * rows)
        own_ref[there] = keep_ref[:rows] + got_ref[:rows].astype(F32)
        for slot, send_ref in enumerate(send_refs, 1):
            part = slice(slot * rows, (slot + 1) * rows)
            send_ref[there] = (keep_ref[part] + got_ref[part].astype(F32)).astype(BF16)


def chip_sum_body(own_ref, *refs):
    total = own_ref[...]
    for got_ref in refs[:-1]:
        total = total + got_ref[...].astype(F32)
    refs[-1][...] = total.astype(BF16)


def scan_sum_body(*refs):
    terms = [ref[...].astype(F32) for ref in refs[:-1]]
    while len(terms) > 1:
        terms = [a + b for a, b in zip(terms[::2], terms[1::2], strict=True)]
    refs[-1][...] = terms[0].astype(BF16)


def unpack_body(scale, layers, *refs):
    *refs, all_ref, sems = refs
    piece_refs, outs, locals_ = refs[: -2 * layers], refs[-2 * layers : -layers], refs[-layers:]
    me = lax.axis_index("space")
    rows = piece_refs[0].shape[0] // layers
    count, chans = locals_[0].shape[0], locals_[0].shape[1]
    lane = lax.broadcasted_iota(I32, (chans, LANES), 1)
    copies = []
    for layer in range(layers):
        for slot, piece_ref in enumerate(piece_refs):
            piece = jnp.bitwise_xor(me, slot)
            block = piece_ref[layer * rows : (layer + 1) * rows].astype(F32)
            all_ref[pl.ds(pl.multiple_of(piece * rows, rows), rows), :] = block
        for k in range(count):
            tile, shift = divmod(k * chans, LANES)
            block = all_ref[tile * chans : (tile + 1) * chans, :]
            if shift:
                block = pltpu.roll(block, LANES - shift, 1)
            if shift + chans > LANES:
                after = pltpu.roll(all_ref[(tile + 1) * chans : (tile + 2) * chans, :], LANES - shift, 1)
                block = jnp.where(lane < LANES - shift, block, after)
            locals_[layer][k] = block[:, :chans] * scale
        copies.append(pltpu.make_async_copy(locals_[layer], outs[layer], sems.at[layer]))
        copies[-1].start()
    for copy in copies:
        copy.wait()


def swap(block, axis, bit):
    return lax.ppermute(block, axis, [(i, i ^ bit) for i in range(lax.axis_size(axis))])


def swap_neighbours(block):
    bricks = lax.axis_size("space")
    near = swap(block, "space", 1)
    inner = range(1, bricks - 1)
    far = lax.ppermute(block, "space", [(i, i + 1 if i % 2 else i - 1) for i in inner])
    return near, far


def summed(parts, weight_shape, scale, beside):
    layers = len(parts)
    slots = lax.axis_size("space") // 2
    scans = lax.axis_size("scan")
    packed = 2 * parts[0][0].shape[0]
    rows = layers * packed // (2 * slots)
    outs = [shape((rows, LANES), F32)] + [shape((rows, LANES), BF16)] * (slots - 1)
    own, *sends = call(functools.partial(core_sum_body, layers), outs, [x for part in parts for x in part])
    gots = [swap(block, "space", 2 * slot) for slot, block in enumerate(sends, 1)]
    own, step = beside[0](own)
    part = call(chip_sum_body, shape((rows, LANES), BF16), [own, *gots])
    if scans & (scans - 1):
        part, result = beside[1](part, step)
        total = lax.psum(part, "scan")
    else:
        terms = [part] + [swap(part, "scan", bit) for bit in range(1, scans)]
        terms[0], result = beside[1](terms[0], step)
        total = call(scan_sum_body, shape((rows, LANES), BF16), terms)
    pieces = []
    for slot in range(slots):
        piece = swap(total, "space", 2 * slot) if slot else total
        pieces += [piece, swap(piece, "space", 1)]
    return result, call(
        functools.partial(unpack_body, scale, layers),
        [shape(weight_shape, F32)] * layers,
        pieces,
        scratch=[pltpu.VMEM(weight_shape, F32)] * layers + [pltpu.VMEM((packed, LANES), F32), pltpu.SemaphoreType.DMA((layers,))],
        outs_in=HBM,
    )


def shards(act_zero, pre_act, cot_out, weight_one, weight_two, in_map, out_map, send_lo, send_hi):
    zero, pre, cot = (x[0, 0].T for x in (act_zero, pre_act, cot_out))
    ins, outs = (x[0, 0][:, None, :] for x in (in_map, out_map))
    lo, hi = send_lo[0], send_hi[0]
    chans, rows = zero.shape
    count, _, pairs = ins.shape
    rim = 2 * lo.shape[1]
    ext = rows + rim
    scenes = lax.axis_size("scan")
    bricks = lax.axis_size("space")
    tiles = -(-count * chans // LANES)
    tall = tiles * LANES
    unit = 16 * bricks
    packed = -(-tiles * chans // unit) * unit
    halves = [shape((packed // 2, LANES), F32), shape((packed // 2, LANES), BF16)]
    packed_sum = pltpu.VMEM((packed, LANES), F32)
    gather_flops = 2 * count * chans * ext * rows
    back_flops = 2 * count * chans * chans * ext

    operands = [outs, cot, ins, weight_two, hi, lo, zero, pre]
    t_two, own, edge = call(
        two_body,
        [shape((tall, ext), BF16), shape((chans + -(-count // 8) * 8, ext), F32), shape((4 * chans, rim), BF16)],
        operands,
        scratch=[pltpu.VMEM(x.shape, x.dtype) for x in operands]
        + [
            pltpu.VMEM((tall, ext), BF16),
            pltpu.VMEM((count * (chans + 16), pairs), BF16),
            pltpu.VMEM((chans, ext), F32),
            pltpu.SemaphoreType.DMA((len(operands) + 1,)),
        ],
        flops=gather_flops + back_flops,
        moved=8 << 20,
        args_in=HBM,
        outs_in=(HBM, VMEM, VMEM),
        room=WHOLE,
    )
    near, far = swap_neighbours(edge)
    t_one, keep_one, send_one = call(
        functools.partial(one_body, count),
        [shape((tall, ext), BF16), *halves],
        [own, near, far, hi, lo, pre, zero],
        scratch=[pltpu.VMEM((chans, rows), BF16), packed_sum],
        flops=gather_flops + back_flops,
        moved=8 << 20,
    )
    got_one = swap(send_one, "space", 1)
    near, far, t_one = lax.optimization_barrier((near, far, t_one))
    keep_two, send_two = call(two_weights_body, halves, [pre, near, far, t_two], scratch=[packed_sum], flops=back_flops, moved=6 << 20)
    got_two = swap(send_two, "space", 1)
    t_one, keep_two = lax.optimization_barrier((t_one, keep_two))
    own, edge = call(
        back_body,
        [shape((chans, rows), F32), shape((2 * chans, rim), BF16)],
        [weight_one, t_one],
        scratch=[pltpu.VMEM((chans, ext), F32)],
        flops=back_flops,
        moved=6 << 20,
    )
    keep_one, edge = lax.optimization_barrier((keep_one, edge))
    def swap_edges(held):
        held, block = lax.optimization_barrier((held, edge))
        near, far = swap_neighbours(block)
        held, near, far = lax.optimization_barrier((held, near, far))
        return held, (near, far)

    def settle(held, edges):
        held, own_rows, near, far = lax.optimization_barrier((held, own, *edges))
        grad_act = call(settle_body, shape((chans, rows), BF16), [own_rows, near, far, hi, lo])
        return lax.optimization_barrier((held, grad_act))

    grad_act, (grad_one, grad_two) = summed(
        [(keep_one, got_one), (keep_two, got_two)], weight_one.shape, 1.0 / scenes, (swap_edges, settle)
    )
    return grad_act.T[None, None], grad_one, grad_two


def solution(mesh):
    return jax.shard_map(
        shards,
        mesh=mesh,
        in_specs=(
            P("scan", "space", None, None),
            P("scan", "space", None, None),
            P("scan", "space", None, None),
            P(),
            P(),
            P("scan", "space", None, None),
            P("scan", "space", None, None),
            P("scan", "space", None),
            P("scan", "space", None),
        ),
        out_specs=(P("scan", "space", None, None), P(), P()),
        check_vma=False,
    )
```

```python
import functools

import jax
import jax.numpy as jnp
from jax import lax
from jax.experimental import pallas as pl
from jax.experimental.pallas import tpu as pltpu
from jax.sharding import PartitionSpec as P

F32, BF16, I32 = jnp.float32, jnp.bfloat16, jnp.int32
VMEM = pl.BlockSpec(memory_space=pltpu.VMEM)
HBM = pl.BlockSpec(memory_space=pltpu.HBM)
LANES = 128
BLOCK = 256
CHUNK = 9
WHOLE = 62 << 20
UNROLL = 9
NT = (((1,), (1,)), ((), ()))


def call(body, outs, args, scratch=(), flops=0, moved=0, args_in=VMEM, outs_in=VMEM, room=40 << 20):
    single = not isinstance(outs, (list, tuple))
    return pl.pallas_call(
        body,
        out_shape=outs if single else tuple(outs),
        in_specs=[args_in] * len(args),
        out_specs=outs_in if single or isinstance(outs_in, tuple) else (outs_in,) * len(outs),
        scratch_shapes=scratch,
        compiler_params=pltpu.CompilerParams(vmem_limit_bytes=room),
        cost_estimate=pl.CostEstimate(flops=flops, bytes_accessed=moved, transcendentals=0),
    )(*args)


def shape(dims, dtype):
    return jax.ShapeDtypeStruct(dims, dtype)


def loop(steps, body):
    unroll = next(u for u in range(UNROLL, 0, -1) if steps % u == 0)

    def step(i, carry):
        body(i)
        return carry

    lax.fori_loop(0, steps, step, 0, unroll=unroll)


def one_hot(rows, index):
    count = lax.broadcasted_iota(I32, (min(rows, BLOCK), index.shape[1]), 0).astype(F32).astype(BF16)
    blocks = []
    for start in range(0, rows, BLOCK):
        wanted = (index - start).astype(F32).astype(BF16)
        hit = count[: min(BLOCK, rows - start)] == wanted
        blocks.append(jnp.where(hit, jnp.ones((), BF16), jnp.zeros((), BF16)))
    return jnp.concatenate(blocks, 0)


def dot(a, b):
    return jnp.dot(a, b, preferred_element_type=F32)


def dot_nt(a, b):
    return lax.dot_general(a, b, NT, preferred_element_type=F32)


def offset_rows(k, chans):
    return pl.ds(pl.multiple_of(k * chans, chans), chans)


def rim_index(hi_ref, lo_ref):
    return jnp.concatenate([hi_ref[...], lo_ref[...]], 1)


def halves(x, y):
    x, y = x.astype(F32), y.astype(F32)
    width = x.shape[1]
    left = lax.broadcasted_iota(I32, x.shape, 1) < width // 2
    return jnp.where(left, x, pltpu.roll(y, width // 2, 1)), jnp.where(left, pltpu.roll(x, width // 2, 1), y)


def by_parity(x, y):
    even = lax.rem(lax.axis_index("space"), 2) == 0
    return jnp.where(even, x, y), jnp.where(even, y, x)


def put_edges(near_ref, far_ref, at, up, down):
    rows = slice(at, at + up.shape[0])
    for ref, value in zip((near_ref, far_ref), by_parity(up, down), strict=True):
        ref[rows] = value.astype(BF16)


def rim_gradients(near_ref, far_ref, total):
    high = total.astype(BF16).astype(F32)
    down, up = halves(high, total - high)
    put_edges(near_ref, far_ref, 0, up, down)


def add_back(weight_ref, t_ref, total_ref):
    count, chans = weight_ref.shape[0], weight_ref.shape[1]
    total_ref[...] = jnp.zeros_like(total_ref)

    def body(g):
        part = None
        for j in range(3):
            k = g * 3 + j
            term = dot(weight_ref[k], t_ref[offset_rows(k, chans), :])
            part = term if part is None else part + term
        total_ref[...] += part

    assert count % 3 == 0
    loop(count // 3, body)


def two_body(*refs):
    operands, (t_out, own_ref, near_ref, far_ref), scratch = refs[:8], refs[8:12], refs[12:]
    locals_, (t_ref, c_ref, total_ref, sems) = scratch[:8], scratch[8:]
    copies = [
        pltpu.make_async_copy(operand, local, sems.at[i]) for i, (operand, local) in enumerate(zip(operands, locals_, strict=True))
    ]
    for copy in copies:
        copy.start()
    outs_ref, cot_ref, ins_ref, weight_ref, hi_ref, lo_ref, zero_ref, pre_ref = locals_
    count, pairs = ins_ref.shape[0], ins_ref.shape[2]
    chans, rows = cot_ref.shape
    ext = t_ref.shape[1]
    tall = chans + 16
    row = lax.broadcasted_iota(I32, (16, pairs), 0)
    t_ref[count * chans :, :] = jnp.zeros((t_ref.shape[0] - count * chans, ext), BF16)

    def pick_outs(k):
        index = outs_ref[k]
        base = pl.multiple_of(k * tall, 16)
        c_ref[pl.ds(base, chans), :] = dot(cot_ref[...], one_hot(rows, index)).astype(BF16)
        left = rows - index
        code = jnp.where(row == 0, left // 16, jnp.where(row == 1, left % 16, 0))
        c_ref[pl.ds(base + chans, 16), :] = code.astype(F32).astype(BF16)

    copies[0].wait()
    copies[1].wait()
    loop(count, pick_outs)

    def put_ins(k):
        picked = c_ref[pl.ds(pl.multiple_of(k * tall, 16), tall), :]
        placed = dot_nt(picked, one_hot(ext, ins_ref[k]))
        t_ref[offset_rows(k, chans), :] = placed[:chans].astype(BF16)
        code = placed[chans : chans + 1] * 16.0 + placed[chans + 1 : chans + 2]
        own_ref[pl.ds(chans + k, 1), :] = rows - code

    copies[2].wait()
    loop(count, put_ins)
    stored = pltpu.make_async_copy(t_ref, t_out, sems.at[len(operands)])
    stored.start()
    copies[3].wait()
    add_back(weight_ref, t_ref, total_ref)
    own_ref[:chans] = total_ref[...]
    rim_gradients(near_ref, far_ref, total_ref[:, rows:])
    for copy in copies[4:]:
        copy.wait()
    pick = one_hot(rows, rim_index(hi_ref, lo_ref))
    one = jnp.maximum(pre_ref[...], jnp.zeros_like(pre_ref))
    up, down = halves(dot(zero_ref[...], pick), dot(one, pick))
    put_edges(near_ref, far_ref, chans, up, down)
    stored.wait()


def packed_products(feats, t_ref, columns, sum_ref, base_ref=None):
    chans = feats.shape[0]
    tiles = t_ref.shape[0] // LANES
    for start in range(0, tiles, 2):
        width = min(2, tiles - start)
        grad = dot_nt(feats, t_ref[start * LANES : (start + width) * LANES, columns])
        for j in range(width):
            rows = slice((start + j) * chans, (start + j + 1) * chans)
            block = grad[:, j * LANES : (j + 1) * LANES]
            sum_ref[rows, :] = block if base_ref is None else block + base_ref[rows, :]
    sum_ref[tiles * chans :, :] = jnp.zeros((sum_ref.shape[0] - tiles * chans, LANES), F32)


def cut(sum_ref, layer, keep_ref, send_ref):
    me = lax.axis_index("space")
    slots = lax.axis_size("space") // 2
    rows = sum_ref.shape[0] // (2 * slots)
    for slot in range(slots):
        there = pl.ds((layer * slots + slot) * rows, rows)
        for out_ref, bit in ((keep_ref, 0), (send_ref, 1)):
            piece = jnp.bitwise_xor(me, 2 * slot + bit)
            block = sum_ref[pl.ds(pl.multiple_of(piece * rows, rows), rows), :]
            out_ref[there, :] = block.astype(out_ref.dtype)


def two_weights_body(pre_ref, t_ref, sum_ref):
    one = jnp.maximum(pre_ref[...], jnp.zeros_like(pre_ref))
    packed_products(one, t_ref, slice(0, one.shape[1]), sum_ref)


def settled(own, near, far, hi_ref, lo_ref):
    above, below = by_parity(near, far)
    place = one_hot(own.shape[1], rim_index(hi_ref, lo_ref))
    for part in halves(above, below):
        own = own + dot_nt(part.astype(BF16), place)
    return own


def one_body(
    count, own_ref, near_ref, far_ref, hi_ref, lo_ref, pre_ref, zero_ref, t_two_ref, sum_two_ref, t_ref, keep_ref, send_ref, cot_ref, sum_ref
):
    chans, rows = pre_ref.shape
    ext = own_ref.shape[1]
    back = settled(own_ref[:chans, :rows], near_ref[:chans], far_ref[:chans], hi_ref, lo_ref)
    cot_ref[...] = jnp.where(pre_ref[...].astype(F32) > 0, back, 0.0).astype(BF16)

    def place(k):
        t_ref[offset_rows(k, chans), :] = dot(cot_ref[...], one_hot(rows, own_ref[pl.ds(chans + k, 1), :])).astype(BF16)

    loop(count, place)
    t_ref[count * chans :, :] = jnp.zeros((t_ref.shape[0] - count * chans, ext), BF16)
    above, below = by_parity(near_ref[chans:], far_ref[chans:])
    zero_rim, one_rim = halves(below, above)
    feats = jnp.concatenate([zero_ref[...], zero_rim.astype(BF16)], 1)
    packed_products(feats, t_ref, slice(0, ext), sum_ref)
    cut(sum_ref, 0, keep_ref, send_ref)
    packed_products(one_rim.astype(BF16), t_two_ref, slice(rows, ext), sum_ref, sum_two_ref)
    cut(sum_ref, 1, keep_ref, send_ref)


def back_body(weight_ref, t_ref, own_ref, near_ref, far_ref, total_ref):
    rows = own_ref.shape[1]
    add_back(weight_ref, t_ref, total_ref)
    own_ref[...] = total_ref[:, :rows]
    rim_gradients(near_ref, far_ref, total_ref[:, rows:])


def settle_body(own_ref, near_ref, far_ref, hi_ref, lo_ref, out_ref):
    out_ref[...] = settled(own_ref[...], near_ref[...], far_ref[...], hi_ref, lo_ref).astype(BF16)


def core_sum_body(layers, keep_ref, got_ref, own_ref, *send_refs):
    rows = own_ref.shape[0] // layers
    slots = len(send_refs) + 1
    for layer in range(layers):
        there = slice(layer * rows, (layer + 1) * rows)
        for slot, out_ref in enumerate((own_ref, *send_refs)):
            part = slice((layer * slots + slot) * rows, (layer * slots + slot + 1) * rows)
            out_ref[there] = (keep_ref[part] + got_ref[part].astype(F32)).astype(out_ref.dtype)


def chip_sum_body(own_ref, *refs):
    total = own_ref[...]
    for got_ref in refs[:-1]:
        total = total + got_ref[...].astype(F32)
    refs[-1][...] = total.astype(BF16)


def scan_sum_body(own_ref, got_ref, total_ref):
    total_ref[...] = (own_ref[...].astype(F32) + got_ref[...].astype(F32)).astype(BF16)


def unpack_body(scale, layers, *refs):
    *refs, all_ref, sems = refs
    piece_refs, outs, locals_ = refs[: -2 * layers], refs[-2 * layers : -layers], refs[-layers:]
    me = lax.axis_index("space")
    rows = piece_refs[0].shape[0] // layers
    count, chans = locals_[0].shape[0], locals_[0].shape[1]
    lane = lax.broadcasted_iota(I32, (chans, LANES), 1)
    copies = []
    for layer in range(layers):
        for slot, piece_ref in enumerate(piece_refs):
            piece = jnp.bitwise_xor(me, slot)
            block = piece_ref[layer * rows : (layer + 1) * rows].astype(F32)
            all_ref[pl.ds(pl.multiple_of(piece * rows, rows), rows), :] = block
        for first in range(0, count, CHUNK):
            chunk = pl.ds(first, min(CHUNK, count - first))
            for k in range(first, first + chunk.size):
                tile, shift = divmod(k * chans, LANES)
                block = all_ref[tile * chans : (tile + 1) * chans, :]
                if shift:
                    block = pltpu.roll(block, LANES - shift, 1)
                if shift + chans > LANES:
                    after = pltpu.roll(all_ref[(tile + 1) * chans : (tile + 2) * chans, :], LANES - shift, 1)
                    block = jnp.where(lane < LANES - shift, block, after)
                locals_[layer][k] = block[:, :chans] * scale
            copies.append(pltpu.make_async_copy(locals_[layer].at[chunk], outs[layer].at[chunk], sems.at[len(copies)]))
            copies[-1].start()
    for copy in copies:
        copy.wait()


def swap(block, axis, bit):
    return lax.ppermute(block, axis, [(i, i ^ bit) for i in range(lax.axis_size(axis))])


def swap_neighbours(near, far):
    inner = range(1, lax.axis_size("space") - 1)
    far = lax.ppermute(far, "space", [(i, i + 1 if i % 2 else i - 1) for i in inner])
    return swap(near, "space", 1), far


def swap_scans(block, step, steps):
    scans = lax.axis_size("scan")
    bits = (1 << step, 1 << (steps - 1 - step))
    bricks = range(lax.axis_size("space"))
    pairs = [(b * scans + z, b * scans + (z ^ bits[b % 2])) for b in bricks for z in range(scans)]
    return lax.ppermute(block, ("space", "scan"), pairs)


def summed(keep, got, layers, weight_shape, scale, beside):
    slots = lax.axis_size("space") // 2
    scans = lax.axis_size("scan")
    packed = 2 * keep.shape[0] // layers
    rows = keep.shape[0] // slots
    outs = [shape((rows, LANES), F32)] + [shape((rows, LANES), BF16)] * (slots - 1)
    own, *sends = call(functools.partial(core_sum_body, layers), outs, [keep, got])
    gots = [swap(block, "space", 2 * slot) for slot, block in enumerate(sends, 1)]
    total = call(chip_sum_body, shape((rows, LANES), BF16), [own, *gots])
    waiting = list(beside)
    state = None
    if scans & (scans - 1):
        total = lax.psum(total, "scan")
    else:
        steps = scans.bit_length() - 1
        for step in range(steps):
            more = swap_scans(total, step, steps)
            if waiting:
                total, state = waiting.pop(0)(total, state)
            total = call(scan_sum_body, shape((rows, LANES), BF16), [total, more])
    for work in waiting:
        total, state = work(total, state)
    pieces = []
    for slot in range(slots):
        piece = swap(total, "space", 2 * slot) if slot else total
        pieces += [piece, swap(piece, "space", 1)]
    return state, call(
        functools.partial(unpack_body, scale, layers),
        [shape(weight_shape, F32)] * layers,
        pieces,
        scratch=[pltpu.VMEM(weight_shape, F32)] * layers + [pltpu.VMEM((packed, LANES), F32), pltpu.SemaphoreType.DMA((layers * -(-weight_shape[0] // CHUNK),))],
        outs_in=HBM,
    )


def shards(act_zero, pre_act, cot_out, weight_one, weight_two, in_map, out_map, send_lo, send_hi):
    zero, pre, cot = (x[0, 0].T for x in (act_zero, pre_act, cot_out))
    ins, outs = (x[0, 0][:, None, :] for x in (in_map, out_map))
    lo, hi = send_lo[0], send_hi[0]
    chans, rows = zero.shape
    count, _, pairs = ins.shape
    rim = 2 * lo.shape[1]
    ext = rows + rim
    scenes = lax.axis_size("scan")
    bricks = lax.axis_size("space")
    tiles = -(-count * chans // LANES)
    tall = tiles * LANES
    unit = 16 * bricks
    packed = -(-tiles * chans // unit) * unit
    gather_flops = 2 * count * chans * ext * rows
    back_flops = 2 * count * chans * chans * ext

    operands = [outs, cot, ins, weight_two, hi, lo, zero, pre]
    t_two, own, near, far = call(
        two_body,
        [shape((tall, ext), BF16), shape((chans + -(-count // 8) * 8, ext), F32), shape((2 * chans, rim), BF16), shape((2 * chans, rim), BF16)],
        operands,
        scratch=[pltpu.VMEM(x.shape, x.dtype) for x in operands]
        + [
            pltpu.VMEM((tall, ext), BF16),
            pltpu.VMEM((count * (chans + 16), pairs), BF16),
            pltpu.VMEM((chans, ext), F32),
            pltpu.SemaphoreType.DMA((len(operands) + 1,)),
        ],
        flops=gather_flops + back_flops,
        moved=8 << 20,
        args_in=HBM,
        outs_in=(HBM, VMEM, VMEM, VMEM),
        room=WHOLE,
    )
    near, far = swap_neighbours(near, far)
    sum_two = call(two_weights_body, shape((packed, LANES), F32), [pre, t_two], flops=back_flops, moved=6 << 20)
    t_one, keep, send = call(
        functools.partial(one_body, count),
        [shape((tall, ext), BF16), shape((packed, LANES), F32), shape((packed, LANES), BF16)],
        [own, near, far, hi, lo, pre, zero, t_two, sum_two],
        scratch=[pltpu.VMEM((chans, rows), BF16), pltpu.VMEM((packed, LANES), F32)],
        flops=gather_flops + back_flops,
        moved=8 << 20,
    )
    got = swap(send, "space", 1)
    own, near, far = call(
        back_body,
        [shape((chans, rows), F32), shape((chans, rim), BF16), shape((chans, rim), BF16)],
        [weight_one, t_one],
        scratch=[pltpu.VMEM((chans, ext), F32)],
        flops=back_flops,
        moved=6 << 20,
    )
    keep, near, far = lax.optimization_barrier((keep, near, far))

    def swap_edges(held, _):
        held, *edges = lax.optimization_barrier((held, near, far))
        held, *edges = lax.optimization_barrier((held, *swap_neighbours(*edges)))
        return held, edges

    def settle(held, edges):
        held, own_rows, *edges = lax.optimization_barrier((held, own, *edges))
        grad_act = call(settle_body, shape((chans, rows), BF16), [own_rows, *edges, hi, lo])
        return lax.optimization_barrier((held, grad_act))

    grad_act, (grad_one, grad_two) = summed(keep, got, 2, weight_one.shape, 1.0 / scenes, (swap_edges, settle))
    return grad_act.T[None, None], grad_one, grad_two


def solution(mesh):
    return jax.shard_map(
        shards,
        mesh=mesh,
        in_specs=(
            P("scan", "space", None, None),
            P("scan", "space", None, None),
            P("scan", "space", None, None),
            P(),
            P(),
            P("scan", "space", None, None),
            P("scan", "space", None, None),
            P("scan", "space", None),
            P("scan", "space", None),
        ),
        out_specs=(P("scan", "space", None, None), P(), P()),
        check_vma=False,
    )
```

```python
import functools

import jax
import jax.numpy as jnp
from jax import lax
from jax.experimental import pallas as pl
from jax.experimental.pallas import tpu as pltpu
from jax.sharding import PartitionSpec as P

F32, BF16, I32 = jnp.float32, jnp.bfloat16, jnp.int32
VMEM = pl.BlockSpec(memory_space=pltpu.VMEM)
HBM = pl.BlockSpec(memory_space=pltpu.HBM)
LANES = 128
BLOCK = 256
CHUNK = 9
WHOLE = 62 << 20
UNROLL = 9
NT = (((1,), (1,)), ((), ()))


def call(body, outs, args, scratch=(), flops=0, moved=0, args_in=VMEM, outs_in=VMEM, room=40 << 20):
    single = not isinstance(outs, (list, tuple))
    return pl.pallas_call(
        body,
        out_shape=outs if single else tuple(outs),
        in_specs=[args_in] * len(args),
        out_specs=outs_in if single or isinstance(outs_in, tuple) else (outs_in,) * len(outs),
        scratch_shapes=scratch,
        compiler_params=pltpu.CompilerParams(vmem_limit_bytes=room),
        cost_estimate=pl.CostEstimate(flops=flops, bytes_accessed=moved, transcendentals=0),
    )(*args)


def shape(dims, dtype):
    return jax.ShapeDtypeStruct(dims, dtype)


def loop(steps, body):
    unroll = next(u for u in range(UNROLL, 0, -1) if steps % u == 0)

    def step(i, carry):
        body(i)
        return carry

    lax.fori_loop(0, steps, step, 0, unroll=unroll)


def one_hot(rows, index):
    count = lax.broadcasted_iota(I32, (min(rows, BLOCK), index.shape[1]), 0).astype(F32).astype(BF16)
    blocks = []
    for start in range(0, rows, BLOCK):
        wanted = (index - start).astype(F32).astype(BF16)
        hit = count[: min(BLOCK, rows - start)] == wanted
        blocks.append(jnp.where(hit, jnp.ones((), BF16), jnp.zeros((), BF16)))
    return jnp.concatenate(blocks, 0)


def dot(a, b):
    return jnp.dot(a, b, preferred_element_type=F32)


def dot_nt(a, b):
    return lax.dot_general(a, b, NT, preferred_element_type=F32)


def offset_rows(k, chans):
    return pl.ds(pl.multiple_of(k * chans, chans), chans)


def rim_index(hi_ref, lo_ref):
    return jnp.concatenate([hi_ref[...], lo_ref[...]], 1)


def halves(x, y):
    x, y = x.astype(F32), y.astype(F32)
    width = x.shape[1]
    left = lax.broadcasted_iota(I32, x.shape, 1) < width // 2
    return jnp.where(left, x, pltpu.roll(y, width // 2, 1)), jnp.where(left, pltpu.roll(x, width // 2, 1), y)


def by_parity(x, y):
    even = lax.rem(lax.axis_index("space"), 2) == 0
    return jnp.where(even, x, y), jnp.where(even, y, x)


def put_edges(near_ref, far_ref, at, up, down):
    rows = slice(at, at + up.shape[0])
    for ref, value in zip((near_ref, far_ref), by_parity(up, down), strict=True):
        ref[rows] = value.astype(BF16)


def rim_gradients(near_ref, far_ref, total):
    high = total.astype(BF16).astype(F32)
    down, up = halves(high, total - high)
    put_edges(near_ref, far_ref, 0, up, down)


def add_back(weight_ref, t_ref, total_ref):
    count, chans = weight_ref.shape[0], weight_ref.shape[1]
    total_ref[...] = jnp.zeros_like(total_ref)

    def body(g):
        part = None
        for j in range(3):
            k = g * 3 + j
            term = dot(weight_ref[k], t_ref[offset_rows(k, chans), :])
            part = term if part is None else part + term
        total_ref[...] += part

    assert count % 3 == 0
    loop(count // 3, body)


def pick_body(outs_ref, cot_ref, c_ref):
    chans, rows = cot_ref.shape
    pairs = outs_ref.shape[2]
    tall = chans + 16
    row = lax.broadcasted_iota(I32, (16, pairs), 0)

    def pick(k):
        index = outs_ref[k]
        base = pl.multiple_of(k * tall, 16)
        c_ref[pl.ds(base, chans), :] = dot(cot_ref[...], one_hot(rows, index)).astype(BF16)
        left = rows - index
        code = jnp.where(row == 0, left // 16, jnp.where(row == 1, left % 16, 0))
        c_ref[pl.ds(base + chans, 16), :] = code.astype(F32).astype(BF16)

    loop(outs_ref.shape[0], pick)


def two_body(ins_ref, c_ref, weight_ref, hi_ref, lo_ref, zero_ref, pre_ref, t_ref, own_ref, near_ref, far_ref, total_ref):
    count = ins_ref.shape[0]
    chans, rows = zero_ref.shape
    ext = t_ref.shape[1]
    tall = chans + 16
    t_ref[count * chans :, :] = jnp.zeros((t_ref.shape[0] - count * chans, ext), BF16)

    def place(k):
        picked = c_ref[pl.ds(pl.multiple_of(k * tall, 16), tall), :]
        placed = dot_nt(picked, one_hot(ext, ins_ref[k]))
        t_ref[offset_rows(k, chans), :] = placed[:chans].astype(BF16)
        code = placed[chans : chans + 1] * 16.0 + placed[chans + 1 : chans + 2]
        own_ref[pl.ds(chans + k, 1), :] = rows - code

    loop(count, place)
    add_back(weight_ref, t_ref, total_ref)
    own_ref[:chans] = total_ref[...]
    rim_gradients(near_ref, far_ref, total_ref[:, rows:])
    pick = one_hot(rows, rim_index(hi_ref, lo_ref))
    one = jnp.maximum(pre_ref[...], jnp.zeros_like(pre_ref))
    up, down = halves(dot(zero_ref[...], pick), dot(one, pick))
    put_edges(near_ref, far_ref, chans, up, down)


def packed_products(feats, t_ref, columns, sum_ref, base_ref=None):
    chans = feats.shape[0]
    tiles = t_ref.shape[0] // LANES
    for start in range(0, tiles, 2):
        width = min(2, tiles - start)
        grad = dot_nt(feats, t_ref[start * LANES : (start + width) * LANES, columns])
        for j in range(width):
            rows = slice((start + j) * chans, (start + j + 1) * chans)
            block = grad[:, j * LANES : (j + 1) * LANES]
            sum_ref[rows, :] = block if base_ref is None else block + base_ref[rows, :]
    sum_ref[tiles * chans :, :] = jnp.zeros((sum_ref.shape[0] - tiles * chans, LANES), F32)


def cut(sum_ref, layer, keep_ref, send_ref):
    me = lax.axis_index("space")
    slots = lax.axis_size("space") // 2
    rows = sum_ref.shape[0] // (2 * slots)
    for slot in range(slots):
        there = pl.ds((layer * slots + slot) * rows, rows)
        for out_ref, bit in ((keep_ref, 0), (send_ref, 1)):
            piece = jnp.bitwise_xor(me, 2 * slot + bit)
            block = sum_ref[pl.ds(pl.multiple_of(piece * rows, rows), rows), :]
            out_ref[there, :] = block.astype(out_ref.dtype)


def two_weights_body(pre_ref, t_ref, sum_ref):
    one = jnp.maximum(pre_ref[...], jnp.zeros_like(pre_ref))
    packed_products(one, t_ref, slice(0, one.shape[1]), sum_ref)


def settled(own, near, far, hi_ref, lo_ref):
    above, below = by_parity(near, far)
    place = one_hot(own.shape[1], rim_index(hi_ref, lo_ref))
    for part in halves(above, below):
        own = own + dot_nt(part.astype(BF16), place)
    return own


def one_body(
    count, own_ref, near_ref, far_ref, hi_ref, lo_ref, pre_ref, zero_ref, t_two_ref, sum_two_ref, t_ref, keep_ref, send_ref, cot_ref, sum_ref
):
    chans, rows = pre_ref.shape
    ext = own_ref.shape[1]
    back = settled(own_ref[:chans, :rows], near_ref[:chans], far_ref[:chans], hi_ref, lo_ref)
    cot_ref[...] = jnp.where(pre_ref[...].astype(F32) > 0, back, 0.0).astype(BF16)

    def place(k):
        t_ref[offset_rows(k, chans), :] = dot(cot_ref[...], one_hot(rows, own_ref[pl.ds(chans + k, 1), :])).astype(BF16)

    loop(count, place)
    t_ref[count * chans :, :] = jnp.zeros((t_ref.shape[0] - count * chans, ext), BF16)
    above, below = by_parity(near_ref[chans:], far_ref[chans:])
    zero_rim, one_rim = halves(below, above)
    feats = jnp.concatenate([zero_ref[...], zero_rim.astype(BF16)], 1)
    packed_products(feats, t_ref, slice(0, ext), sum_ref)
    cut(sum_ref, 0, keep_ref, send_ref)
    packed_products(one_rim.astype(BF16), t_two_ref, slice(rows, ext), sum_ref, sum_two_ref)
    cut(sum_ref, 1, keep_ref, send_ref)


def back_body(weight_ref, t_ref, own_ref, near_ref, far_ref, total_ref):
    rows = own_ref.shape[1]
    add_back(weight_ref, t_ref, total_ref)
    own_ref[...] = total_ref[:, :rows]
    rim_gradients(near_ref, far_ref, total_ref[:, rows:])


def settle_body(own_ref, near_ref, far_ref, hi_ref, lo_ref, out_ref):
    out_ref[...] = settled(own_ref[...], near_ref[...], far_ref[...], hi_ref, lo_ref).astype(BF16)


def core_sum_body(layers, keep_ref, got_ref, own_ref, *send_refs):
    rows = own_ref.shape[0] // layers
    slots = len(send_refs) + 1
    for layer in range(layers):
        there = slice(layer * rows, (layer + 1) * rows)
        for slot, out_ref in enumerate((own_ref, *send_refs)):
            part = slice((layer * slots + slot) * rows, (layer * slots + slot + 1) * rows)
            out_ref[there] = (keep_ref[part] + got_ref[part].astype(F32)).astype(out_ref.dtype)


def chip_sum_body(own_ref, *refs):
    total = own_ref[...]
    for got_ref in refs[:-1]:
        total = total + got_ref[...].astype(F32)
    refs[-1][...] = total.astype(BF16)


def scan_sum_body(own_ref, got_ref, total_ref):
    total_ref[...] = (own_ref[...].astype(F32) + got_ref[...].astype(F32)).astype(BF16)


def unpack_body(scale, layers, *refs):
    *refs, all_ref, sems = refs
    piece_refs, outs, locals_ = refs[: -2 * layers], refs[-2 * layers : -layers], refs[-layers:]
    me = lax.axis_index("space")
    rows = piece_refs[0].shape[0] // layers
    count, chans = locals_[0].shape[0], locals_[0].shape[1]
    lane = lax.broadcasted_iota(I32, (chans, LANES), 1)
    copies = []
    for layer in range(layers):
        for slot, piece_ref in enumerate(piece_refs):
            piece = jnp.bitwise_xor(me, slot)
            block = piece_ref[layer * rows : (layer + 1) * rows].astype(F32)
            all_ref[pl.ds(pl.multiple_of(piece * rows, rows), rows), :] = block
        for first in range(0, count, CHUNK):
            chunk = pl.ds(first, min(CHUNK, count - first))
            for k in range(first, first + chunk.size):
                tile, shift = divmod(k * chans, LANES)
                block = all_ref[tile * chans : (tile + 1) * chans, :]
                if shift:
                    block = pltpu.roll(block, LANES - shift, 1)
                if shift + chans > LANES:
                    after = pltpu.roll(all_ref[(tile + 1) * chans : (tile + 2) * chans, :], LANES - shift, 1)
                    block = jnp.where(lane < LANES - shift, block, after)
                locals_[layer][k] = block[:, :chans] * scale
            copies.append(pltpu.make_async_copy(locals_[layer].at[chunk], outs[layer].at[chunk], sems.at[len(copies)]))
            copies[-1].start()
    for copy in copies:
        copy.wait()


def swap(block, axis, bit):
    return lax.ppermute(block, axis, [(i, i ^ bit) for i in range(lax.axis_size(axis))])


def swap_neighbours(near, far):
    inner = range(1, lax.axis_size("space") - 1)
    far = lax.ppermute(far, "space", [(i, i + 1 if i % 2 else i - 1) for i in inner])
    return swap(near, "space", 1), far


def swap_scans(block, step, steps):
    scans = lax.axis_size("scan")
    bits = (1 << step, 1 << (steps - 1 - step))
    bricks = range(lax.axis_size("space"))
    pairs = [(b * scans + z, b * scans + (z ^ bits[b % 2])) for b in bricks for z in range(scans)]
    return lax.ppermute(block, ("space", "scan"), pairs)


def summed(keep, got, layers, weight_shape, scale, beside):
    slots = lax.axis_size("space") // 2
    scans = lax.axis_size("scan")
    packed = 2 * keep.shape[0] // layers
    rows = keep.shape[0] // slots
    outs = [shape((rows, LANES), F32)] + [shape((rows, LANES), BF16)] * (slots - 1)
    own, *sends = call(functools.partial(core_sum_body, layers), outs, [keep, got])
    gots = [swap(block, "space", 2 * slot) for slot, block in enumerate(sends, 1)]
    waiting = list(beside)
    own, state = waiting.pop(0)(own, None)
    total = call(chip_sum_body, shape((rows, LANES), BF16), [own, *gots])
    if scans & (scans - 1):
        total = lax.psum(total, "scan")
    else:
        steps = scans.bit_length() - 1
        for step in range(steps):
            more = swap_scans(total, step, steps)
            if waiting:
                total, state = waiting.pop(0)(total, state)
            total = call(scan_sum_body, shape((rows, LANES), BF16), [total, more])
    for work in waiting:
        total, state = work(total, state)
    pieces = []
    for slot in range(slots):
        piece = swap(total, "space", 2 * slot) if slot else total
        pieces += [piece, swap(piece, "space", 1)]
    return state, call(
        functools.partial(unpack_body, scale, layers),
        [shape(weight_shape, F32)] * layers,
        pieces,
        scratch=[pltpu.VMEM(weight_shape, F32)] * layers + [pltpu.VMEM((packed, LANES), F32), pltpu.SemaphoreType.DMA((layers * -(-weight_shape[0] // CHUNK),))],
        outs_in=HBM,
    )


def shards(act_zero, pre_act, cot_out, weight_one, weight_two, in_map, out_map, send_lo, send_hi):
    zero, pre, cot = (x[0, 0].T for x in (act_zero, pre_act, cot_out))
    ins, outs = (x[0, 0][:, None, :] for x in (in_map, out_map))
    lo, hi = send_lo[0], send_hi[0]
    chans, rows = zero.shape
    count, _, pairs = ins.shape
    rim = 2 * lo.shape[1]
    ext = rows + rim
    scenes = lax.axis_size("scan")
    bricks = lax.axis_size("space")
    tiles = -(-count * chans // LANES)
    tall = tiles * LANES
    unit = 16 * bricks
    packed = -(-tiles * chans // unit) * unit
    gather_flops = 2 * count * chans * ext * rows
    back_flops = 2 * count * chans * chans * ext

    picked = call(
        pick_body,
        shape((count * (chans + 16), pairs), BF16),
        [outs, cot],
        flops=2 * count * chans * rows * pairs,
        moved=2 << 20,
    )
    t_two, own, near, far = call(
        two_body,
        [
            shape((tall, ext), BF16),
            shape((chans + -(-count // 8) * 8, ext), F32),
            shape((2 * chans, rim), BF16),
            shape((2 * chans, rim), BF16),
        ],
        [ins, picked, weight_two, hi, lo, zero, pre],
        scratch=[pltpu.VMEM((chans, ext), F32)],
        flops=gather_flops + back_flops,
        moved=8 << 20,
    )
    near, far = swap_neighbours(near, far)
    sum_two = call(two_weights_body, shape((packed, LANES), F32), [pre, t_two], flops=back_flops, moved=6 << 20)
    t_one, keep, send = call(
        functools.partial(one_body, count),
        [shape((tall, ext), BF16), shape((packed, LANES), F32), shape((packed, LANES), BF16)],
        [own, near, far, hi, lo, pre, zero, t_two, sum_two],
        scratch=[pltpu.VMEM((chans, rows), BF16), pltpu.VMEM((packed, LANES), F32)],
        flops=gather_flops + back_flops,
        moved=8 << 20,
    )
    got = swap(send, "space", 1)
    own, near, far = call(
        back_body,
        [shape((chans, rows), F32), shape((chans, rim), BF16), shape((chans, rim), BF16)],
        [weight_one, t_one],
        scratch=[pltpu.VMEM((chans, ext), F32)],
        flops=back_flops,
        moved=6 << 20,
    )
    keep, near, far = lax.optimization_barrier((keep, near, far))

    def swap_edges(held, _):
        held, *edges = lax.optimization_barrier((held, near, far))
        held, *edges = lax.optimization_barrier((held, *swap_neighbours(*edges)))
        return held, edges

    def settle(held, edges):
        held, own_rows, *edges = lax.optimization_barrier((held, own, *edges))
        grad_act = call(settle_body, shape((chans, rows), BF16), [own_rows, *edges, hi, lo])
        return lax.optimization_barrier((held, grad_act))

    grad_act, (grad_one, grad_two) = summed(keep, got, 2, weight_one.shape, 1.0 / scenes, (swap_edges, settle))
    return grad_act.T[None, None], grad_one, grad_two


def solution(mesh):
    return jax.shard_map(
        shards,
        mesh=mesh,
        in_specs=(
            P("scan", "space", None, None),
            P("scan", "space", None, None),
            P("scan", "space", None, None),
            P(),
            P(),
            P("scan", "space", None, None),
            P("scan", "space", None, None),
            P("scan", "space", None),
            P("scan", "space", None),
        ),
        out_specs=(P("scan", "space", None, None), P(), P()),
        check_vma=False,
    )
```

```python
import functools

import jax
import jax.numpy as jnp
from jax import lax
from jax.experimental import pallas as pl
from jax.experimental.pallas import tpu as pltpu
from jax.sharding import PartitionSpec as P

F32, BF16, I32 = jnp.float32, jnp.bfloat16, jnp.int32
VMEM = pl.BlockSpec(memory_space=pltpu.VMEM)
HBM = pl.BlockSpec(memory_space=pltpu.HBM)
LANES = 128
BLOCK = 256
CHUNK = 9
WHOLE = 62 << 20
UNROLL = 9
NT = (((1,), (1,)), ((), ()))


def call(body, outs, args, scratch=(), flops=0, moved=0, args_in=VMEM, outs_in=VMEM, room=40 << 20):
    single = not isinstance(outs, (list, tuple))
    return pl.pallas_call(
        body,
        out_shape=outs if single else tuple(outs),
        in_specs=[args_in] * len(args),
        out_specs=outs_in if single or isinstance(outs_in, tuple) else (outs_in,) * len(outs),
        scratch_shapes=scratch,
        compiler_params=pltpu.CompilerParams(vmem_limit_bytes=room),
        cost_estimate=pl.CostEstimate(flops=flops, bytes_accessed=moved, transcendentals=0),
    )(*args)


def shape(dims, dtype):
    return jax.ShapeDtypeStruct(dims, dtype)


def loop(steps, body):
    unroll = next(u for u in range(UNROLL, 0, -1) if steps % u == 0)

    def step(i, carry):
        body(i)
        return carry

    lax.fori_loop(0, steps, step, 0, unroll=unroll)


def one_hot(rows, index):
    count = lax.broadcasted_iota(I32, (min(rows, BLOCK), index.shape[1]), 0).astype(F32).astype(BF16)
    blocks = []
    for start in range(0, rows, BLOCK):
        wanted = (index - start).astype(F32).astype(BF16)
        hit = count[: min(BLOCK, rows - start)] == wanted
        blocks.append(jnp.where(hit, jnp.ones((), BF16), jnp.zeros((), BF16)))
    return jnp.concatenate(blocks, 0)


def dot(a, b):
    return jnp.dot(a, b, preferred_element_type=F32)


def dot_nt(a, b):
    return lax.dot_general(a, b, NT, preferred_element_type=F32)


def offset_rows(k, chans):
    return pl.ds(pl.multiple_of(k * chans, chans), chans)


def rim_index(hi_ref, lo_ref):
    return jnp.concatenate([hi_ref[...], lo_ref[...]], 1)


def halves(x, y):
    x, y = x.astype(F32), y.astype(F32)
    width = x.shape[1]
    left = lax.broadcasted_iota(I32, x.shape, 1) < width // 2
    return jnp.where(left, x, pltpu.roll(y, width // 2, 1)), jnp.where(left, pltpu.roll(x, width // 2, 1), y)


def by_parity(x, y):
    even = lax.rem(lax.axis_index("space"), 2) == 0
    return jnp.where(even, x, y), jnp.where(even, y, x)


def put_edges(near_ref, far_ref, at, up, down):
    rows = slice(at, at + up.shape[0])
    for ref, value in zip((near_ref, far_ref), by_parity(up, down), strict=True):
        ref[rows] = value.astype(BF16)


def rim_gradients(near_ref, far_ref, total):
    high = total.astype(BF16).astype(F32)
    down, up = halves(high, total - high)
    put_edges(near_ref, far_ref, 0, up, down)


def add_back(weight_ref, t_ref, total_ref):
    count, chans = weight_ref.shape[0], weight_ref.shape[1]
    total_ref[...] = jnp.zeros_like(total_ref)

    def body(g):
        part = None
        for j in range(3):
            k = g * 3 + j
            term = dot(weight_ref[k], t_ref[offset_rows(k, chans), :])
            part = term if part is None else part + term
        total_ref[...] += part

    assert count % 3 == 0
    loop(count // 3, body)


def place_rows(ins_ref, c_ref, first, t_ref, inv_ref, inv_at):
    count = ins_ref.shape[0]
    ext = t_ref.shape[1]
    tall = c_ref.shape[0] // count
    chans = tall - 16
    t_ref[count * chans :, :] = jnp.zeros((t_ref.shape[0] - count * chans, ext), BF16)

    def place(k):
        picked = c_ref[pl.ds(pl.multiple_of(k * tall, 16), tall), :]
        placed = dot_nt(picked, one_hot(ext, ins_ref[k] - first))
        t_ref[offset_rows(k, chans), :] = placed[:chans].astype(BF16)
        code = placed[chans : chans + 1] * 16.0 + placed[chans + 1 : chans + 2]
        inv_ref[pl.ds(inv_at + k, 1), :] = code

    loop(count, place)


def rim_body(*refs):
    operands, (c_ref, t_ref, inv_ref, near_ref, far_ref), scratch = refs[:8], refs[8:13], refs[13:]
    locals_, (total_ref, sems) = scratch[:8], scratch[8:]
    copies = [
        pltpu.make_async_copy(operand, local, sems.at[i]) for i, (operand, local) in enumerate(zip(operands, locals_, strict=True))
    ]
    for copy in copies:
        copy.start()
    outs_ref, cot_ref, ins_ref, weight_ref, hi_ref, lo_ref, zero_ref, pre_ref = locals_
    count, pairs = ins_ref.shape[0], ins_ref.shape[2]
    chans, rows = cot_ref.shape
    tall = chans + 16
    row = lax.broadcasted_iota(I32, (16, pairs), 0)

    def pick(k):
        index = outs_ref[k]
        base = pl.multiple_of(k * tall, 16)
        c_ref[pl.ds(base, chans), :] = dot(cot_ref[...], one_hot(rows, index)).astype(BF16)
        left = rows - index
        code = jnp.where(row == 0, left // 16, jnp.where(row == 1, left % 16, 0))
        c_ref[pl.ds(base + chans, 16), :] = code.astype(F32).astype(BF16)

    copies[0].wait()
    copies[1].wait()
    loop(count, pick)
    copies[2].wait()
    place_rows(ins_ref, c_ref, rows, t_ref, inv_ref, 0)
    copies[3].wait()
    add_back(weight_ref, t_ref, total_ref)
    rim_gradients(near_ref, far_ref, total_ref[...])
    for copy in copies[4:]:
        copy.wait()
    wanted = one_hot(rows, rim_index(hi_ref, lo_ref))
    one = jnp.maximum(pre_ref[...], jnp.zeros_like(pre_ref))
    up, down = halves(dot(zero_ref[...], wanted), dot(one, wanted))
    put_edges(near_ref, far_ref, chans, up, down)


def own_body(ins_ref, c_ref, weight_ref, t_ref, own_ref, total_ref):
    chans = total_ref.shape[0]
    place_rows(ins_ref, c_ref, 0, t_ref, own_ref, chans)
    add_back(weight_ref, t_ref, total_ref)
    own_ref[:chans] = total_ref[...]


def packed_products(feats, t_ref, sum_ref, base_ref=None):
    chans = feats.shape[0]
    tiles = t_ref.shape[0] // LANES
    for start in range(0, tiles, 2):
        width = min(2, tiles - start)
        grad = dot_nt(feats, t_ref[start * LANES : (start + width) * LANES, :])
        for j in range(width):
            rows = slice((start + j) * chans, (start + j + 1) * chans)
            block = grad[:, j * LANES : (j + 1) * LANES]
            sum_ref[rows, :] = block if base_ref is None else block + base_ref[rows, :]
    sum_ref[tiles * chans :, :] = jnp.zeros((sum_ref.shape[0] - tiles * chans, LANES), F32)


def cut(sum_ref, layer, keep_ref, send_ref):
    me = lax.axis_index("space")
    slots = lax.axis_size("space") // 2
    rows = sum_ref.shape[0] // (2 * slots)
    for slot in range(slots):
        there = pl.ds((layer * slots + slot) * rows, rows)
        for out_ref, bit in ((keep_ref, 0), (send_ref, 1)):
            piece = jnp.bitwise_xor(me, 2 * slot + bit)
            block = sum_ref[pl.ds(pl.multiple_of(piece * rows, rows), rows), :]
            out_ref[there, :] = block.astype(out_ref.dtype)


def two_weights_body(pre_ref, t_ref, sum_ref):
    one = jnp.maximum(pre_ref[...], jnp.zeros_like(pre_ref))
    packed_products(one, t_ref, sum_ref)


def settled(own, near, far, hi_ref, lo_ref):
    above, below = by_parity(near, far)
    place = one_hot(own.shape[1], rim_index(hi_ref, lo_ref))
    for part in halves(above, below):
        own = own + dot_nt(part.astype(BF16), place)
    return own


def one_body(
    count, own_ref, inv_ref, near_ref, far_ref, hi_ref, lo_ref, pre_ref, zero_ref, t_two_ref, sum_two_ref, t_ref, keep_ref, send_ref, cot_ref, sum_ref
):
    chans, rows = pre_ref.shape
    back = settled(own_ref[:chans], near_ref[:chans], far_ref[:chans], hi_ref, lo_ref)
    cot_ref[...] = jnp.where(pre_ref[...].astype(F32) > 0, back, 0.0).astype(BF16)

    def place(k):
        there = offset_rows(k, chans)
        for index, columns in ((own_ref[pl.ds(chans + k, 1), :], slice(0, rows)), (inv_ref[pl.ds(k, 1), :], slice(rows, None))):
            t_ref[there, columns] = dot(cot_ref[...], one_hot(rows, rows - index)).astype(BF16)

    loop(count, place)
    t_ref[count * chans :, :] = jnp.zeros((t_ref.shape[0] - count * chans, t_ref.shape[1]), BF16)
    above, below = by_parity(near_ref[chans:], far_ref[chans:])
    zero_rim, one_rim = halves(below, above)
    feats = jnp.concatenate([zero_ref[...], zero_rim.astype(BF16)], 1)
    packed_products(feats, t_ref, sum_ref)
    cut(sum_ref, 0, keep_ref, send_ref)
    packed_products(one_rim.astype(BF16), t_two_ref, sum_ref, sum_two_ref)
    cut(sum_ref, 1, keep_ref, send_ref)


def back_body(weight_ref, t_ref, own_ref, near_ref, far_ref, total_ref):
    rows = own_ref.shape[1]
    add_back(weight_ref, t_ref, total_ref)
    own_ref[...] = total_ref[:, :rows]
    rim_gradients(near_ref, far_ref, total_ref[:, rows:])


def settle_body(own_ref, near_ref, far_ref, hi_ref, lo_ref, out_ref):
    out_ref[...] = settled(own_ref[...], near_ref[...], far_ref[...], hi_ref, lo_ref).astype(BF16)


def core_sum_body(layers, keep_ref, got_ref, own_ref, *send_refs):
    rows = own_ref.shape[0] // layers
    slots = len(send_refs) + 1
    for layer in range(layers):
        there = slice(layer * rows, (layer + 1) * rows)
        for slot, out_ref in enumerate((own_ref, *send_refs)):
            part = slice((layer * slots + slot) * rows, (layer * slots + slot + 1) * rows)
            out_ref[there] = (keep_ref[part] + got_ref[part].astype(F32)).astype(out_ref.dtype)


def chip_sum_body(own_ref, *refs):
    layers = 2
    total = own_ref[...]
    for got_ref in refs[:-layers]:
        total = total + got_ref[...].astype(F32)
    rows = total.shape[0] // layers
    for layer, out_ref in enumerate(refs[-layers:]):
        out_ref[...] = total[layer * rows : (layer + 1) * rows].astype(BF16)


def scan_sum_body(*refs):
    *terms, total_ref = refs
    rows = terms[0].shape[0]
    for i in range(0, len(terms), 2):
        total_ref[i // 2 * rows : (i // 2 + 1) * rows] = (terms[i][...].astype(F32) + terms[i + 1][...].astype(F32)).astype(BF16)


def unpack_body(scale, layers, *refs):
    *refs, all_ref, sems = refs
    piece_refs, outs, locals_ = refs[: -2 * layers], refs[-2 * layers : -layers], refs[-layers:]
    me = lax.axis_index("space")
    rows = piece_refs[0].shape[0] // layers
    count, chans = locals_[0].shape[0], locals_[0].shape[1]
    lane = lax.broadcasted_iota(I32, (chans, LANES), 1)
    copies = []
    for layer in range(layers):
        for slot, piece_ref in enumerate(piece_refs):
            piece = jnp.bitwise_xor(me, slot)
            block = piece_ref[layer * rows : (layer + 1) * rows].astype(F32)
            all_ref[pl.ds(pl.multiple_of(piece * rows, rows), rows), :] = block
        for first in range(0, count, CHUNK):
            chunk = pl.ds(first, min(CHUNK, count - first))
            for k in range(first, first + chunk.size):
                tile, shift = divmod(k * chans, LANES)
                block = all_ref[tile * chans : (tile + 1) * chans, :]
                if shift:
                    block = pltpu.roll(block, LANES - shift, 1)
                if shift + chans > LANES:
                    after = pltpu.roll(all_ref[(tile + 1) * chans : (tile + 2) * chans, :], LANES - shift, 1)
                    block = jnp.where(lane < LANES - shift, block, after)
                locals_[layer][k] = block[:, :chans] * scale
            copies.append(pltpu.make_async_copy(locals_[layer].at[chunk], outs[layer].at[chunk], sems.at[len(copies)]))
            copies[-1].start()
    for copy in copies:
        copy.wait()


def swap(block, axis, bit):
    return lax.ppermute(block, axis, [(i, i ^ bit) for i in range(lax.axis_size(axis))])


def swap_neighbours(near, far):
    inner = range(1, lax.axis_size("space") - 1)
    far = lax.ppermute(far, "space", [(i, i + 1 if i % 2 else i - 1) for i in inner])
    return swap(near, "space", 1), far


def swap_scans(block, step, steps):
    scans = lax.axis_size("scan")
    bits = (1 << step, 1 << (steps - 1 - step))
    bricks = range(lax.axis_size("space"))
    pairs = [(b * scans + z, b * scans + (z ^ bits[b % 2])) for b in bricks for z in range(scans)]
    return lax.ppermute(block, ("space", "scan"), pairs)


def summed(keep, got, layers, weight_shape, scale, beside):
    slots = lax.axis_size("space") // 2
    scans = lax.axis_size("scan")
    packed = 2 * keep.shape[0] // layers
    rows = keep.shape[0] // slots
    outs = [shape((rows, LANES), F32)] + [shape((rows, LANES), BF16)] * (slots - 1)
    own, *sends = call(functools.partial(core_sum_body, layers), outs, [keep, got])
    gots = [swap(block, "space", 2 * slot) for slot, block in enumerate(sends, 1)]
    waiting = list(beside)
    own, state = waiting.pop(0)(own, None)
    part = rows // layers
    totals = call(chip_sum_body, [shape((part, LANES), BF16)] * layers, [own, *gots])
    if scans & (scans - 1):
        total = lax.psum(jnp.concatenate(totals), "scan")
    else:
        steps = scans.bit_length() - 1
        for step in range(steps):
            more = [swap_scans(total, step, steps) for total in totals]
            if waiting:
                totals, state = waiting.pop(0)(totals, state)
            if step + 1 < steps:
                totals = [call(scan_sum_body, shape((part, LANES), BF16), [x, y]) for x, y in zip(totals, more, strict=True)]
            else:
                total = call(scan_sum_body, shape((rows, LANES), BF16), [x for pair in zip(totals, more, strict=True) for x in pair])
    for work in waiting:
        total, state = work(total, state)
    pieces = []
    for slot in range(slots):
        piece = swap(total, "space", 2 * slot) if slot else total
        pieces += [piece, swap(piece, "space", 1)]
    return state, call(
        functools.partial(unpack_body, scale, layers),
        [shape(weight_shape, F32)] * layers,
        pieces,
        scratch=[pltpu.VMEM(weight_shape, F32)] * layers + [pltpu.VMEM((packed, LANES), F32), pltpu.SemaphoreType.DMA((layers * -(-weight_shape[0] // CHUNK),))],
        outs_in=HBM,
    )


def shards(act_zero, pre_act, cot_out, weight_one, weight_two, in_map, out_map, send_lo, send_hi):
    zero, pre, cot = (x[0, 0].T for x in (act_zero, pre_act, cot_out))
    ins, outs = (x[0, 0][:, None, :] for x in (in_map, out_map))
    lo, hi = send_lo[0], send_hi[0]
    chans, rows = zero.shape
    count, _, pairs = ins.shape
    rim = 2 * lo.shape[1]
    ext = rows + rim
    scenes = lax.axis_size("scan")
    bricks = lax.axis_size("space")
    tiles = -(-count * chans // LANES)
    tall = tiles * LANES
    unit = 16 * bricks
    packed = -(-tiles * chans // unit) * unit
    gather_flops = 2 * count * chans * ext * rows
    back_flops = 2 * count * chans * chans * ext

    operands = [pltpu.with_memory_space_constraint(x, pltpu.HBM) for x in (outs, cot, ins, weight_two, hi, lo, zero, pre)]
    rounded = -(-count // 8) * 8
    c_two, t_rim, inv_rim, near, far = call(
        rim_body,
        [
            shape((count * (chans + 16), pairs), BF16),
            shape((tall, rim), BF16),
            shape((rounded, rim), F32),
            shape((2 * chans, rim), BF16),
            shape((2 * chans, rim), BF16),
        ],
        operands,
        scratch=[pltpu.VMEM(x.shape, x.dtype) for x in operands]
        + [pltpu.VMEM((chans, rim), F32), pltpu.SemaphoreType.DMA((len(operands),))],
        flops=2 * count * chans * rows * pairs,
        moved=4 << 20,
        args_in=HBM,
    )
    near, far = swap_neighbours(near, far)
    t_own, own = call(
        own_body,
        [shape((tall, rows), BF16), shape((chans + rounded, rows), F32)],
        [ins, c_two, weight_two],
        scratch=[pltpu.VMEM((chans, rows), F32)],
        flops=gather_flops // 2,
        moved=8 << 20,
    )
    sum_two = call(two_weights_body, shape((packed, LANES), F32), [pre, t_own], flops=back_flops, moved=6 << 20)
    t_one, keep, send = call(
        functools.partial(one_body, count),
        [shape((tall, ext), BF16), shape((packed, LANES), F32), shape((packed, LANES), BF16)],
        [own, inv_rim, near, far, hi, lo, pre, zero, t_rim, sum_two],
        scratch=[pltpu.VMEM((chans, rows), BF16), pltpu.VMEM((packed, LANES), F32)],
        flops=gather_flops + back_flops,
        moved=8 << 20,
    )
    got = swap(send, "space", 1)
    own, near, far = call(
        back_body,
        [shape((chans, rows), F32), shape((chans, rim), BF16), shape((chans, rim), BF16)],
        [weight_one, t_one],
        scratch=[pltpu.VMEM((chans, ext), F32)],
        flops=back_flops,
        moved=6 << 20,
    )
    keep, near, far = lax.optimization_barrier((keep, near, far))

    def swap_edges(held, _):
        held, *edges = lax.optimization_barrier((held, near, far))
        held, *edges = lax.optimization_barrier((held, *swap_neighbours(*edges)))
        return held, edges

    def settle(held, edges):
        held, own_rows, *edges = lax.optimization_barrier((held, own, *edges))
        grad_act = call(settle_body, shape((chans, rows), BF16), [own_rows, *edges, hi, lo])
        return lax.optimization_barrier((held, grad_act))

    grad_act, (grad_one, grad_two) = summed(keep, got, 2, weight_one.shape, 1.0 / scenes, (swap_edges, settle))
    return grad_act.T[None, None], grad_one, grad_two


def solution(mesh):
    return jax.shard_map(
        shards,
        mesh=mesh,
        in_specs=(
            P("scan", "space", None, None),
            P("scan", "space", None, None),
            P("scan", "space", None, None),
            P(),
            P(),
            P("scan", "space", None, None),
            P("scan", "space", None, None),
            P("scan", "space", None),
            P("scan", "space", None),
        ),
        out_specs=(P("scan", "space", None, None), P(), P()),
        check_vma=False,
    )
```

```python
import functools

import jax
import jax.numpy as jnp
from jax import lax
from jax.experimental import pallas as pl
from jax.experimental.pallas import tpu as pltpu
from jax.sharding import PartitionSpec as P

F32, BF16, I32 = jnp.float32, jnp.bfloat16, jnp.int32
VMEM = pl.BlockSpec(memory_space=pltpu.VMEM)
HBM = pl.BlockSpec(memory_space=pltpu.HBM)
LANES = 128
BLOCK = 256
CHUNK = 9
WHOLE = 62 << 20
UNROLL = 27
NT = (((1,), (1,)), ((), ()))


def call(body, outs, args, scratch=(), flops=0, moved=0, args_in=VMEM, outs_in=VMEM, room=40 << 20):
    single = not isinstance(outs, (list, tuple))
    return pl.pallas_call(
        body,
        out_shape=outs if single else tuple(outs),
        in_specs=[args_in] * len(args),
        out_specs=outs_in if single or isinstance(outs_in, tuple) else (outs_in,) * len(outs),
        scratch_shapes=scratch,
        compiler_params=pltpu.CompilerParams(vmem_limit_bytes=room),
        cost_estimate=pl.CostEstimate(flops=flops, bytes_accessed=moved, transcendentals=0),
    )(*args)


def shape(dims, dtype):
    return jax.ShapeDtypeStruct(dims, dtype)


def loop(steps, body):
    unroll = next(u for u in range(UNROLL, 0, -1) if steps % u == 0)

    def step(i, carry):
        body(i)
        return carry

    lax.fori_loop(0, steps, step, 0, unroll=unroll)


def one_hot(rows, index):
    count = lax.broadcasted_iota(I32, (min(rows, BLOCK), index.shape[1]), 0).astype(F32).astype(BF16)
    blocks = []
    for start in range(0, rows, BLOCK):
        wanted = (index - start).astype(F32).astype(BF16)
        hit = count[: min(BLOCK, rows - start)] == wanted
        blocks.append(jnp.where(hit, jnp.ones((), BF16), jnp.zeros((), BF16)))
    return jnp.concatenate(blocks, 0)


def one_hot_columns(index, width):
    count = lax.broadcasted_iota(I32, (index.shape[0], min(width, BLOCK)), 1).astype(F32).astype(BF16)
    blocks = []
    for start in range(0, width, BLOCK):
        size = min(BLOCK, width - start)
        hit = count[:, :size] == jnp.broadcast_to((index - start).astype(BF16), (index.shape[0], size))
        blocks.append(jnp.where(hit, jnp.ones((), BF16), jnp.zeros((), BF16)))
    return jnp.concatenate(blocks, 1)


def take_columns(source_ref, index):
    dims = (source_ref.shape[0], LANES)
    lane, tile = jnp.broadcast_to(index % LANES, dims), jnp.broadcast_to(index // LANES, dims)
    taken = jnp.zeros(dims, F32)
    for t in range(source_ref.shape[1] // LANES):
        block = source_ref[:, t * LANES : (t + 1) * LANES]
        taken = jnp.where(tile == t, jnp.take_along_axis(block, lane, axis=1, mode="promise_in_bounds"), taken)
    return taken


def dot(a, b):
    return jnp.dot(a, b, preferred_element_type=F32)


def dot_nt(a, b):
    return lax.dot_general(a, b, NT, preferred_element_type=F32)


def offset_rows(k, chans):
    return pl.ds(pl.multiple_of(k * chans, chans), chans)


def rim_index(hi_ref, lo_ref):
    return jnp.concatenate([hi_ref[...], lo_ref[...]], 1)


def halves(x, y):
    x, y = x.astype(F32), y.astype(F32)
    width = x.shape[1]
    left = lax.broadcasted_iota(I32, x.shape, 1) < width // 2
    return jnp.where(left, x, pltpu.roll(y, width // 2, 1)), jnp.where(left, pltpu.roll(x, width // 2, 1), y)


def by_parity(x, y):
    even = lax.rem(lax.axis_index("space"), 2) == 0
    return jnp.where(even, x, y), jnp.where(even, y, x)


def put_edges(near_ref, far_ref, at, up, down):
    rows = slice(at, at + up.shape[0])
    for ref, value in zip((near_ref, far_ref), by_parity(up, down), strict=True):
        ref[rows] = value.astype(BF16)


def rim_gradients(near_ref, far_ref, total):
    high = total.astype(BF16).astype(F32)
    down, up = halves(high, total - high)
    put_edges(near_ref, far_ref, 0, up, down)


def add_back(weight_ref, t_ref, total_ref):
    count, chans = weight_ref.shape[0], weight_ref.shape[1]
    total_ref[...] = jnp.zeros_like(total_ref)

    def body(g):
        part = None
        for j in range(3):
            k = g * 3 + j
            term = dot(weight_ref[k], t_ref[offset_rows(k, chans), :])
            part = term if part is None else part + term
        total_ref[...] += part

    assert count % 3 == 0
    loop(count // 3, body)


def place_rows(ins_ref, c_ref, first, t_ref, inv_ref, inv_at):
    count = ins_ref.shape[0]
    ext = t_ref.shape[1]
    tall = c_ref.shape[0] // count
    chans = tall - 16
    t_ref[count * chans :, :] = jnp.zeros((t_ref.shape[0] - count * chans, ext), BF16)

    def place(k):
        picked = c_ref[pl.ds(pl.multiple_of(k * tall, 16), tall), :]
        placed = dot_nt(picked, one_hot(ext, ins_ref[k] - first))
        t_ref[offset_rows(k, chans), :] = placed[:chans].astype(BF16)
        code = placed[chans : chans + 1] * 16.0 + placed[chans + 1 : chans + 2]
        inv_ref[pl.ds(inv_at + k, 1), :] = code

    loop(count, place)


def rim_body(*refs):
    operands, (c_ref, t_ref, inv_ref, near_ref, far_ref), scratch = refs[:8], refs[8:13], refs[13:]
    locals_, (source_ref, total_ref, sems) = scratch[:8], scratch[8:]
    copies = [
        pltpu.make_async_copy(operand, local, sems.at[i]) for i, (operand, local) in enumerate(zip(operands, locals_, strict=True))
    ]
    for copy in copies:
        copy.start()
    outs_ref, cot_ref, ins_ref, weight_ref, hi_ref, lo_ref, zero_ref, pre_ref = locals_
    count, pairs = ins_ref.shape[0], ins_ref.shape[2]
    chans, rows = cot_ref.shape
    tall = chans + 16
    row = lax.broadcasted_iota(I32, (16, pairs), 0)

    def pick(k):
        index = outs_ref[k]
        base = pl.multiple_of(k * tall, 16)
        half = pairs - LANES
        c_ref[pl.ds(base, chans), :half] = dot(cot_ref[...], one_hot(rows, index[:, :half])).astype(BF16)
        c_ref[pl.ds(base, chans), half:] = take_columns(source_ref, index[:, half:]).astype(BF16)
        left = rows - index
        code = jnp.where(row == 0, left // 16, jnp.where(row == 1, left % 16, 0))
        c_ref[pl.ds(base + chans, 16), :] = code.astype(F32).astype(BF16)

    copies[0].wait()
    copies[1].wait()
    source_ref[...] = cot_ref[...].astype(F32)
    loop(count, pick)
    copies[2].wait()
    place_rows(ins_ref, c_ref, rows, t_ref, inv_ref, 0)
    copies[3].wait()
    add_back(weight_ref, t_ref, total_ref)
    rim_gradients(near_ref, far_ref, total_ref[...])
    for copy in copies[4:]:
        copy.wait()
    wanted = one_hot(rows, rim_index(hi_ref, lo_ref))
    one = jnp.maximum(pre_ref[...], jnp.zeros_like(pre_ref))
    up, down = halves(dot(zero_ref[...], wanted), dot(one, wanted))
    put_edges(near_ref, far_ref, chans, up, down)


def own_body(ins_ref, c_ref, weight_ref, t_ref, own_ref, total_ref, columns_ref):
    count, pairs = ins_ref.shape[0], ins_ref.shape[2]
    chans, rows = total_ref.shape
    tall = chans + 16
    step = columns_ref.shape[0]
    lot = count // step
    t_ref[count * chans :, :] = jnp.zeros((t_ref.shape[0] - count * chans, rows), BF16)
    for g in range(step):
        lines = [ins_ref[g * lot + j] for j in range(lot)] + [jnp.zeros((-lot % 8, pairs), I32)]
        columns_ref[g, :, : lot + -lot % 8] = jnp.concatenate(lines, 0).astype(F32).T

    def place(g, carry):
        index = columns_ref[g]
        for j in range(lot):
            k = g * lot + j
            picked = c_ref[pl.ds(pl.multiple_of(k * tall, 16), tall), :]
            placed = dot(picked, one_hot_columns(index[:, j : j + 1], rows))
            t_ref[offset_rows(k, chans), :] = placed[:chans].astype(BF16)
            own_ref[pl.ds(chans + k, 1), :] = placed[chans : chans + 1] * 16.0 + placed[chans + 1 : chans + 2]
        return carry

    lax.fori_loop(0, step, place, 0)
    add_back(weight_ref, t_ref, total_ref)
    own_ref[:chans] = total_ref[...]


def packed_products(feats, t_ref, sum_ref, base_ref=None):
    chans = feats.shape[0]
    tiles = t_ref.shape[0] // LANES
    for start in range(0, tiles, 2):
        width = min(2, tiles - start)
        grad = dot_nt(feats, t_ref[start * LANES : (start + width) * LANES, :])
        for j in range(width):
            rows = slice((start + j) * chans, (start + j + 1) * chans)
            block = grad[:, j * LANES : (j + 1) * LANES]
            sum_ref[rows, :] = block if base_ref is None else block + base_ref[rows, :]
    sum_ref[tiles * chans :, :] = jnp.zeros((sum_ref.shape[0] - tiles * chans, LANES), F32)


def cut(sum_ref, layer, keep_ref, send_ref):
    me = lax.axis_index("space")
    slots = lax.axis_size("space") // 2
    rows = sum_ref.shape[0] // (2 * slots)
    for slot in range(slots):
        there = pl.ds((layer * slots + slot) * rows, rows)
        for out_ref, bit in ((keep_ref, 0), (send_ref, 1)):
            piece = jnp.bitwise_xor(me, 2 * slot + bit)
            block = sum_ref[pl.ds(pl.multiple_of(piece * rows, rows), rows), :]
            out_ref[there, :] = block.astype(out_ref.dtype)


def two_weights_body(pre_ref, t_ref, sum_ref):
    one = jnp.maximum(pre_ref[...], jnp.zeros_like(pre_ref))
    packed_products(one, t_ref, sum_ref)


def settled(own, near, far, hi_ref, lo_ref):
    above, below = by_parity(near, far)
    place = one_hot(own.shape[1], rim_index(hi_ref, lo_ref))
    for part in halves(above, below):
        own = own + dot_nt(part.astype(BF16), place)
    return own


def one_body(
    count, own_ref, inv_ref, near_ref, far_ref, hi_ref, lo_ref, pre_ref, zero_ref, t_two_ref, sum_two_ref, t_ref, keep_ref, send_ref, cot_ref, source_ref, sum_ref
):
    chans, rows = pre_ref.shape
    back = settled(own_ref[:chans], near_ref[:chans], far_ref[:chans], hi_ref, lo_ref)
    cot_ref[...] = jnp.where(pre_ref[...].astype(F32) > 0, back, 0.0).astype(BF16)

    source_ref[...] = cot_ref[...].astype(F32)
    part = rows - LANES

    def place(k):
        there = offset_rows(k, chans)
        index = rows - own_ref[pl.ds(chans + k, 1), :]
        t_ref[there, :part] = dot(cot_ref[...], one_hot(rows, index[:, :part])).astype(BF16)
        t_ref[there, part:rows] = take_columns(source_ref, index[:, part:].astype(I32)).astype(BF16)
        index = rows - inv_ref[pl.ds(k, 1), :]
        t_ref[there, rows:] = take_columns(source_ref, index.astype(I32)).astype(BF16)

    loop(count, place)
    t_ref[count * chans :, :] = jnp.zeros((t_ref.shape[0] - count * chans, t_ref.shape[1]), BF16)
    above, below = by_parity(near_ref[chans:], far_ref[chans:])
    zero_rim, one_rim = halves(below, above)
    feats = jnp.concatenate([zero_ref[...], zero_rim.astype(BF16)], 1)
    packed_products(feats, t_ref, sum_ref)
    cut(sum_ref, 0, keep_ref, send_ref)
    packed_products(one_rim.astype(BF16), t_two_ref, sum_ref, sum_two_ref)
    cut(sum_ref, 1, keep_ref, send_ref)


def back_body(weight_ref, t_ref, own_ref, near_ref, far_ref, total_ref):
    rows = own_ref.shape[1]
    add_back(weight_ref, t_ref, total_ref)
    own_ref[...] = total_ref[:, :rows]
    rim_gradients(near_ref, far_ref, total_ref[:, rows:])


def settle_body(own_ref, near_ref, far_ref, hi_ref, lo_ref, out_ref):
    out_ref[...] = settled(own_ref[...], near_ref[...], far_ref[...], hi_ref, lo_ref).astype(BF16)


def core_sum_body(layers, keep_ref, got_ref, own_ref, *send_refs):
    rows = own_ref.shape[0] // layers
    slots = len(send_refs) + 1
    for layer in range(layers):
        there = slice(layer * rows, (layer + 1) * rows)
        for slot, out_ref in enumerate((own_ref, *send_refs)):
            part = slice((layer * slots + slot) * rows, (layer * slots + slot + 1) * rows)
            out_ref[there] = (keep_ref[part] + got_ref[part].astype(F32)).astype(out_ref.dtype)


def chip_sum_body(own_ref, *refs):
    layers = 2
    total = own_ref[...]
    for got_ref in refs[:-layers]:
        total = total + got_ref[...].astype(F32)
    rows = total.shape[0] // layers
    for layer, out_ref in enumerate(refs[-layers:]):
        out_ref[...] = total[layer * rows : (layer + 1) * rows].astype(BF16)


def scan_sum_body(*refs):
    *terms, total_ref = refs
    rows = terms[0].shape[0]
    for i in range(0, len(terms), 2):
        total_ref[i // 2 * rows : (i // 2 + 1) * rows] = (terms[i][...].astype(F32) + terms[i + 1][...].astype(F32)).astype(BF16)


def unpack_body(scale, layers, *refs):
    *refs, all_ref, sems = refs
    piece_refs, outs, locals_ = refs[: -2 * layers], refs[-2 * layers : -layers], refs[-layers:]
    me = lax.axis_index("space")
    rows = piece_refs[0].shape[0] // layers
    count, chans = locals_[0].shape[0], locals_[0].shape[1]
    lane = lax.broadcasted_iota(I32, (chans, LANES), 1)
    copies = []
    for layer in range(layers):
        for slot, piece_ref in enumerate(piece_refs):
            piece = jnp.bitwise_xor(me, slot)
            block = piece_ref[layer * rows : (layer + 1) * rows].astype(F32)
            all_ref[pl.ds(pl.multiple_of(piece * rows, rows), rows), :] = block
        for first in range(0, count, CHUNK):
            chunk = pl.ds(first, min(CHUNK, count - first))
            for k in range(first, first + chunk.size):
                tile, shift = divmod(k * chans, LANES)
                block = all_ref[tile * chans : (tile + 1) * chans, :]
                if shift:
                    block = pltpu.roll(block, LANES - shift, 1)
                if shift + chans > LANES:
                    after = pltpu.roll(all_ref[(tile + 1) * chans : (tile + 2) * chans, :], LANES - shift, 1)
                    block = jnp.where(lane < LANES - shift, block, after)
                locals_[layer][k] = block[:, :chans] * scale
            copies.append(pltpu.make_async_copy(locals_[layer].at[chunk], outs[layer].at[chunk], sems.at[len(copies)]))
            copies[-1].start()
    for copy in copies:
        copy.wait()


def swap(block, axis, bit):
    return lax.ppermute(block, axis, [(i, i ^ bit) for i in range(lax.axis_size(axis))])


def swap_neighbours(near, far):
    inner = range(1, lax.axis_size("space") - 1)
    far = lax.ppermute(far, "space", [(i, i + 1 if i % 2 else i - 1) for i in inner])
    return swap(near, "space", 1), far


def swap_scans(block, step, steps):
    scans = lax.axis_size("scan")
    bits = (1 << step, 1 << (steps - 1 - step))
    bricks = range(lax.axis_size("space"))
    pairs = [(b * scans + z, b * scans + (z ^ bits[b % 2])) for b in bricks for z in range(scans)]
    return lax.ppermute(block, ("space", "scan"), pairs)


def summed(keep, got, layers, weight_shape, scale, beside):
    slots = lax.axis_size("space") // 2
    scans = lax.axis_size("scan")
    packed = 2 * keep.shape[0] // layers
    rows = keep.shape[0] // slots
    outs = [shape((rows, LANES), F32)] + [shape((rows, LANES), BF16)] * (slots - 1)
    own, *sends = call(functools.partial(core_sum_body, layers), outs, [keep, got])
    gots = [swap(block, "space", 2 * slot) for slot, block in enumerate(sends, 1)]
    waiting = list(beside)
    own, state = waiting.pop(0)(own, None)
    part = rows // layers
    totals = call(chip_sum_body, [shape((part, LANES), BF16)] * layers, [own, *gots])
    if scans & (scans - 1):
        total = lax.psum(jnp.concatenate(totals), "scan")
    else:
        steps = scans.bit_length() - 1
        for step in range(steps):
            more = [swap_scans(total, step, steps) for total in totals]
            if waiting:
                totals, state = waiting.pop(0)(totals, state)
            if step + 1 < steps:
                totals = [call(scan_sum_body, shape((part, LANES), BF16), [x, y]) for x, y in zip(totals, more, strict=True)]
            else:
                total = call(scan_sum_body, shape((rows, LANES), BF16), [x for pair in zip(totals, more, strict=True) for x in pair])
    for work in waiting:
        total, state = work(total, state)
    pieces = []
    for slot in range(slots):
        piece = swap(total, "space", 2 * slot) if slot else total
        pieces += [piece, swap(piece, "space", 1)]
    return state, call(
        functools.partial(unpack_body, scale, layers),
        [shape(weight_shape, F32)] * layers,
        pieces,
        scratch=[pltpu.VMEM(weight_shape, F32)] * layers + [pltpu.VMEM((packed, LANES), F32), pltpu.SemaphoreType.DMA((layers * -(-weight_shape[0] // CHUNK),))],
        outs_in=HBM,
    )


def shards(act_zero, pre_act, cot_out, weight_one, weight_two, in_map, out_map, send_lo, send_hi):
    zero, pre, cot = (x[0, 0].T for x in (act_zero, pre_act, cot_out))
    ins, outs = (x[0, 0][:, None, :] for x in (in_map, out_map))
    lo, hi = send_lo[0], send_hi[0]
    chans, rows = zero.shape
    count, _, pairs = ins.shape
    rim = 2 * lo.shape[1]
    ext = rows + rim
    scenes = lax.axis_size("scan")
    bricks = lax.axis_size("space")
    tiles = -(-count * chans // LANES)
    tall = tiles * LANES
    unit = 16 * bricks
    packed = -(-tiles * chans // unit) * unit
    gather_flops = 2 * count * chans * ext * rows
    back_flops = 2 * count * chans * chans * ext

    operands = [pltpu.with_memory_space_constraint(x, pltpu.HBM) for x in (outs, cot, ins, weight_two, hi, lo, zero, pre)]
    rounded = -(-count // 8) * 8
    c_two, t_rim, inv_rim, near, far = call(
        rim_body,
        [
            shape((count * (chans + 16), pairs), BF16),
            shape((tall, rim), BF16),
            shape((rounded, rim), F32),
            shape((2 * chans, rim), BF16),
            shape((2 * chans, rim), BF16),
        ],
        operands,
        scratch=[pltpu.VMEM(x.shape, x.dtype) for x in operands]
        + [pltpu.VMEM((chans, rows), F32), pltpu.VMEM((chans, rim), F32), pltpu.SemaphoreType.DMA((len(operands),))],
        flops=2 * count * chans * rows * pairs,
        moved=4 << 20,
        args_in=HBM,
    )
    near, far = swap_neighbours(near, far)
    t_own, own = call(
        own_body,
        [shape((tall, rows), BF16), shape((chans + rounded, rows), F32)],
        [ins, c_two, weight_two],
        scratch=[pltpu.VMEM((chans, rows), F32), pltpu.VMEM((-(-count // UNROLL), pairs, LANES), F32)],
        flops=gather_flops // 2,
        moved=8 << 20,
    )
    sum_two = call(two_weights_body, shape((packed, LANES), F32), [pre, t_own], flops=back_flops, moved=6 << 20)
    t_one, keep, send = call(
        functools.partial(one_body, count),
        [shape((tall, ext), BF16), shape((packed, LANES), F32), shape((packed, LANES), BF16)],
        [own, inv_rim, near, far, hi, lo, pre, zero, t_rim, sum_two],
        scratch=[pltpu.VMEM((chans, rows), BF16), pltpu.VMEM((chans, rows), F32), pltpu.VMEM((packed, LANES), F32)],
        flops=gather_flops + back_flops,
        moved=8 << 20,
    )
    got = swap(send, "space", 1)
    own, near, far = call(
        back_body,
        [shape((chans, rows), F32), shape((chans, rim), BF16), shape((chans, rim), BF16)],
        [weight_one, t_one],
        scratch=[pltpu.VMEM((chans, ext), F32)],
        flops=back_flops,
        moved=6 << 20,
    )
    keep, near, far = lax.optimization_barrier((keep, near, far))

    def swap_edges(held, _):
        held, *edges = lax.optimization_barrier((held, near, far))
        held, *edges = lax.optimization_barrier((held, *swap_neighbours(*edges)))
        return held, edges

    def settle(held, edges):
        held, own_rows, *edges = lax.optimization_barrier((held, own, *edges))
        grad_act = call(settle_body, shape((chans, rows), BF16), [own_rows, *edges, hi, lo])
        return lax.optimization_barrier((held, grad_act))

    grad_act, (grad_one, grad_two) = summed(keep, got, 2, weight_one.shape, 1.0 / scenes, (swap_edges, settle))
    return grad_act.T[None, None], grad_one, grad_two


def solution(mesh):
    return jax.shard_map(
        shards,
        mesh=mesh,
        in_specs=(
            P("scan", "space", None, None),
            P("scan", "space", None, None),
            P("scan", "space", None, None),
            P(),
            P(),
            P("scan", "space", None, None),
            P("scan", "space", None, None),
            P("scan", "space", None),
            P("scan", "space", None),
        ),
        out_specs=(P("scan", "space", None, None), P(), P()),
        check_vma=False,
    )
```

```python
import functools

import jax
import jax.numpy as jnp
from jax import lax
from jax.experimental import pallas as pl
from jax.experimental.pallas import tpu as pltpu
from jax.sharding import PartitionSpec as P

F32, BF16, I32 = jnp.float32, jnp.bfloat16, jnp.int32
VMEM = pl.BlockSpec(memory_space=pltpu.VMEM)
HBM = pl.BlockSpec(memory_space=pltpu.HBM)
LANES = 128
BLOCK = 256
CHUNK = 9
WHOLE = 62 << 20
NT = (((1,), (1,)), ((), ()))


def call(body, outs, args, scratch=(), flops=0, moved=0, args_in=VMEM, outs_in=VMEM, room=40 << 20):
    single = not isinstance(outs, (list, tuple))
    return pl.pallas_call(
        body,
        out_shape=outs if single else tuple(outs),
        in_specs=[args_in] * len(args),
        out_specs=outs_in if single or isinstance(outs_in, tuple) else (outs_in,) * len(outs),
        scratch_shapes=scratch,
        compiler_params=pltpu.CompilerParams(vmem_limit_bytes=room),
        cost_estimate=pl.CostEstimate(flops=flops, bytes_accessed=moved, transcendentals=0),
    )(*args)


def shape(dims, dtype):
    return jax.ShapeDtypeStruct(dims, dtype)


def one_hot(rows, index):
    count = lax.broadcasted_iota(I32, (min(rows, BLOCK), index.shape[1]), 0).astype(F32).astype(BF16)
    blocks = []
    for start in range(0, rows, BLOCK):
        wanted = (index - start).astype(F32).astype(BF16)
        hit = count[: min(BLOCK, rows - start)] == wanted
        blocks.append(jnp.where(hit, jnp.ones((), BF16), jnp.zeros((), BF16)))
    return jnp.concatenate(blocks, 0)


def one_hot_columns(index, width):
    count = lax.broadcasted_iota(I32, (index.shape[0], min(width, BLOCK)), 1).astype(F32).astype(BF16)
    blocks = []
    for start in range(0, width, BLOCK):
        size = min(BLOCK, width - start)
        hit = count[:, :size] == jnp.broadcast_to((index - start).astype(BF16), (index.shape[0], size))
        blocks.append(jnp.where(hit, jnp.ones((), BF16), jnp.zeros((), BF16)))
    return jnp.concatenate(blocks, 1)


def take_columns(source_ref, index):
    dims = (source_ref.shape[0], LANES)
    lane, tile = jnp.broadcast_to(index % LANES, dims), jnp.broadcast_to(index // LANES, dims)
    taken = jnp.zeros(dims, F32)
    for t in range(source_ref.shape[1] // LANES):
        block = source_ref[:, t * LANES : (t + 1) * LANES]
        taken = jnp.where(tile == t, jnp.take_along_axis(block, lane, axis=1, mode="promise_in_bounds"), taken)
    return taken


def dot(a, b):
    return jnp.dot(a, b, preferred_element_type=F32)


def dot_nt(a, b):
    return lax.dot_general(a, b, NT, preferred_element_type=F32)


def offset_rows(k, chans):
    return slice(k * chans, (k + 1) * chans)


def rim_index(hi_ref, lo_ref):
    return jnp.concatenate([hi_ref[...], lo_ref[...]], 1)


def halves(x, y):
    x, y = x.astype(F32), y.astype(F32)
    width = x.shape[1]
    left = lax.broadcasted_iota(I32, x.shape, 1) < width // 2
    return jnp.where(left, x, pltpu.roll(y, width // 2, 1)), jnp.where(left, pltpu.roll(x, width // 2, 1), y)


def by_parity(x, y):
    even = lax.rem(lax.axis_index("space"), 2) == 0
    return jnp.where(even, x, y), jnp.where(even, y, x)


def put_edges(near_ref, far_ref, at, up, down):
    rows = slice(at, at + up.shape[0])
    for ref, value in zip((near_ref, far_ref), by_parity(up, down), strict=True):
        ref[rows] = value.astype(BF16)


def rim_gradients(near_ref, far_ref, total):
    high = total.astype(BF16).astype(F32)
    down, up = halves(high, total - high)
    put_edges(near_ref, far_ref, 0, up, down)


def add_back(weight_ref, t_ref, total_ref):
    count, chans = weight_ref.shape[0], weight_ref.shape[1]
    total_ref[...] = jnp.zeros_like(total_ref)

    def body(g):
        part = None
        for j in range(3):
            k = g * 3 + j
            term = dot(weight_ref[k], t_ref[offset_rows(k, chans), :])
            part = term if part is None else part + term
        total_ref[...] += part

    assert count % 3 == 0
    for g in range(count // 3):
        body(g)


def place_rows(ins_ref, c_ref, first, t_ref, inv_ref, inv_at):
    count = ins_ref.shape[0]
    ext = t_ref.shape[1]
    tall = c_ref.shape[0] // count
    chans = tall - 16
    t_ref[count * chans :, :] = jnp.zeros((t_ref.shape[0] - count * chans, ext), BF16)

    def place(k):
        picked = c_ref[k * tall : (k + 1) * tall, :]
        placed = dot_nt(picked, one_hot(ext, ins_ref[k] - first))
        t_ref[offset_rows(k, chans), :] = placed[:chans].astype(BF16)
        code = placed[chans : chans + 1] * 16.0 + placed[chans + 1 : chans + 2]
        inv_ref[pl.ds(inv_at + k, 1), :] = code

    for k in range(count):
        place(k)


def rim_body(*refs):
    operands, (c_ref, t_ref, inv_ref, near_ref, far_ref), scratch = refs[:8], refs[8:13], refs[13:]
    locals_, (source_ref, total_ref, sems) = scratch[:8], scratch[8:]
    copies = [
        pltpu.make_async_copy(operand, local, sems.at[i]) for i, (operand, local) in enumerate(zip(operands, locals_, strict=True))
    ]
    for copy in copies:
        copy.start()
    outs_ref, cot_ref, ins_ref, weight_ref, hi_ref, lo_ref, zero_ref, pre_ref = locals_
    count, pairs = ins_ref.shape[0], ins_ref.shape[2]
    chans, rows = cot_ref.shape
    tall = chans + 16
    row = lax.broadcasted_iota(I32, (16, pairs), 0)

    def pick(k):
        index = outs_ref[k]
        base = k * tall
        if k % 4:
            there = dot(cot_ref[...], one_hot(rows, index)).astype(BF16)
        else:
            there = [take_columns(source_ref, index[:, at : at + LANES]).astype(BF16) for at in range(0, pairs, LANES)]
            there = jnp.concatenate(there, 1)
        c_ref[pl.ds(base, chans), :] = there
        left = rows - index
        code = jnp.where(row == 0, left // 16, jnp.where(row == 1, left % 16, 0))
        c_ref[pl.ds(base + chans, 16), :] = code.astype(F32).astype(BF16)

    copies[0].wait()
    copies[1].wait()
    source_ref[...] = cot_ref[...].astype(F32)
    for k in range(count):
        pick(k)
    copies[2].wait()
    place_rows(ins_ref, c_ref, rows, t_ref, inv_ref, 0)
    copies[3].wait()
    add_back(weight_ref, t_ref, total_ref)
    rim_gradients(near_ref, far_ref, total_ref[...])
    for copy in copies[4:]:
        copy.wait()
    wanted = one_hot(rows, rim_index(hi_ref, lo_ref))
    one = jnp.maximum(pre_ref[...], jnp.zeros_like(pre_ref))
    up, down = halves(dot(zero_ref[...], wanted), dot(one, wanted))
    put_edges(near_ref, far_ref, chans, up, down)


def own_body(ins_ref, c_ref, weight_ref, t_ref, own_ref, total_ref, columns_ref):
    count, pairs = ins_ref.shape[0], ins_ref.shape[2]
    chans, rows = total_ref.shape
    tall = chans + 16
    t_ref[count * chans :, :] = jnp.zeros((t_ref.shape[0] - count * chans, rows), BF16)
    lines = [ins_ref[k] for k in range(count)] + [jnp.zeros((-count % 8, pairs), I32)]
    columns_ref[:, : count + -count % 8] = jnp.concatenate(lines, 0).astype(F32).T
    index = columns_ref[...]
    for k in range(count):
        picked = c_ref[k * tall : (k + 1) * tall, :]
        placed = dot(picked, one_hot_columns(index[:, k : k + 1], rows))
        t_ref[offset_rows(k, chans), :] = placed[:chans].astype(BF16)
        own_ref[chans + k : chans + k + 1, :] = placed[chans : chans + 1] * 16.0 + placed[chans + 1 : chans + 2]
    add_back(weight_ref, t_ref, total_ref)
    own_ref[:chans] = total_ref[...]


def packed_products(feats, t_ref, sum_ref, base_ref=None):
    chans = feats.shape[0]
    tiles = t_ref.shape[0] // LANES
    for start in range(0, tiles, 2):
        width = min(2, tiles - start)
        grad = dot_nt(feats, t_ref[start * LANES : (start + width) * LANES, :])
        for j in range(width):
            rows = slice((start + j) * chans, (start + j + 1) * chans)
            block = grad[:, j * LANES : (j + 1) * LANES]
            sum_ref[rows, :] = block if base_ref is None else block + base_ref[rows, :]
    sum_ref[tiles * chans :, :] = jnp.zeros((sum_ref.shape[0] - tiles * chans, LANES), F32)


def cut(sum_ref, layer, keep_ref, send_ref):
    me = lax.axis_index("space")
    slots = lax.axis_size("space") // 2
    rows = sum_ref.shape[0] // (2 * slots)
    for slot in range(slots):
        there = pl.ds((layer * slots + slot) * rows, rows)
        for out_ref, bit in ((keep_ref, 0), (send_ref, 1)):
            piece = jnp.bitwise_xor(me, 2 * slot + bit)
            block = sum_ref[pl.ds(pl.multiple_of(piece * rows, rows), rows), :]
            out_ref[there, :] = block.astype(out_ref.dtype)


def two_weights_body(pre_ref, t_ref, sum_ref):
    one = jnp.maximum(pre_ref[...], jnp.zeros_like(pre_ref))
    packed_products(one, t_ref, sum_ref)


def settled(own, near, far, hi_ref, lo_ref):
    above, below = by_parity(near, far)
    place = one_hot(own.shape[1], rim_index(hi_ref, lo_ref))
    for part in halves(above, below):
        own = own + dot_nt(part.astype(BF16), place)
    return own


def one_body(
    count, own_ref, inv_ref, near_ref, far_ref, hi_ref, lo_ref, pre_ref, zero_ref, t_two_ref, sum_two_ref, t_ref, keep_ref, send_ref, cot_ref, source_ref, sum_ref
):
    chans, rows = pre_ref.shape
    back = settled(own_ref[:chans], near_ref[:chans], far_ref[:chans], hi_ref, lo_ref)
    cot_ref[...] = jnp.where(pre_ref[...].astype(F32) > 0, back, 0.0).astype(BF16)

    source_ref[...] = cot_ref[...].astype(F32)

    def place(k):
        there = offset_rows(k, chans)
        part = rows - (LANES if k % 3 else 2 * LANES)
        index = rows - own_ref[chans + k : chans + k + 1, :]
        t_ref[there, :part] = dot(cot_ref[...], one_hot(rows, index[:, :part])).astype(BF16)
        index = jnp.concatenate([index[:, part:], rows - inv_ref[k : k + 1, :]], 1).astype(I32)
        for at in range(0, index.shape[1], LANES):
            t_ref[there, part + at : part + at + LANES] = take_columns(source_ref, index[:, at : at + LANES]).astype(BF16)

    for k in range(count):
        place(k)
    t_ref[count * chans :, :] = jnp.zeros((t_ref.shape[0] - count * chans, t_ref.shape[1]), BF16)
    above, below = by_parity(near_ref[chans:], far_ref[chans:])
    zero_rim, one_rim = halves(below, above)
    feats = jnp.concatenate([zero_ref[...], zero_rim.astype(BF16)], 1)
    packed_products(feats, t_ref, sum_ref)
    cut(sum_ref, 0, keep_ref, send_ref)
    packed_products(one_rim.astype(BF16), t_two_ref, sum_ref, sum_two_ref)
    cut(sum_ref, 1, keep_ref, send_ref)


def back_body(weight_ref, t_ref, own_ref, near_ref, far_ref, total_ref):
    rows = own_ref.shape[1]
    add_back(weight_ref, t_ref, total_ref)
    own_ref[...] = total_ref[:, :rows]
    rim_gradients(near_ref, far_ref, total_ref[:, rows:])


def settle_body(own_ref, near_ref, far_ref, hi_ref, lo_ref, out_ref):
    out_ref[...] = settled(own_ref[...], near_ref[...], far_ref[...], hi_ref, lo_ref).astype(BF16)


def core_sum_body(layers, keep_ref, got_ref, own_ref, *send_refs):
    rows = own_ref.shape[0] // layers
    slots = len(send_refs) + 1
    for layer in range(layers):
        there = slice(layer * rows, (layer + 1) * rows)
        for slot, out_ref in enumerate((own_ref, *send_refs)):
            part = slice((layer * slots + slot) * rows, (layer * slots + slot + 1) * rows)
            out_ref[there] = (keep_ref[part] + got_ref[part].astype(F32)).astype(out_ref.dtype)


def chip_sum_body(own_ref, *refs):
    layers = 2
    total = own_ref[...]
    for got_ref in refs[:-layers]:
        total = total + got_ref[...].astype(F32)
    rows = total.shape[0] // layers
    for layer, out_ref in enumerate(refs[-layers:]):
        out_ref[...] = total[layer * rows : (layer + 1) * rows].astype(BF16)


def scan_sum_body(*refs):
    *terms, total_ref = refs
    rows = terms[0].shape[0]
    for i in range(0, len(terms), 2):
        total_ref[i // 2 * rows : (i // 2 + 1) * rows] = (terms[i][...].astype(F32) + terms[i + 1][...].astype(F32)).astype(BF16)


def unpack_body(scale, layers, *refs):
    *refs, all_ref, sems = refs
    piece_refs, outs, locals_ = refs[: -2 * layers], refs[-2 * layers : -layers], refs[-layers:]
    me = lax.axis_index("space")
    rows = piece_refs[0].shape[0] // layers
    count, chans = locals_[0].shape[0], locals_[0].shape[1]
    lane = lax.broadcasted_iota(I32, (chans, LANES), 1)
    copies = []
    for layer in range(layers):
        for slot, piece_ref in enumerate(piece_refs):
            piece = jnp.bitwise_xor(me, slot)
            block = piece_ref[layer * rows : (layer + 1) * rows].astype(F32)
            all_ref[pl.ds(pl.multiple_of(piece * rows, rows), rows), :] = block
        for first in range(0, count, CHUNK):
            chunk = pl.ds(first, min(CHUNK, count - first))
            for k in range(first, first + chunk.size):
                tile, shift = divmod(k * chans, LANES)
                block = all_ref[tile * chans : (tile + 1) * chans, :]
                if shift:
                    block = pltpu.roll(block, LANES - shift, 1)
                if shift + chans > LANES:
                    after = pltpu.roll(all_ref[(tile + 1) * chans : (tile + 2) * chans, :], LANES - shift, 1)
                    block = jnp.where(lane < LANES - shift, block, after)
                locals_[layer][k] = block[:, :chans] * scale
            copies.append(pltpu.make_async_copy(locals_[layer].at[chunk], outs[layer].at[chunk], sems.at[len(copies)]))
            copies[-1].start()
    for copy in copies:
        copy.wait()


def swap(block, axis, bit):
    return lax.ppermute(block, axis, [(i, i ^ bit) for i in range(lax.axis_size(axis))])


def swap_neighbours(near, far):
    inner = range(1, lax.axis_size("space") - 1)
    far = lax.ppermute(far, "space", [(i, i + 1 if i % 2 else i - 1) for i in inner])
    return swap(near, "space", 1), far


def swap_scans(block, step, steps):
    scans = lax.axis_size("scan")
    bits = (1 << step, 1 << (steps - 1 - step))
    bricks = range(lax.axis_size("space"))
    pairs = [(b * scans + z, b * scans + (z ^ bits[b % 2])) for b in bricks for z in range(scans)]
    return lax.ppermute(block, ("space", "scan"), pairs)


def summed(keep, got, layers, weight_shape, scale, beside):
    slots = lax.axis_size("space") // 2
    scans = lax.axis_size("scan")
    packed = 2 * keep.shape[0] // layers
    rows = keep.shape[0] // slots
    outs = [shape((rows, LANES), F32)] + [shape((rows, LANES), BF16)] * (slots - 1)
    own, *sends = call(functools.partial(core_sum_body, layers), outs, [keep, got])
    gots = [swap(block, "space", 2 * slot) for slot, block in enumerate(sends, 1)]
    waiting = list(beside)
    own, state = waiting.pop(0)(own, None)
    part = rows // layers
    totals = call(chip_sum_body, [shape((part, LANES), BF16)] * layers, [own, *gots])
    if scans & (scans - 1):
        total = lax.psum(jnp.concatenate(totals), "scan")
    else:
        steps = scans.bit_length() - 1
        for step in range(steps):
            more = [swap_scans(total, step, steps) for total in totals]
            if waiting:
                totals, state = waiting.pop(0)(totals, state)
            if step + 1 < steps:
                totals = [call(scan_sum_body, shape((part, LANES), BF16), [x, y]) for x, y in zip(totals, more, strict=True)]
            else:
                total = call(scan_sum_body, shape((rows, LANES), BF16), [x for pair in zip(totals, more, strict=True) for x in pair])
    for work in waiting:
        total, state = work(total, state)
    pieces = []
    for slot in range(slots):
        piece = swap(total, "space", 2 * slot) if slot else total
        pieces += [piece, swap(piece, "space", 1)]
    return state, call(
        functools.partial(unpack_body, scale, layers),
        [shape(weight_shape, F32)] * layers,
        pieces,
        scratch=[pltpu.VMEM(weight_shape, F32)] * layers + [pltpu.VMEM((packed, LANES), F32), pltpu.SemaphoreType.DMA((layers * -(-weight_shape[0] // CHUNK),))],
        outs_in=HBM,
    )


def shards(act_zero, pre_act, cot_out, weight_one, weight_two, in_map, out_map, send_lo, send_hi):
    zero, pre, cot = (x[0, 0].T for x in (act_zero, pre_act, cot_out))
    ins, outs = (x[0, 0][:, None, :] for x in (in_map, out_map))
    lo, hi = send_lo[0], send_hi[0]
    chans, rows = zero.shape
    count, _, pairs = ins.shape
    rim = 2 * lo.shape[1]
    ext = rows + rim
    scenes = lax.axis_size("scan")
    bricks = lax.axis_size("space")
    tiles = -(-count * chans // LANES)
    tall = tiles * LANES
    unit = 16 * bricks
    packed = -(-tiles * chans // unit) * unit
    gather_flops = 2 * count * chans * ext * rows
    back_flops = 2 * count * chans * chans * ext

    operands = [pltpu.with_memory_space_constraint(x, pltpu.HBM) for x in (outs, cot, ins, weight_two, hi, lo, zero, pre)]
    rounded = -(-count // 8) * 8
    c_two, t_rim, inv_rim, near, far = call(
        rim_body,
        [
            shape((count * (chans + 16), pairs), BF16),
            shape((tall, rim), BF16),
            shape((rounded, rim), F32),
            shape((2 * chans, rim), BF16),
            shape((2 * chans, rim), BF16),
        ],
        operands,
        scratch=[pltpu.VMEM(x.shape, x.dtype) for x in operands]
        + [pltpu.VMEM((chans, rows), F32), pltpu.VMEM((chans, rim), F32), pltpu.SemaphoreType.DMA((len(operands),))],
        flops=2 * count * chans * rows * pairs,
        moved=4 << 20,
        args_in=HBM,
    )
    near, far = swap_neighbours(near, far)
    t_own, own = call(
        own_body,
        [shape((tall, rows), BF16), shape((chans + rounded, rows), F32)],
        [ins, c_two, weight_two],
        scratch=[pltpu.VMEM((chans, rows), F32), pltpu.VMEM((pairs, LANES), F32)],
        flops=gather_flops // 2,
        moved=8 << 20,
    )
    sum_two = call(two_weights_body, shape((packed, LANES), F32), [pre, t_own], flops=back_flops, moved=6 << 20)
    t_one, keep, send = call(
        functools.partial(one_body, count),
        [shape((tall, ext), BF16), shape((packed, LANES), F32), shape((packed, LANES), BF16)],
        [own, inv_rim, near, far, hi, lo, pre, zero, t_rim, sum_two],
        scratch=[pltpu.VMEM((chans, rows), BF16), pltpu.VMEM((chans, rows), F32), pltpu.VMEM((packed, LANES), F32)],
        flops=gather_flops + back_flops,
        moved=8 << 20,
    )
    got = swap(send, "space", 1)
    own, near, far = call(
        back_body,
        [shape((chans, rows), F32), shape((chans, rim), BF16), shape((chans, rim), BF16)],
        [weight_one, t_one],
        scratch=[pltpu.VMEM((chans, ext), F32)],
        flops=back_flops,
        moved=6 << 20,
    )
    keep, near, far = lax.optimization_barrier((keep, near, far))

    def swap_edges(held, _):
        held, *edges = lax.optimization_barrier((held, near, far))
        held, *edges = lax.optimization_barrier((held, *swap_neighbours(*edges)))
        return held, edges

    def settle(held, edges):
        held, own_rows, *edges = lax.optimization_barrier((held, own, *edges))
        grad_act = call(settle_body, shape((chans, rows), BF16), [own_rows, *edges, hi, lo])
        return lax.optimization_barrier((held, grad_act))

    grad_act, (grad_one, grad_two) = summed(keep, got, 2, weight_one.shape, 1.0 / scenes, (swap_edges, settle))
    return grad_act.T[None, None], grad_one, grad_two


def solution(mesh):
    return jax.shard_map(
        shards,
        mesh=mesh,
        in_specs=(
            P("scan", "space", None, None),
            P("scan", "space", None, None),
            P("scan", "space", None, None),
            P(),
            P(),
            P("scan", "space", None, None),
            P("scan", "space", None, None),
            P("scan", "space", None),
            P("scan", "space", None),
        ),
        out_specs=(P("scan", "space", None, None), P(), P()),
        check_vma=False,
    )
```

```python
import functools

import jax
import jax.numpy as jnp
from jax import lax
from jax.experimental import pallas as pl
from jax.experimental.pallas import tpu as pltpu
from jax.sharding import PartitionSpec as P

F32, BF16, I32 = jnp.float32, jnp.bfloat16, jnp.int32
VMEM = pl.BlockSpec(memory_space=pltpu.VMEM)
HBM = pl.BlockSpec(memory_space=pltpu.HBM)
LANES = 128
BLOCK = 256
WHOLE = 62 << 20
NT = (((1,), (1,)), ((), ()))


def call(body, outs, args, scratch=(), flops=0, moved=0, args_in=VMEM, outs_in=VMEM, room=40 << 20, aliases=()):
    single = not isinstance(outs, (list, tuple))
    return pl.pallas_call(
        body,
        out_shape=outs if single else tuple(outs),
        in_specs=list(args_in) if isinstance(args_in, (list, tuple)) else [args_in] * len(args),
        input_output_aliases=dict(aliases),
        out_specs=outs_in if single or isinstance(outs_in, tuple) else (outs_in,) * len(outs),
        scratch_shapes=scratch,
        compiler_params=pltpu.CompilerParams(vmem_limit_bytes=room),
        cost_estimate=pl.CostEstimate(flops=flops, bytes_accessed=moved, transcendentals=0),
    )(*args)


def shape(dims, dtype):
    return jax.ShapeDtypeStruct(dims, dtype)


def one_hot(rows, index):
    count = lax.broadcasted_iota(I32, (min(rows, BLOCK), index.shape[1]), 0).astype(F32).astype(BF16)
    blocks = []
    for start in range(0, rows, BLOCK):
        wanted = (index - start).astype(F32).astype(BF16)
        hit = count[: min(BLOCK, rows - start)] == wanted
        blocks.append(jnp.where(hit, jnp.ones((), BF16), jnp.zeros((), BF16)))
    return jnp.concatenate(blocks, 0)


def one_hot_columns(index, width):
    count = lax.broadcasted_iota(I32, (index.shape[0], min(width, BLOCK)), 1).astype(F32).astype(BF16)
    blocks = []
    for start in range(0, width, BLOCK):
        size = min(BLOCK, width - start)
        hit = count[:, :size] == jnp.broadcast_to((index - start).astype(BF16), (index.shape[0], size))
        blocks.append(jnp.where(hit, jnp.ones((), BF16), jnp.zeros((), BF16)))
    return jnp.concatenate(blocks, 1)


def take_columns(source_ref, index):
    dims = (source_ref.shape[0], LANES)
    lane, tile = jnp.broadcast_to(index % LANES, dims), jnp.broadcast_to(index // LANES, dims)
    taken = jnp.zeros(dims, F32)
    for t in range(source_ref.shape[1] // LANES):
        block = source_ref[:, t * LANES : (t + 1) * LANES]
        taken = jnp.where(tile == t, jnp.take_along_axis(block, lane, axis=1, mode="promise_in_bounds"), taken)
    return taken


def dot(a, b):
    return jnp.dot(a, b, preferred_element_type=F32)


def dot_nt(a, b):
    return lax.dot_general(a, b, NT, preferred_element_type=F32)


def offset_rows(k, chans):
    return slice(k * chans, (k + 1) * chans)


def rim_index(hi_ref, lo_ref):
    return jnp.concatenate([hi_ref[...], lo_ref[...]], 1)


def halves(x, y):
    x, y = x.astype(F32), y.astype(F32)
    width = x.shape[1]
    left = lax.broadcasted_iota(I32, x.shape, 1) < width // 2
    return jnp.where(left, x, pltpu.roll(y, width // 2, 1)), jnp.where(left, pltpu.roll(x, width // 2, 1), y)


def by_parity(x, y):
    even = lax.rem(lax.axis_index("space"), 2) == 0
    return jnp.where(even, x, y), jnp.where(even, y, x)


def put_edges(near_ref, far_ref, at, up, down):
    rows = slice(at, at + up.shape[0])
    for ref, value in zip((near_ref, far_ref), by_parity(up, down), strict=True):
        ref[rows] = value.astype(BF16)


def rim_gradients(near_ref, far_ref, total):
    high = total.astype(BF16).astype(F32)
    down, up = halves(high, total - high)
    put_edges(near_ref, far_ref, 0, up, down)


def add_back(weight_ref, t_ref, total_ref):
    count, chans = weight_ref.shape[0], weight_ref.shape[1]
    total_ref[...] = jnp.zeros_like(total_ref)

    def body(g):
        part = None
        for j in range(3):
            k = g * 3 + j
            term = dot(weight_ref[k], t_ref[offset_rows(k, chans), :])
            part = term if part is None else part + term
        total_ref[...] += part

    assert count % 3 == 0
    for g in range(count // 3):
        body(g)


def place_rows(ins_ref, c_ref, first, t_ref, inv_ref, inv_at):
    count = ins_ref.shape[0]
    ext = t_ref.shape[1]
    tall = c_ref.shape[0] // count
    chans = tall - 16
    t_ref[count * chans :, :] = jnp.zeros((t_ref.shape[0] - count * chans, ext), BF16)

    def place(k):
        picked = c_ref[k * tall : (k + 1) * tall, :]
        placed = dot_nt(picked, one_hot(ext, ins_ref[k] - first))
        t_ref[offset_rows(k, chans), :] = placed[:chans].astype(BF16)
        code = placed[chans : chans + 1] * 16.0 + placed[chans + 1 : chans + 2]
        inv_ref[pl.ds(inv_at + k, 1), :] = code

    for k in range(count):
        place(k)


def rim_body(*refs):
    operands, (c_ref, t_ref, inv_ref, near_ref, far_ref), scratch = refs[:8], refs[8:13], refs[13:]
    locals_, (source_ref, total_ref, sems) = scratch[:8], scratch[8:]
    copies = [
        pltpu.make_async_copy(operand, local, sems.at[i]) for i, (operand, local) in enumerate(zip(operands, locals_, strict=True))
    ]
    for copy in copies:
        copy.start()
    outs_ref, cot_ref, ins_ref, weight_ref, hi_ref, lo_ref, zero_ref, pre_ref = locals_
    count, pairs = ins_ref.shape[0], ins_ref.shape[2]
    chans, rows = cot_ref.shape
    tall = chans + 16
    row = lax.broadcasted_iota(I32, (16, pairs), 0)

    def pick(k):
        index = outs_ref[k]
        base = k * tall
        if k % 4:
            there = dot(cot_ref[...], one_hot(rows, index)).astype(BF16)
        else:
            there = [take_columns(source_ref, index[:, at : at + LANES]).astype(BF16) for at in range(0, pairs, LANES)]
            there = jnp.concatenate(there, 1)
        c_ref[pl.ds(base, chans), :] = there
        left = rows - index
        code = jnp.where(row == 0, left // 16, jnp.where(row == 1, left % 16, 0))
        c_ref[pl.ds(base + chans, 16), :] = code.astype(F32).astype(BF16)

    copies[0].wait()
    copies[1].wait()
    source_ref[...] = cot_ref[...].astype(F32)
    for k in range(count):
        pick(k)
    copies[2].wait()
    place_rows(ins_ref, c_ref, rows, t_ref, inv_ref, 0)
    copies[3].wait()
    add_back(weight_ref, t_ref, total_ref)
    rim_gradients(near_ref, far_ref, total_ref[...])
    for copy in copies[4:]:
        copy.wait()
    wanted = one_hot(rows, rim_index(hi_ref, lo_ref))
    one = jnp.maximum(pre_ref[...], jnp.zeros_like(pre_ref))
    up, down = halves(dot(zero_ref[...], wanted), dot(one, wanted))
    put_edges(near_ref, far_ref, chans, up, down)


def own_body(ins_ref, c_ref, weight_ref, t_ref, own_ref, total_ref, columns_ref):
    count, pairs = ins_ref.shape[0], ins_ref.shape[2]
    chans, rows = total_ref.shape
    tall = chans + 16
    t_ref[count * chans :, :] = jnp.zeros((t_ref.shape[0] - count * chans, rows), BF16)
    lines = [ins_ref[k] for k in range(count)] + [jnp.zeros((-count % 8, pairs), I32)]
    columns_ref[:, : count + -count % 8] = jnp.concatenate(lines, 0).astype(F32).T
    index = columns_ref[...]
    for k in range(count):
        picked = c_ref[k * tall : (k + 1) * tall, :]
        placed = dot(picked, one_hot_columns(index[:, k : k + 1], rows))
        t_ref[offset_rows(k, chans), :] = placed[:chans].astype(BF16)
        own_ref[chans + k : chans + k + 1, :] = placed[chans : chans + 1] * 16.0 + placed[chans + 1 : chans + 2]
    add_back(weight_ref, t_ref, total_ref)
    own_ref[:chans] = total_ref[...]


def packed_products(feats, t_ref, sum_ref, base_ref=None):
    chans = feats.shape[0]
    tiles = t_ref.shape[0] // LANES
    for start in range(0, tiles, 2):
        width = min(2, tiles - start)
        grad = dot_nt(feats, t_ref[start * LANES : (start + width) * LANES, :])
        for j in range(width):
            rows = slice((start + j) * chans, (start + j + 1) * chans)
            block = grad[:, j * LANES : (j + 1) * LANES]
            sum_ref[rows, :] = block if base_ref is None else block + base_ref[rows, :]
    sum_ref[tiles * chans :, :] = jnp.zeros((sum_ref.shape[0] - tiles * chans, LANES), F32)


def place_of(device, slots):
    return jnp.bitwise_and(device, 1) * slots + lax.shift_right_logical(device, 1)


def cut(sum_ref, layer, keep_ref, send_ref):
    me = lax.axis_index("space")
    slots = lax.axis_size("space") // 2
    rows = sum_ref.shape[0] // (2 * slots)
    for slot in range(slots):
        there = pl.ds((layer * slots + slot) * rows, rows)
        for out_ref, bit in ((keep_ref, 0), (send_ref, 1)):
            piece = place_of(jnp.bitwise_xor(me, 2 * slot + bit), slots)
            block = sum_ref[pl.ds(pl.multiple_of(piece * rows, rows), rows), :]
            out_ref[there, :] = block.astype(out_ref.dtype)


def two_weights_body(pre_ref, t_ref, sum_ref):
    one = jnp.maximum(pre_ref[...], jnp.zeros_like(pre_ref))
    packed_products(one, t_ref, sum_ref)


def settled(own, near, far, hi_ref, lo_ref):
    above, below = by_parity(near, far)
    place = one_hot(own.shape[1], rim_index(hi_ref, lo_ref))
    for part in halves(above, below):
        own = own + dot_nt(part.astype(BF16), place)
    return own


def one_body(
    count, own_ref, inv_ref, near_ref, far_ref, hi_ref, lo_ref, pre_ref, zero_ref, t_two_ref, sum_two_ref, t_ref, keep_ref, send_ref, cot_ref, source_ref, sum_ref
):
    chans, rows = pre_ref.shape
    back = settled(own_ref[:chans], near_ref[:chans], far_ref[:chans], hi_ref, lo_ref)
    cot_ref[...] = jnp.where(pre_ref[...].astype(F32) > 0, back, 0.0).astype(BF16)

    source_ref[...] = cot_ref[...].astype(F32)

    def place(k):
        there = offset_rows(k, chans)
        part = rows - (LANES if k % 3 else 2 * LANES)
        index = rows - own_ref[chans + k : chans + k + 1, :]
        t_ref[there, :part] = dot(cot_ref[...], one_hot(rows, index[:, :part])).astype(BF16)
        index = jnp.concatenate([index[:, part:], rows - inv_ref[k : k + 1, :]], 1).astype(I32)
        for at in range(0, index.shape[1], LANES):
            t_ref[there, part + at : part + at + LANES] = take_columns(source_ref, index[:, at : at + LANES]).astype(BF16)

    for k in range(count):
        place(k)
    t_ref[count * chans :, :] = jnp.zeros((t_ref.shape[0] - count * chans, t_ref.shape[1]), BF16)
    above, below = by_parity(near_ref[chans:], far_ref[chans:])
    zero_rim, one_rim = halves(below, above)
    feats = jnp.concatenate([zero_ref[...], zero_rim.astype(BF16)], 1)
    packed_products(feats, t_ref, sum_ref)
    cut(sum_ref, 0, keep_ref, send_ref)
    packed_products(one_rim.astype(BF16), t_two_ref, sum_ref, sum_two_ref)
    cut(sum_ref, 1, keep_ref, send_ref)


def back_body(weight_ref, t_ref, own_ref, near_ref, far_ref, total_ref):
    rows = own_ref.shape[1]
    add_back(weight_ref, t_ref, total_ref)
    own_ref[...] = total_ref[:, :rows]
    rim_gradients(near_ref, far_ref, total_ref[:, rows:])


def settle_body(own_ref, near_ref, far_ref, hi_ref, lo_ref, out_ref):
    out_ref[...] = settled(own_ref[...], near_ref[...], far_ref[...], hi_ref, lo_ref).astype(BF16)


def core_sum_body(layers, keep_ref, got_ref, own_ref, *send_refs):
    rows = own_ref.shape[0] // layers
    slots = len(send_refs) + 1
    for layer in range(layers):
        there = slice(layer * rows, (layer + 1) * rows)
        for slot, out_ref in enumerate((own_ref, *send_refs)):
            part = slice((layer * slots + slot) * rows, (layer * slots + slot + 1) * rows)
            out_ref[there] = (keep_ref[part] + got_ref[part].astype(F32)).astype(out_ref.dtype)


def chip_sum_body(own_ref, *refs):
    layers = 2
    total = own_ref[...]
    for got_ref in refs[:-layers]:
        total = total + got_ref[...].astype(F32)
    rows = total.shape[0] // layers
    for layer, out_ref in enumerate(refs[-layers:]):
        out_ref[...] = total[layer * rows : (layer + 1) * rows].astype(BF16)


def scan_sum_body(*refs):
    *terms, total_ref = refs
    rows = terms[0].shape[0]
    for i in range(0, len(terms), 2):
        total_ref[i // 2 * rows : (i // 2 + 1) * rows] = (terms[i][...].astype(F32) + terms[i + 1][...].astype(F32)).astype(BF16)


def tiles_of(k, chans):
    return k * chans // LANES, -(-(k + 1) * chans // LANES)


def unpack_body(scale, layers, early, *refs):
    *refs, all_ref, sems = refs
    piece_refs, outs, locals_ = refs[: -2 * layers], refs[-2 * layers : -layers], refs[-layers:]
    if not early:
        piece_refs = piece_refs[:-layers]
    me = lax.axis_index("space")
    slots = lax.axis_size("space") // 2
    step = 2 * slots // len(piece_refs)
    rows = piece_refs[0].shape[0] // layers
    half = rows * slots
    count, chans = locals_[0].shape[0], locals_[0].shape[1]
    lane = lax.broadcasted_iota(I32, (chans, LANES), 1)

    def unpack(core):
        spans = [tiles_of(k, chans) for k in range(count)]
        inside = [last * chans <= half if core == 0 else first * chans >= half for first, last in spans]
        wanted = [k for k in range(count) if inside[k] == early]
        assert wanted == list(range(wanted[0], wanted[-1] + 1))
        middle = (wanted[0] + wanted[-1] + 1) // 2
        copies = []
        for layer in range(layers):
            for i, piece_ref in enumerate(piece_refs):
                piece = place_of(jnp.bitwise_xor(me, step * i), slots)
                block = piece_ref[layer * rows : (layer + 1) * rows].astype(F32)
                all_ref[pl.ds(pl.multiple_of(piece * rows, rows), rows), :] = block
            for first, last in ((wanted[0], middle), (middle, wanted[-1] + 1)):
                for k in range(first, last):
                    tile, shift = divmod(k * chans, LANES)
                    block = all_ref[tile * chans : (tile + 1) * chans, :]
                    if shift:
                        block = pltpu.roll(block, LANES - shift, 1)
                    if shift + chans > LANES:
                        after = pltpu.roll(all_ref[(tile + 1) * chans : (tile + 2) * chans, :], LANES - shift, 1)
                        block = jnp.where(lane < LANES - shift, block, after)
                    locals_[layer][k] = block[:, :chans] * scale
                chunk = pl.ds(first, last - first)
                copies.append(pltpu.make_async_copy(locals_[layer].at[chunk], outs[layer].at[chunk], sems.at[len(copies)]))
                copies[-1].start()
        for copy in copies:
            copy.wait()

    for core in range(2):
        pl.when(jnp.bitwise_and(me, 1) == core)(functools.partial(unpack, core))


def swap(block, axis, bit):
    return lax.ppermute(block, axis, [(i, i ^ bit) for i in range(lax.axis_size(axis))])


def swap_neighbours(near, far):
    inner = range(1, lax.axis_size("space") - 1)
    far = lax.ppermute(far, "space", [(i, i + 1 if i % 2 else i - 1) for i in inner])
    return swap(near, "space", 1), far


def swap_scans(block, step, steps):
    scans = lax.axis_size("scan")
    bits = (1 << step, 1 << (steps - 1 - step))
    bricks = range(lax.axis_size("space"))
    pairs = [(b * scans + z, b * scans + (z ^ bits[b % 2])) for b in bricks for z in range(scans)]
    return lax.ppermute(block, ("space", "scan"), pairs)


def summed(keep, got, layers, weight_shape, scale, beside):
    slots = lax.axis_size("space") // 2
    scans = lax.axis_size("scan")
    packed = 2 * keep.shape[0] // layers
    rows = keep.shape[0] // slots
    outs = [shape((rows, LANES), F32)] + [shape((rows, LANES), BF16)] * (slots - 1)
    own, *sends = call(functools.partial(core_sum_body, layers), outs, [keep, got])
    gots = [swap(block, "space", 2 * slot) for slot, block in enumerate(sends, 1)]
    waiting = list(beside)
    own, state = waiting.pop(0)(own, None)
    part = rows // layers
    totals = call(chip_sum_body, [shape((part, LANES), BF16)] * layers, [own, *gots])
    if scans & (scans - 1):
        total = lax.psum(jnp.concatenate(totals), "scan")
    else:
        steps = scans.bit_length() - 1
        for step in range(steps):
            more = [swap_scans(total, step, steps) for total in totals]
            if waiting:
                totals, state = waiting.pop(0)(totals, state)
            if step + 1 < steps:
                totals = [call(scan_sum_body, shape((part, LANES), BF16), [x, y]) for x, y in zip(totals, more, strict=True)]
            else:
                total = call(scan_sum_body, shape((rows, LANES), BF16), [x for pair in zip(totals, more, strict=True) for x in pair])
    for work in waiting:
        total, state = work(total, state)
    pieces = []
    for slot in range(slots):
        piece = swap(total, "space", 2 * slot) if slot else total
        pieces += [piece, swap(piece, "space", 1)]
    outs = ()
    for early, given in ((True, pieces[::2]), (False, pieces)):
        outs = call(
            functools.partial(unpack_body, scale, layers, early),
            [shape(weight_shape, F32)] * layers,
            [*given, *outs],
            scratch=[pltpu.VMEM(weight_shape, F32)] * layers
            + [pltpu.VMEM((packed, LANES), F32), pltpu.SemaphoreType.DMA((2 * layers,))],
            args_in=[VMEM] * len(given) + [HBM] * len(outs),
            outs_in=HBM,
            aliases=[(len(given) + i, i) for i in range(len(outs))],
            moved=4 << 20,
        )
    return state, outs


def shards(act_zero, pre_act, cot_out, weight_one, weight_two, in_map, out_map, send_lo, send_hi):
    zero, pre, cot = (x[0, 0].T for x in (act_zero, pre_act, cot_out))
    ins, outs = (x[0, 0][:, None, :] for x in (in_map, out_map))
    lo, hi = send_lo[0], send_hi[0]
    chans, rows = zero.shape
    count, _, pairs = ins.shape
    rim = 2 * lo.shape[1]
    ext = rows + rim
    scenes = lax.axis_size("scan")
    bricks = lax.axis_size("space")
    tiles = -(-count * chans // LANES)
    tall = tiles * LANES
    unit = 16 * bricks
    packed = -(-tiles * chans // unit) * unit
    gather_flops = 2 * count * chans * ext * rows
    back_flops = 2 * count * chans * chans * ext

    operands = [pltpu.with_memory_space_constraint(x, pltpu.HBM) for x in (outs, cot, ins, weight_two, hi, lo, zero, pre)]
    rounded = -(-count // 8) * 8
    c_two, t_rim, inv_rim, near, far = call(
        rim_body,
        [
            shape((count * (chans + 16), pairs), BF16),
            shape((tall, rim), BF16),
            shape((rounded, rim), F32),
            shape((2 * chans, rim), BF16),
            shape((2 * chans, rim), BF16),
        ],
        operands,
        scratch=[pltpu.VMEM(x.shape, x.dtype) for x in operands]
        + [pltpu.VMEM((chans, rows), F32), pltpu.VMEM((chans, rim), F32), pltpu.SemaphoreType.DMA((len(operands),))],
        flops=2 * count * chans * rows * pairs,
        moved=4 << 20,
        args_in=HBM,
    )
    near, far = swap_neighbours(near, far)
    t_own, own = call(
        own_body,
        [shape((tall, rows), BF16), shape((chans + rounded, rows), F32)],
        [ins, c_two, weight_two],
        scratch=[pltpu.VMEM((chans, rows), F32), pltpu.VMEM((pairs, LANES), F32)],
        flops=gather_flops // 2,
        moved=8 << 20,
    )
    sum_two = call(two_weights_body, shape((packed, LANES), F32), [pre, t_own], flops=back_flops, moved=6 << 20)
    t_one, keep, send = call(
        functools.partial(one_body, count),
        [shape((tall, ext), BF16), shape((packed, LANES), F32), shape((packed, LANES), BF16)],
        [own, inv_rim, near, far, hi, lo, pre, zero, t_rim, sum_two],
        scratch=[pltpu.VMEM((chans, rows), BF16), pltpu.VMEM((chans, rows), F32), pltpu.VMEM((packed, LANES), F32)],
        flops=gather_flops + back_flops,
        moved=8 << 20,
    )
    got = swap(send, "space", 1)
    own, near, far = call(
        back_body,
        [shape((chans, rows), F32), shape((chans, rim), BF16), shape((chans, rim), BF16)],
        [weight_one, t_one],
        scratch=[pltpu.VMEM((chans, ext), F32)],
        flops=back_flops,
        moved=6 << 20,
    )
    keep, near, far = lax.optimization_barrier((keep, near, far))

    def swap_edges(held, _):
        held, *edges = lax.optimization_barrier((held, near, far))
        held, *edges = lax.optimization_barrier((held, *swap_neighbours(*edges)))
        return held, edges

    def settle(held, edges):
        held, own_rows, *edges = lax.optimization_barrier((held, own, *edges))
        grad_act = call(settle_body, shape((chans, rows), BF16), [own_rows, *edges, hi, lo])
        return lax.optimization_barrier((held, grad_act))

    grad_act, (grad_one, grad_two) = summed(keep, got, 2, weight_one.shape, 1.0 / scenes, (swap_edges, settle))
    return grad_act.T[None, None], grad_one, grad_two


def solution(mesh):
    return jax.shard_map(
        shards,
        mesh=mesh,
        in_specs=(
            P("scan", "space", None, None),
            P("scan", "space", None, None),
            P("scan", "space", None, None),
            P(),
            P(),
            P("scan", "space", None, None),
            P("scan", "space", None, None),
            P("scan", "space", None),
            P("scan", "space", None),
        ),
        out_specs=(P("scan", "space", None, None), P(), P()),
        check_vma=False,
    )
```

```python
import functools

import jax
import jax.numpy as jnp
from jax import lax
from jax.experimental import pallas as pl
from jax.experimental.pallas import tpu as pltpu
from jax.sharding import PartitionSpec as P

F32, BF16, I32 = jnp.float32, jnp.bfloat16, jnp.int32
VMEM = pl.BlockSpec(memory_space=pltpu.VMEM)
HBM = pl.BlockSpec(memory_space=pltpu.HBM)
LANES = 128
BLOCK = 256
WHOLE = 62 << 20
NT = (((1,), (1,)), ((), ()))


def call(body, outs, args, scratch=(), flops=0, moved=0, args_in=VMEM, outs_in=VMEM, room=40 << 20, aliases=()):
    single = not isinstance(outs, (list, tuple))
    return pl.pallas_call(
        body,
        out_shape=outs if single else tuple(outs),
        in_specs=list(args_in) if isinstance(args_in, (list, tuple)) else [args_in] * len(args),
        input_output_aliases=dict(aliases),
        out_specs=outs_in if single or isinstance(outs_in, tuple) else (outs_in,) * len(outs),
        scratch_shapes=scratch,
        compiler_params=pltpu.CompilerParams(vmem_limit_bytes=room),
        cost_estimate=pl.CostEstimate(flops=flops, bytes_accessed=moved, transcendentals=0),
    )(*args)


def shape(dims, dtype):
    return jax.ShapeDtypeStruct(dims, dtype)


def one_hot(rows, index):
    count = lax.broadcasted_iota(I32, (min(rows, BLOCK), index.shape[1]), 0).astype(F32).astype(BF16)
    blocks = []
    for start in range(0, rows, BLOCK):
        wanted = (index - start).astype(F32).astype(BF16)
        hit = count[: min(BLOCK, rows - start)] == wanted
        blocks.append(jnp.where(hit, jnp.ones((), BF16), jnp.zeros((), BF16)))
    return jnp.concatenate(blocks, 0)


def one_hot_columns(index, width):
    count = lax.broadcasted_iota(I32, (index.shape[0], min(width, BLOCK)), 1).astype(F32).astype(BF16)
    blocks = []
    for start in range(0, width, BLOCK):
        size = min(BLOCK, width - start)
        hit = count[:, :size] == jnp.broadcast_to((index - start).astype(BF16), (index.shape[0], size))
        blocks.append(jnp.where(hit, jnp.ones((), BF16), jnp.zeros((), BF16)))
    return jnp.concatenate(blocks, 1)


def take_columns(source_ref, index):
    dims = (source_ref.shape[0], LANES)
    lane, tile = jnp.broadcast_to(index % LANES, dims), jnp.broadcast_to(index // LANES, dims)
    taken = jnp.zeros(dims, F32)
    for t in range(source_ref.shape[1] // LANES):
        block = source_ref[:, t * LANES : (t + 1) * LANES]
        taken = jnp.where(tile == t, jnp.take_along_axis(block, lane, axis=1, mode="promise_in_bounds"), taken)
    return taken


def dot(a, b):
    return jnp.dot(a, b, preferred_element_type=F32)


def dot_nt(a, b):
    return lax.dot_general(a, b, NT, preferred_element_type=F32)


def offset_rows(k, chans):
    return slice(k * chans, (k + 1) * chans)


def rim_index(hi_ref, lo_ref):
    return jnp.concatenate([hi_ref[...], lo_ref[...]], 1)


def halves(x, y):
    x, y = x.astype(F32), y.astype(F32)
    width = x.shape[1]
    left = lax.broadcasted_iota(I32, x.shape, 1) < width // 2
    return jnp.where(left, x, pltpu.roll(y, width // 2, 1)), jnp.where(left, pltpu.roll(x, width // 2, 1), y)


def by_parity(x, y):
    even = lax.rem(lax.axis_index("space"), 2) == 0
    return jnp.where(even, x, y), jnp.where(even, y, x)


def put_edges(near_ref, far_ref, at, up, down):
    rows = slice(at, at + up.shape[0])
    for ref, value in zip((near_ref, far_ref), by_parity(up, down), strict=True):
        ref[rows] = value.astype(BF16)


def rim_gradients(near_ref, far_ref, total):
    high = total.astype(BF16).astype(F32)
    down, up = halves(high, total - high)
    put_edges(near_ref, far_ref, 0, up, down)


def add_back(weight_ref, t_ref, total_ref):
    count, chans = weight_ref.shape[0], weight_ref.shape[1]
    total_ref[...] = jnp.zeros_like(total_ref)

    def body(g):
        part = None
        for j in range(3):
            k = g * 3 + j
            term = dot(weight_ref[k], t_ref[offset_rows(k, chans), :])
            part = term if part is None else part + term
        total_ref[...] += part

    assert count % 3 == 0
    for g in range(count // 3):
        body(g)


def place_rows(ins_ref, c_ref, first, t_ref, inv_ref, inv_at):
    count = ins_ref.shape[0]
    ext = t_ref.shape[1]
    tall = c_ref.shape[0] // count
    chans = tall - 16
    t_ref[count * chans :, :] = jnp.zeros((t_ref.shape[0] - count * chans, ext), BF16)

    def place(k):
        picked = c_ref[k * tall : (k + 1) * tall, :]
        placed = dot_nt(picked, one_hot(ext, ins_ref[k] - first))
        t_ref[offset_rows(k, chans), :] = placed[:chans].astype(BF16)
        code = placed[chans : chans + 1] * 16.0 + placed[chans + 1 : chans + 2]
        inv_ref[pl.ds(inv_at + k, 1), :] = code

    for k in range(count):
        place(k)


def rim_body(*refs):
    operands, (c_ref, t_ref, inv_ref, near_ref, far_ref), scratch = refs[:8], refs[8:13], refs[13:]
    locals_, (source_ref, total_ref, sems) = scratch[:8], scratch[8:]
    copies = [
        pltpu.make_async_copy(operand, local, sems.at[i]) for i, (operand, local) in enumerate(zip(operands, locals_, strict=True))
    ]
    for copy in copies:
        copy.start()
    outs_ref, cot_ref, ins_ref, weight_ref, hi_ref, lo_ref, zero_ref, pre_ref = locals_
    count, pairs = ins_ref.shape[0], ins_ref.shape[2]
    chans, rows = cot_ref.shape
    tall = chans + 16
    row = lax.broadcasted_iota(I32, (16, pairs), 0)

    def pick(k):
        index = outs_ref[k]
        base = k * tall
        if k % 4:
            there = dot(cot_ref[...], one_hot(rows, index)).astype(BF16)
        else:
            there = [take_columns(source_ref, index[:, at : at + LANES]).astype(BF16) for at in range(0, pairs, LANES)]
            there = jnp.concatenate(there, 1)
        c_ref[pl.ds(base, chans), :] = there
        left = rows - index
        code = jnp.where(row == 0, left // 16, jnp.where(row == 1, left % 16, 0))
        c_ref[pl.ds(base + chans, 16), :] = code.astype(F32).astype(BF16)

    copies[0].wait()
    copies[1].wait()
    source_ref[...] = cot_ref[...].astype(F32)
    for k in range(count):
        pick(k)
    copies[2].wait()
    place_rows(ins_ref, c_ref, rows, t_ref, inv_ref, 0)
    copies[3].wait()
    add_back(weight_ref, t_ref, total_ref)
    rim_gradients(near_ref, far_ref, total_ref[...])
    for copy in copies[4:]:
        copy.wait()
    wanted = one_hot(rows, rim_index(hi_ref, lo_ref))
    one = jnp.maximum(pre_ref[...], jnp.zeros_like(pre_ref))
    up, down = halves(dot(zero_ref[...], wanted), dot(one, wanted))
    put_edges(near_ref, far_ref, chans, up, down)


def own_body(ins_ref, c_ref, weight_ref, t_ref, own_ref, total_ref, columns_ref):
    count, pairs = ins_ref.shape[0], ins_ref.shape[2]
    chans, rows = total_ref.shape
    tall = chans + 16
    t_ref[count * chans :, :] = jnp.zeros((t_ref.shape[0] - count * chans, rows), BF16)
    lines = [ins_ref[k] for k in range(count)] + [jnp.zeros((-count % 8, pairs), I32)]
    columns_ref[:, : count + -count % 8] = jnp.concatenate(lines, 0).astype(F32).T
    index = columns_ref[...]
    for k in range(count):
        picked = c_ref[k * tall : (k + 1) * tall, :]
        placed = dot(picked, one_hot_columns(index[:, k : k + 1], rows))
        t_ref[offset_rows(k, chans), :] = placed[:chans].astype(BF16)
        own_ref[chans + k : chans + k + 1, :] = placed[chans : chans + 1] * 16.0 + placed[chans + 1 : chans + 2]
    add_back(weight_ref, t_ref, total_ref)
    own_ref[:chans] = total_ref[...]


def packed_products(feats, t_ref, sum_ref, base_ref=None):
    chans = feats.shape[0]
    tiles = t_ref.shape[0] // LANES
    for start in range(0, tiles, 2):
        width = min(2, tiles - start)
        grad = dot_nt(feats, t_ref[start * LANES : (start + width) * LANES, :])
        for j in range(width):
            rows = slice((start + j) * chans, (start + j + 1) * chans)
            block = grad[:, j * LANES : (j + 1) * LANES]
            sum_ref[rows, :] = block if base_ref is None else block + base_ref[rows, :]
    sum_ref[tiles * chans :, :] = jnp.zeros((sum_ref.shape[0] - tiles * chans, LANES), F32)


def place_of(device, slots):
    return jnp.bitwise_and(device, 1) * slots + lax.shift_right_logical(device, 1)


def cut(sum_ref, layer, keep_ref, send_ref):
    me = lax.axis_index("space")
    slots = lax.axis_size("space") // 2
    rows = sum_ref.shape[0] // (2 * slots)
    for slot in range(slots):
        there = pl.ds((layer * slots + slot) * rows, rows)
        for out_ref, bit in ((keep_ref, 0), (send_ref, 1)):
            piece = place_of(jnp.bitwise_xor(me, 2 * slot + bit), slots)
            block = sum_ref[pl.ds(pl.multiple_of(piece * rows, rows), rows), :]
            out_ref[there, :] = block.astype(out_ref.dtype)


def two_weights_body(pre_ref, t_ref, sum_ref):
    one = jnp.maximum(pre_ref[...], jnp.zeros_like(pre_ref))
    packed_products(one, t_ref, sum_ref)


def settled(own, near, far, hi_ref, lo_ref):
    above, below = by_parity(near, far)
    place = one_hot(own.shape[1], rim_index(hi_ref, lo_ref))
    for part in halves(above, below):
        own = own + dot_nt(part.astype(BF16), place)
    return own


def one_body(
    count, own_ref, inv_ref, near_ref, far_ref, hi_ref, lo_ref, pre_ref, zero_ref, t_two_ref, sum_two_ref, t_ref, keep_ref, send_ref, cot_ref, source_ref, sum_ref
):
    chans, rows = pre_ref.shape
    back = settled(own_ref[:chans], near_ref[:chans], far_ref[:chans], hi_ref, lo_ref)
    cot_ref[...] = jnp.where(pre_ref[...].astype(F32) > 0, back, 0.0).astype(BF16)

    source_ref[...] = cot_ref[...].astype(F32)

    def place(k):
        there = offset_rows(k, chans)
        part = rows - (LANES if k % 3 else 2 * LANES)
        index = rows - own_ref[chans + k : chans + k + 1, :]
        t_ref[there, :part] = dot(cot_ref[...], one_hot(rows, index[:, :part])).astype(BF16)
        index = jnp.concatenate([index[:, part:], rows - inv_ref[k : k + 1, :]], 1).astype(I32)
        for at in range(0, index.shape[1], LANES):
            t_ref[there, part + at : part + at + LANES] = take_columns(source_ref, index[:, at : at + LANES]).astype(BF16)

    for k in range(count):
        place(k)
    t_ref[count * chans :, :] = jnp.zeros((t_ref.shape[0] - count * chans, t_ref.shape[1]), BF16)
    above, below = by_parity(near_ref[chans:], far_ref[chans:])
    zero_rim, one_rim = halves(below, above)
    feats = jnp.concatenate([zero_ref[...], zero_rim.astype(BF16)], 1)
    packed_products(feats, t_ref, sum_ref)
    cut(sum_ref, 0, keep_ref, send_ref)
    packed_products(one_rim.astype(BF16), t_two_ref, sum_ref, sum_two_ref)
    cut(sum_ref, 1, keep_ref, send_ref)


def back_body(weight_ref, t_ref, own_ref, near_ref, far_ref, total_ref):
    rows = own_ref.shape[1]
    add_back(weight_ref, t_ref, total_ref)
    own_ref[...] = total_ref[:, :rows]
    rim_gradients(near_ref, far_ref, total_ref[:, rows:])


def settle_body(own_ref, near_ref, far_ref, hi_ref, lo_ref, out_ref):
    out_ref[...] = settled(own_ref[...], near_ref[...], far_ref[...], hi_ref, lo_ref).astype(BF16)


def core_sum_body(layers, keep_ref, got_ref, own_ref, *send_refs):
    rows = own_ref.shape[0] // layers
    slots = len(send_refs) + 1
    for layer in range(layers):
        there = slice(layer * rows, (layer + 1) * rows)
        for slot, out_ref in enumerate((own_ref, *send_refs)):
            part = slice((layer * slots + slot) * rows, (layer * slots + slot + 1) * rows)
            out_ref[there] = (keep_ref[part] + got_ref[part].astype(F32)).astype(out_ref.dtype)


def chip_sum_body(own_ref, *refs):
    layers = 2
    total = own_ref[...]
    for got_ref in refs[:-layers]:
        total = total + got_ref[...].astype(F32)
    rows = total.shape[0] // layers
    for layer, out_ref in enumerate(refs[-layers:]):
        out_ref[...] = total[layer * rows : (layer + 1) * rows].astype(BF16)


def scan_sum_body(*refs):
    *terms, total_ref = refs
    rows = terms[0].shape[0]
    for i in range(0, len(terms), 2):
        total_ref[i // 2 * rows : (i // 2 + 1) * rows] = (terms[i][...].astype(F32) + terms[i + 1][...].astype(F32)).astype(BF16)


def tiles_of(k, chans):
    return k * chans // LANES, -(-(k + 1) * chans // LANES)


def unpack_body(scale, layers, early, *refs):
    *refs, all_ref, sems = refs
    piece_refs, outs, locals_ = refs[: -2 * layers], refs[-2 * layers : -layers], refs[-layers:]
    if not early:
        piece_refs = piece_refs[:-layers]
    me = lax.axis_index("space")
    slots = lax.axis_size("space") // 2
    step = 2 * slots // len(piece_refs)
    rows = piece_refs[0].shape[0] // layers
    half = rows * slots
    count, chans = locals_[0].shape[0], locals_[0].shape[1]
    lane = lax.broadcasted_iota(I32, (chans, LANES), 1)

    def unpack(core):
        spans = [tiles_of(k, chans) for k in range(count)]
        inside = [last * chans <= half if core == 0 else first * chans >= half for first, last in spans]
        wanted = [k for k in range(count) if inside[k] == early]
        assert wanted == list(range(wanted[0], wanted[-1] + 1))
        middle = (wanted[0] + wanted[-1] + 1) // 2
        copies = []
        for layer in range(layers):
            for i, piece_ref in enumerate(piece_refs):
                piece = place_of(jnp.bitwise_xor(me, step * i), slots)
                block = piece_ref[layer * rows : (layer + 1) * rows].astype(F32)
                all_ref[pl.ds(pl.multiple_of(piece * rows, rows), rows), :] = block
            for first, last in ((wanted[0], middle), (middle, wanted[-1] + 1)):
                for k in range(first, last):
                    tile, shift = divmod(k * chans, LANES)
                    block = all_ref[tile * chans : (tile + 1) * chans, :]
                    if shift:
                        block = pltpu.roll(block, LANES - shift, 1)
                    if shift + chans > LANES:
                        after = pltpu.roll(all_ref[(tile + 1) * chans : (tile + 2) * chans, :], LANES - shift, 1)
                        block = jnp.where(lane < LANES - shift, block, after)
                    locals_[layer][k] = block[:, :chans] * scale
                chunk = pl.ds(first, last - first)
                copies.append(pltpu.make_async_copy(locals_[layer].at[chunk], outs[layer].at[chunk], sems.at[len(copies)]))
                copies[-1].start()
        for copy in copies:
            copy.wait()

    for core in range(2):
        pl.when(jnp.bitwise_and(me, 1) == core)(functools.partial(unpack, core))


def swap(block, axis, bit):
    return lax.ppermute(block, axis, [(i, i ^ bit) for i in range(lax.axis_size(axis))])


def swap_neighbours(near, far):
    inner = range(1, lax.axis_size("space") - 1)
    far = lax.ppermute(far, "space", [(i, i + 1 if i % 2 else i - 1) for i in inner])
    return swap(near, "space", 1), far


def swap_scans(block, step, steps):
    scans = lax.axis_size("scan")
    bits = (1 << step, 1 << (steps - 1 - step))
    bricks = range(lax.axis_size("space"))
    pairs = [(b * scans + z, b * scans + (z ^ bits[b % 2])) for b in bricks for z in range(scans)]
    return lax.ppermute(block, ("space", "scan"), pairs)


def summed(keep, got, layers, weight_shape, scale, beside):
    slots = lax.axis_size("space") // 2
    scans = lax.axis_size("scan")
    packed = 2 * keep.shape[0] // layers
    rows = keep.shape[0] // slots
    outs = [shape((rows, LANES), F32)] + [shape((rows, LANES), BF16)] * (slots - 1)
    own, *sends = call(functools.partial(core_sum_body, layers), outs, [keep, got])
    gots = [swap(block, "space", 2 * slot) for slot, block in reversed(list(enumerate(sends, 1)))]
    waiting = list(beside)
    own, state = waiting.pop(0)(own, None)
    part = rows // layers
    totals = call(chip_sum_body, [shape((part, LANES), BF16)] * layers, [own, *gots])
    if scans & (scans - 1):
        total = lax.psum(jnp.concatenate(totals), "scan")
    else:
        steps = scans.bit_length() - 1
        for step in range(steps):
            more = [swap_scans(total, step, steps) for total in totals]
            if waiting:
                totals, state = waiting.pop(0)(totals, state)
            if step + 1 < steps:
                totals = [call(scan_sum_body, shape((part, LANES), BF16), [x, y]) for x, y in zip(totals, more, strict=True)]
            else:
                total = call(scan_sum_body, shape((rows, LANES), BF16), [x for pair in zip(totals, more, strict=True) for x in pair])
    for work in waiting:
        total, state = work(total, state)
    pieces = []
    for slot in range(slots):
        piece = swap(total, "space", 2 * slot) if slot else total
        pieces += [piece, swap(piece, "space", 1)]
    outs = ()
    for early, given in ((True, pieces[::2]), (False, pieces)):
        outs = call(
            functools.partial(unpack_body, scale, layers, early),
            [shape(weight_shape, F32)] * layers,
            [*given, *outs],
            scratch=[pltpu.VMEM(weight_shape, F32)] * layers
            + [pltpu.VMEM((packed, LANES), F32), pltpu.SemaphoreType.DMA((2 * layers,))],
            args_in=[VMEM] * len(given) + [HBM] * len(outs),
            outs_in=HBM,
            aliases=[(len(given) + i, i) for i in range(len(outs))],
            moved=4 << 20,
        )
    return state, outs


def shards(act_zero, pre_act, cot_out, weight_one, weight_two, in_map, out_map, send_lo, send_hi):
    zero, pre, cot = (x[0, 0].T for x in (act_zero, pre_act, cot_out))
    ins, outs = (x[0, 0][:, None, :] for x in (in_map, out_map))
    lo, hi = send_lo[0], send_hi[0]
    chans, rows = zero.shape
    count, _, pairs = ins.shape
    rim = 2 * lo.shape[1]
    ext = rows + rim
    scenes = lax.axis_size("scan")
    bricks = lax.axis_size("space")
    tiles = -(-count * chans // LANES)
    tall = tiles * LANES
    unit = 16 * bricks
    packed = -(-tiles * chans // unit) * unit
    gather_flops = 2 * count * chans * ext * rows
    back_flops = 2 * count * chans * chans * ext

    operands = [pltpu.with_memory_space_constraint(x, pltpu.HBM) for x in (outs, cot, ins, weight_two, hi, lo, zero, pre)]
    rounded = -(-count // 8) * 8
    c_two, t_rim, inv_rim, near, far = call(
        rim_body,
        [
            shape((count * (chans + 16), pairs), BF16),
            shape((tall, rim), BF16),
            shape((rounded, rim), F32),
            shape((2 * chans, rim), BF16),
            shape((2 * chans, rim), BF16),
        ],
        operands,
        scratch=[pltpu.VMEM(x.shape, x.dtype) for x in operands]
        + [pltpu.VMEM((chans, rows), F32), pltpu.VMEM((chans, rim), F32), pltpu.SemaphoreType.DMA((len(operands),))],
        flops=2 * count * chans * rows * pairs,
        moved=4 << 20,
        args_in=HBM,
    )
    near, far = swap_neighbours(near, far)
    t_own, own = call(
        own_body,
        [shape((tall, rows), BF16), shape((chans + rounded, rows), F32)],
        [ins, c_two, weight_two],
        scratch=[pltpu.VMEM((chans, rows), F32), pltpu.VMEM((pairs, LANES), F32)],
        flops=gather_flops // 2,
        moved=8 << 20,
    )
    sum_two = call(two_weights_body, shape((packed, LANES), F32), [pre, t_own], flops=back_flops, moved=6 << 20)
    t_one, keep, send = call(
        functools.partial(one_body, count),
        [shape((tall, ext), BF16), shape((packed, LANES), F32), shape((packed, LANES), BF16)],
        [own, inv_rim, near, far, hi, lo, pre, zero, t_rim, sum_two],
        scratch=[pltpu.VMEM((chans, rows), BF16), pltpu.VMEM((chans, rows), F32), pltpu.VMEM((packed, LANES), F32)],
        flops=gather_flops + back_flops,
        moved=8 << 20,
    )
    got = swap(send, "space", 1)
    own, near, far = call(
        back_body,
        [shape((chans, rows), F32), shape((chans, rim), BF16), shape((chans, rim), BF16)],
        [weight_one, t_one],
        scratch=[pltpu.VMEM((chans, ext), F32)],
        flops=back_flops,
        moved=6 << 20,
    )
    keep, near, far = lax.optimization_barrier((keep, near, far))

    def swap_edges(held, _):
        held, *edges = lax.optimization_barrier((held, near, far))
        held, *edges = lax.optimization_barrier((held, *swap_neighbours(*edges)))
        return held, edges

    def settle(held, edges):
        held, own_rows, *edges = lax.optimization_barrier((held, own, *edges))
        grad_act = call(settle_body, shape((chans, rows), BF16), [own_rows, *edges, hi, lo])
        return lax.optimization_barrier((held, grad_act))

    grad_act, (grad_one, grad_two) = summed(keep, got, 2, weight_one.shape, 1.0 / scenes, (swap_edges, settle))
    return grad_act.T[None, None], grad_one, grad_two


def solution(mesh):
    return jax.shard_map(
        shards,
        mesh=mesh,
        in_specs=(
            P("scan", "space", None, None),
            P("scan", "space", None, None),
            P("scan", "space", None, None),
            P(),
            P(),
            P("scan", "space", None, None),
            P("scan", "space", None, None),
            P("scan", "space", None),
            P("scan", "space", None),
        ),
        out_specs=(P("scan", "space", None, None), P(), P()),
        check_vma=False,
    )
```

```python
import functools

import jax
import jax.numpy as jnp
from jax import lax
from jax.experimental import pallas as pl
from jax.experimental.pallas import tpu as pltpu
from jax.sharding import PartitionSpec as P

F32, BF16, I32 = jnp.float32, jnp.bfloat16, jnp.int32
VMEM = pl.BlockSpec(memory_space=pltpu.VMEM)
HBM = pl.BlockSpec(memory_space=pltpu.HBM)
LANES = 128
BLOCK = 256
WHOLE = 62 << 20
NT = (((1,), (1,)), ((), ()))


def call(body, outs, args, scratch=(), flops=0, moved=0, args_in=VMEM, outs_in=VMEM, room=40 << 20, aliases=()):
    single = not isinstance(outs, (list, tuple))
    return pl.pallas_call(
        body,
        out_shape=outs if single else tuple(outs),
        in_specs=list(args_in) if isinstance(args_in, (list, tuple)) else [args_in] * len(args),
        input_output_aliases=dict(aliases),
        out_specs=outs_in if single or isinstance(outs_in, tuple) else (outs_in,) * len(outs),
        scratch_shapes=scratch,
        compiler_params=pltpu.CompilerParams(vmem_limit_bytes=room),
        cost_estimate=pl.CostEstimate(flops=flops, bytes_accessed=moved, transcendentals=0),
    )(*args)


def shape(dims, dtype):
    return jax.ShapeDtypeStruct(dims, dtype)


def one_hot(rows, index):
    count = lax.broadcasted_iota(I32, (min(rows, BLOCK), index.shape[1]), 0).astype(F32).astype(BF16)
    blocks = []
    for start in range(0, rows, BLOCK):
        wanted = (index - start).astype(F32).astype(BF16)
        hit = count[: min(BLOCK, rows - start)] == wanted
        blocks.append(jnp.where(hit, jnp.ones((), BF16), jnp.zeros((), BF16)))
    return jnp.concatenate(blocks, 0)


def one_hot_columns(index, width):
    count = lax.broadcasted_iota(I32, (index.shape[0], min(width, BLOCK)), 1).astype(F32).astype(BF16)
    blocks = []
    for start in range(0, width, BLOCK):
        size = min(BLOCK, width - start)
        hit = count[:, :size] == jnp.broadcast_to((index - start).astype(BF16), (index.shape[0], size))
        blocks.append(jnp.where(hit, jnp.ones((), BF16), jnp.zeros((), BF16)))
    return jnp.concatenate(blocks, 1)


def take_columns(source_ref, index):
    dims = (source_ref.shape[0], LANES)
    lane, tile = jnp.broadcast_to(index % LANES, dims), jnp.broadcast_to(index // LANES, dims)
    taken = jnp.zeros(dims, F32)
    for t in range(source_ref.shape[1] // LANES):
        block = source_ref[:, t * LANES : (t + 1) * LANES]
        taken = jnp.where(tile == t, jnp.take_along_axis(block, lane, axis=1, mode="promise_in_bounds"), taken)
    return taken


def dot(a, b):
    return jnp.dot(a, b, preferred_element_type=F32)


def dot_nt(a, b):
    return lax.dot_general(a, b, NT, preferred_element_type=F32)


def offset_rows(k, chans):
    return slice(k * chans, (k + 1) * chans)


def rim_index(hi_ref, lo_ref):
    return jnp.concatenate([hi_ref[...], lo_ref[...]], 1)


def halves(x, y):
    x, y = x.astype(F32), y.astype(F32)
    width = x.shape[1]
    left = lax.broadcasted_iota(I32, x.shape, 1) < width // 2
    return jnp.where(left, x, pltpu.roll(y, width // 2, 1)), jnp.where(left, pltpu.roll(x, width // 2, 1), y)


def by_parity(x, y):
    even = lax.rem(lax.axis_index("space"), 2) == 0
    return jnp.where(even, x, y), jnp.where(even, y, x)


def put_edges(near_ref, far_ref, at, up, down):
    rows = slice(at, at + up.shape[0])
    for ref, value in zip((near_ref, far_ref), by_parity(up, down), strict=True):
        ref[rows] = value.astype(BF16)


def rim_gradients(near_ref, far_ref, total):
    high = total.astype(BF16).astype(F32)
    down, up = halves(high, total - high)
    put_edges(near_ref, far_ref, 0, up, down)


def add_back(weight_ref, t_ref, total_ref):
    count, chans = weight_ref.shape[0], weight_ref.shape[1]
    total_ref[...] = jnp.zeros_like(total_ref)

    def body(g):
        part = None
        for j in range(9):
            k = g * 9 + j
            term = dot(weight_ref[k], t_ref[offset_rows(k, chans), :])
            part = term if part is None else part + term
        total_ref[...] += part

    assert count % 9 == 0
    for g in range(count // 9):
        body(g)


def place_rows(ins_ref, c_ref, first, t_ref, inv_ref, inv_at):
    count = ins_ref.shape[0]
    ext = t_ref.shape[1]
    tall = c_ref.shape[0] // count
    chans = tall - 16
    t_ref[count * chans :, :] = jnp.zeros((t_ref.shape[0] - count * chans, ext), BF16)

    def place(k):
        picked = c_ref[k * tall : (k + 1) * tall, :]
        placed = dot_nt(picked, one_hot(ext, ins_ref[k] - first))
        t_ref[offset_rows(k, chans), :] = placed[:chans].astype(BF16)
        code = placed[chans : chans + 1] * 16.0 + placed[chans + 1 : chans + 2]
        inv_ref[pl.ds(inv_at + k, 1), :] = code

    for k in range(count):
        place(k)


def rim_body(*refs):
    operands, (c_ref, t_ref, inv_ref, near_ref, far_ref), scratch = refs[:8], refs[8:13], refs[13:]
    locals_, (source_ref, total_ref, sems) = scratch[:8], scratch[8:]
    copies = [
        pltpu.make_async_copy(operand, local, sems.at[i]) for i, (operand, local) in enumerate(zip(operands, locals_, strict=True))
    ]
    for copy in copies:
        copy.start()
    outs_ref, cot_ref, ins_ref, weight_ref, hi_ref, lo_ref, zero_ref, pre_ref = locals_
    count, pairs = ins_ref.shape[0], ins_ref.shape[2]
    chans, rows = cot_ref.shape
    tall = chans + 16
    row = lax.broadcasted_iota(I32, (16, pairs), 0)

    def pick(k):
        index = outs_ref[k]
        base = k * tall
        if k % 4:
            there = dot(cot_ref[...], one_hot(rows, index)).astype(BF16)
        else:
            there = [take_columns(source_ref, index[:, at : at + LANES]).astype(BF16) for at in range(0, pairs, LANES)]
            there = jnp.concatenate(there, 1)
        c_ref[pl.ds(base, chans), :] = there
        left = rows - index
        code = jnp.where(row == 0, left // 16, jnp.where(row == 1, left % 16, 0))
        c_ref[pl.ds(base + chans, 16), :] = code.astype(F32).astype(BF16)

    copies[0].wait()
    copies[1].wait()
    source_ref[...] = cot_ref[...].astype(F32)
    for k in range(count):
        pick(k)
    copies[2].wait()
    place_rows(ins_ref, c_ref, rows, t_ref, inv_ref, 0)
    copies[3].wait()
    add_back(weight_ref, t_ref, total_ref)
    rim_gradients(near_ref, far_ref, total_ref[...])
    for copy in copies[4:]:
        copy.wait()
    wanted = one_hot(rows, rim_index(hi_ref, lo_ref))
    one = jnp.maximum(pre_ref[...], jnp.zeros_like(pre_ref))
    up, down = halves(dot(zero_ref[...], wanted), dot(one, wanted))
    put_edges(near_ref, far_ref, chans, up, down)


def own_body(ins_ref, c_ref, weight_ref, t_ref, own_ref, total_ref, columns_ref):
    count, pairs = ins_ref.shape[0], ins_ref.shape[2]
    chans, rows = total_ref.shape
    tall = chans + 16
    t_ref[count * chans :, :] = jnp.zeros((t_ref.shape[0] - count * chans, rows), BF16)
    lines = [ins_ref[k] for k in range(count)] + [jnp.zeros((-count % 8, pairs), I32)]
    columns_ref[:, : count + -count % 8] = jnp.concatenate(lines, 0).astype(F32).T
    index = columns_ref[...]
    for k in range(count):
        picked = c_ref[k * tall : (k + 1) * tall, :]
        placed = dot(picked, one_hot_columns(index[:, k : k + 1], rows))
        t_ref[offset_rows(k, chans), :] = placed[:chans].astype(BF16)
        own_ref[chans + k : chans + k + 1, :] = placed[chans : chans + 1] * 16.0 + placed[chans + 1 : chans + 2]
    add_back(weight_ref, t_ref, total_ref)
    own_ref[:chans] = total_ref[...]


def packed_products(feats, t_ref, sum_ref, base_ref=None):
    chans = feats.shape[0]
    tiles = t_ref.shape[0] // LANES
    for start in range(0, tiles, 4):
        width = min(4, tiles - start)
        grad = dot_nt(feats, t_ref[start * LANES : (start + width) * LANES, :])
        for j in range(width):
            rows = slice((start + j) * chans, (start + j + 1) * chans)
            block = grad[:, j * LANES : (j + 1) * LANES]
            sum_ref[rows, :] = block if base_ref is None else block + base_ref[rows, :]
    sum_ref[tiles * chans :, :] = jnp.zeros((sum_ref.shape[0] - tiles * chans, LANES), F32)


def place_of(device, slots):
    return jnp.bitwise_and(device, 1) * slots + lax.shift_right_logical(device, 1)


def cut(sum_ref, layer, keep_ref, send_ref):
    me = lax.axis_index("space")
    slots = lax.axis_size("space") // 2
    rows = sum_ref.shape[0] // (2 * slots)
    for slot in range(slots):
        there = pl.ds((layer * slots + slot) * rows, rows)
        for out_ref, bit in ((keep_ref, 0), (send_ref, 1)):
            piece = place_of(jnp.bitwise_xor(me, 2 * slot + bit), slots)
            block = sum_ref[pl.ds(pl.multiple_of(piece * rows, rows), rows), :]
            out_ref[there, :] = block.astype(out_ref.dtype)


def two_weights_body(pre_ref, t_ref, sum_ref):
    one = jnp.maximum(pre_ref[...], jnp.zeros_like(pre_ref))
    packed_products(one, t_ref, sum_ref)


def settled(own, near, far, hi_ref, lo_ref):
    above, below = by_parity(near, far)
    place = one_hot(own.shape[1], rim_index(hi_ref, lo_ref))
    for part in halves(above, below):
        own = own + dot_nt(part.astype(BF16), place)
    return own


def one_body(
    count, own_ref, inv_ref, near_ref, far_ref, hi_ref, lo_ref, pre_ref, zero_ref, t_two_ref, sum_two_ref, t_ref, keep_ref, send_ref, cot_ref, source_ref, sum_ref
):
    chans, rows = pre_ref.shape
    back = settled(own_ref[:chans], near_ref[:chans], far_ref[:chans], hi_ref, lo_ref)
    cot_ref[...] = jnp.where(pre_ref[...].astype(F32) > 0, back, 0.0).astype(BF16)

    source_ref[...] = cot_ref[...].astype(F32)

    def place(k):
        there = offset_rows(k, chans)
        part = rows - (LANES if k % 3 else 2 * LANES)
        index = rows - own_ref[chans + k : chans + k + 1, :]
        t_ref[there, :part] = dot(cot_ref[...], one_hot(rows, index[:, :part])).astype(BF16)
        index = jnp.concatenate([index[:, part:], rows - inv_ref[k : k + 1, :]], 1).astype(I32)
        for at in range(0, index.shape[1], LANES):
            t_ref[there, part + at : part + at + LANES] = take_columns(source_ref, index[:, at : at + LANES]).astype(BF16)

    for k in range(count):
        place(k)
    t_ref[count * chans :, :] = jnp.zeros((t_ref.shape[0] - count * chans, t_ref.shape[1]), BF16)
    above, below = by_parity(near_ref[chans:], far_ref[chans:])
    zero_rim, one_rim = halves(below, above)
    feats = jnp.concatenate([zero_ref[...], zero_rim.astype(BF16)], 1)
    packed_products(feats, t_ref, sum_ref)
    cut(sum_ref, 0, keep_ref, send_ref)
    packed_products(one_rim.astype(BF16), t_two_ref, sum_ref, sum_two_ref)
    cut(sum_ref, 1, keep_ref, send_ref)


def back_body(weight_ref, t_ref, own_ref, near_ref, far_ref, total_ref):
    rows = own_ref.shape[1]
    add_back(weight_ref, t_ref, total_ref)
    own_ref[...] = total_ref[:, :rows]
    rim_gradients(near_ref, far_ref, total_ref[:, rows:])


def settle_body(own_ref, near_ref, far_ref, hi_ref, lo_ref, out_ref):
    out_ref[...] = settled(own_ref[...], near_ref[...], far_ref[...], hi_ref, lo_ref).astype(BF16)


def core_sum_body(layers, keep_ref, got_ref, own_ref, *send_refs):
    rows = own_ref.shape[0] // layers
    slots = len(send_refs) + 1
    for layer in range(layers):
        there = slice(layer * rows, (layer + 1) * rows)
        for slot, out_ref in enumerate((own_ref, *send_refs)):
            part = slice((layer * slots + slot) * rows, (layer * slots + slot + 1) * rows)
            out_ref[there] = (keep_ref[part] + got_ref[part].astype(F32)).astype(out_ref.dtype)


def chip_sum_body(own_ref, *refs):
    layers = 2
    total = own_ref[...]
    for got_ref in refs[:-layers]:
        total = total + got_ref[...].astype(F32)
    rows = total.shape[0] // layers
    for layer, out_ref in enumerate(refs[-layers:]):
        out_ref[...] = total[layer * rows : (layer + 1) * rows].astype(BF16)


def scan_sum_body(*refs):
    *terms, total_ref = refs
    rows = terms[0].shape[0]
    for i in range(0, len(terms), 2):
        total_ref[i // 2 * rows : (i // 2 + 1) * rows] = (terms[i][...].astype(F32) + terms[i + 1][...].astype(F32)).astype(BF16)


def tiles_of(k, chans):
    return k * chans // LANES, -(-(k + 1) * chans // LANES)


def unpack_body(scale, layers, early, *refs):
    *refs, all_ref, sems = refs
    piece_refs, outs, locals_ = refs[: -2 * layers], refs[-2 * layers : -layers], refs[-layers:]
    if not early:
        piece_refs = piece_refs[:-layers]
    me = lax.axis_index("space")
    slots = lax.axis_size("space") // 2
    step = 2 * slots // len(piece_refs)
    rows = piece_refs[0].shape[0] // layers
    half = rows * slots
    count, chans = locals_[0].shape[0], locals_[0].shape[1]
    lane = lax.broadcasted_iota(I32, (chans, LANES), 1)

    def unpack(core):
        spans = [tiles_of(k, chans) for k in range(count)]
        inside = [last * chans <= half if core == 0 else first * chans >= half for first, last in spans]
        wanted = [k for k in range(count) if inside[k] == early]
        assert wanted == list(range(wanted[0], wanted[-1] + 1))
        ends = [wanted[0] + len(wanted) * i // 3 for i in range(4)]
        copies = []
        for layer in range(layers):
            for i, piece_ref in enumerate(piece_refs):
                piece = place_of(jnp.bitwise_xor(me, step * i), slots)
                block = piece_ref[layer * rows : (layer + 1) * rows].astype(F32)
                all_ref[pl.ds(pl.multiple_of(piece * rows, rows), rows), :] = block
            for first, last in zip(ends, ends[1:]):
                for k in range(first, last):
                    tile, shift = divmod(k * chans, LANES)
                    block = all_ref[tile * chans : (tile + 1) * chans, :]
                    if shift:
                        block = pltpu.roll(block, LANES - shift, 1)
                    if shift + chans > LANES:
                        after = pltpu.roll(all_ref[(tile + 1) * chans : (tile + 2) * chans, :], LANES - shift, 1)
                        block = jnp.where(lane < LANES - shift, block, after)
                    locals_[layer][k] = block[:, :chans] * scale
                chunk = pl.ds(first, last - first)
                copies.append(pltpu.make_async_copy(locals_[layer].at[chunk], outs[layer].at[chunk], sems.at[len(copies)]))
                copies[-1].start()
        for copy in copies:
            copy.wait()

    for core in range(2):
        pl.when(jnp.bitwise_and(me, 1) == core)(functools.partial(unpack, core))


def swap(block, axis, bit):
    return lax.ppermute(block, axis, [(i, i ^ bit) for i in range(lax.axis_size(axis))])


def swap_neighbours(near, far):
    inner = range(1, lax.axis_size("space") - 1)
    far = lax.ppermute(far, "space", [(i, i + 1 if i % 2 else i - 1) for i in inner])
    return swap(near, "space", 1), far


def swap_scans(block, step, steps):
    scans = lax.axis_size("scan")
    bits = (1 << step, 1 << (steps - 1 - step))
    bricks = range(lax.axis_size("space"))
    pairs = [(b * scans + z, b * scans + (z ^ bits[b % 2])) for b in bricks for z in range(scans)]
    return lax.ppermute(block, ("space", "scan"), pairs)


def summed(keep, got, layers, weight_shape, scale, beside):
    slots = lax.axis_size("space") // 2
    scans = lax.axis_size("scan")
    packed = 2 * keep.shape[0] // layers
    rows = keep.shape[0] // slots
    outs = [shape((rows, LANES), F32)] + [shape((rows, LANES), BF16)] * (slots - 1)
    own, *sends = call(functools.partial(core_sum_body, layers), outs, [keep, got])
    gots = [swap(block, "space", 2 * slot) for slot, block in reversed(list(enumerate(sends, 1)))]
    waiting = list(beside)
    own, state = waiting.pop(0)(own, None)
    part = rows // layers
    totals = call(chip_sum_body, [shape((part, LANES), BF16)] * layers, [own, *gots])
    if scans & (scans - 1):
        total = lax.psum(jnp.concatenate(totals), "scan")
    else:
        steps = scans.bit_length() - 1
        for step in range(steps):
            more = [swap_scans(total, step, steps) for total in totals]
            if waiting:
                totals, state = waiting.pop(0)(totals, state)
            if step + 1 < steps:
                totals = [call(scan_sum_body, shape((part, LANES), BF16), [x, y]) for x, y in zip(totals, more, strict=True)]
            else:
                total = call(scan_sum_body, shape((rows, LANES), BF16), [x for pair in zip(totals, more, strict=True) for x in pair])
    for work in waiting:
        total, state = work(total, state)
    pieces = []
    for slot in range(slots):
        piece = swap(total, "space", 2 * slot) if slot else total
        pieces += [piece, swap(piece, "space", 1)]
    outs = ()
    for early, given in ((True, pieces[::2]), (False, pieces)):
        outs = call(
            functools.partial(unpack_body, scale, layers, early),
            [shape(weight_shape, F32)] * layers,
            [*given, *outs],
            scratch=[pltpu.VMEM(weight_shape, F32)] * layers
            + [pltpu.VMEM((packed, LANES), F32), pltpu.SemaphoreType.DMA((3 * layers,))],
            args_in=[VMEM] * len(given) + [HBM] * len(outs),
            outs_in=HBM,
            aliases=[(len(given) + i, i) for i in range(len(outs))],
            moved=4 << 20,
        )
    return state, outs


def shards(act_zero, pre_act, cot_out, weight_one, weight_two, in_map, out_map, send_lo, send_hi):
    zero, pre, cot = (x[0, 0].T for x in (act_zero, pre_act, cot_out))
    ins, outs = (x[0, 0][:, None, :] for x in (in_map, out_map))
    lo, hi = send_lo[0], send_hi[0]
    chans, rows = zero.shape
    count, _, pairs = ins.shape
    rim = 2 * lo.shape[1]
    ext = rows + rim
    scenes = lax.axis_size("scan")
    bricks = lax.axis_size("space")
    tiles = -(-count * chans // LANES)
    tall = tiles * LANES
    unit = 16 * bricks
    packed = -(-tiles * chans // unit) * unit
    gather_flops = 2 * count * chans * ext * rows
    back_flops = 2 * count * chans * chans * ext

    operands = [pltpu.with_memory_space_constraint(x, pltpu.HBM) for x in (outs, cot, ins, weight_two, hi, lo, zero, pre)]
    rounded = -(-count // 8) * 8
    c_two, t_rim, inv_rim, near, far = call(
        rim_body,
        [
            shape((count * (chans + 16), pairs), BF16),
            shape((tall, rim), BF16),
            shape((rounded, rim), F32),
            shape((2 * chans, rim), BF16),
            shape((2 * chans, rim), BF16),
        ],
        operands,
        scratch=[pltpu.VMEM(x.shape, x.dtype) for x in operands]
        + [pltpu.VMEM((chans, rows), F32), pltpu.VMEM((chans, rim), F32), pltpu.SemaphoreType.DMA((len(operands),))],
        flops=2 * count * chans * rows * pairs,
        moved=4 << 20,
        args_in=HBM,
    )
    near, far = swap_neighbours(near, far)
    t_own, own = call(
        own_body,
        [shape((tall, rows), BF16), shape((chans + rounded, rows), F32)],
        [ins, c_two, weight_two],
        scratch=[pltpu.VMEM((chans, rows), F32), pltpu.VMEM((pairs, LANES), F32)],
        flops=gather_flops // 2,
        moved=8 << 20,
    )
    sum_two = call(two_weights_body, shape((packed, LANES), F32), [pre, t_own], flops=back_flops, moved=6 << 20)
    t_one, keep, send = call(
        functools.partial(one_body, count),
        [shape((tall, ext), BF16), shape((packed, LANES), F32), shape((packed, LANES), BF16)],
        [own, inv_rim, near, far, hi, lo, pre, zero, t_rim, sum_two],
        scratch=[pltpu.VMEM((chans, rows), BF16), pltpu.VMEM((chans, rows), F32), pltpu.VMEM((packed, LANES), F32)],
        flops=gather_flops + back_flops,
        moved=8 << 20,
    )
    got = swap(send, "space", 1)
    own, near, far = call(
        back_body,
        [shape((chans, rows), F32), shape((chans, rim), BF16), shape((chans, rim), BF16)],
        [weight_one, t_one],
        scratch=[pltpu.VMEM((chans, ext), F32)],
        flops=back_flops,
        moved=6 << 20,
    )
    keep, near, far = lax.optimization_barrier((keep, near, far))

    def swap_edges(held, _):
        held, *edges = lax.optimization_barrier((held, near, far))
        held, *edges = lax.optimization_barrier((held, *swap_neighbours(*edges)))
        return held, edges

    def settle(held, edges):
        held, own_rows, *edges = lax.optimization_barrier((held, own, *edges))
        grad_act = call(settle_body, shape((chans, rows), BF16), [own_rows, *edges, hi, lo])
        return lax.optimization_barrier((held, grad_act))

    grad_act, (grad_one, grad_two) = summed(keep, got, 2, weight_one.shape, 1.0 / scenes, (swap_edges, settle))
    return grad_act.T[None, None], grad_one, grad_two


def solution(mesh):
    return jax.shard_map(
        shards,
        mesh=mesh,
        in_specs=(
            P("scan", "space", None, None),
            P("scan", "space", None, None),
            P("scan", "space", None, None),
            P(),
            P(),
            P("scan", "space", None, None),
            P("scan", "space", None, None),
            P("scan", "space", None),
            P("scan", "space", None),
        ),
        out_specs=(P("scan", "space", None, None), P(), P()),
        check_vma=False,
    )
```
